32 devices in a mesh: dp: 8 (over y, x, core), seq: 4 (over z).
Axes of the slice: x: 2, y: 2, z: 4, core: 2. Of those that a mesh axis runs over, the one named last changes fastest.
Arguments:
- dec_in: bfloat16 [24, 128, 1024], P('dp', 'seq'), may hold values from -6 to 6
- memory: bfloat16 [24, 7, 128, 1024], P('dp', None, 'seq'), may hold values from -6 to 6
- proj_w: bfloat16 [6, 1024, 1024], P(None, ('dp', 'seq')), may hold values from -0.1875 to 0.1875
- out_w: bfloat16 [2, 1024, 1024], P(None, ('dp', 'seq')), may hold values from -1.25 to 1.25
- ffn_in: bfloat16 [1024, 4096], P(('dp', 'seq')), may hold values from -0.1875 to 0.1875
- ffn_out: bfloat16 [4096, 1024], P(('dp', 'seq')), may hold values from -0.09375 to 0.09375
- biases: float32 [6, 1024], replicated, may hold values from -2 to 2
- out_bias: float32 [1024], replicated, may hold values from -2 to 2
- ffn_bias: float32 [4096], replicated, may hold values from -2 to 2
- norm_gain: float32 [3, 1024], replicated, may hold values from 0.5 to 1.5
- norm_bias: float32 [3, 1024], replicated, may hold values from -2 to 2
- mem_len: int32 [24], replicated, may hold values from 4 to 896, as said below
- dec_len: int32 [24], replicated, may hold values from 64 to 128, as said below
- mem_seg: int32 [24, 7, 128], P('dp'), may hold values from 0 to 3, as said below
- dec_seg: int32 [24, 128], P('dp'), may hold values from 0 to 3, as said below
- cotangent: bfloat16 [24, 128, 1024], P('dp', 'seq'), may hold values from -6 to 6
Outputs:
- mixed: bfloat16 [24, 128, 1024], P('dp', 'seq')
- d_dec: float32 [24, 128, 1024], P('dp', 'seq')
- d_memory: bfloat16 [24, 7, 128, 1024], P('dp', None, 'seq')
- g_proj: float32 [6, 1024, 1024], P(None, 'seq')
- g_out: float32 [2, 1024, 1024], P(None, 'seq')
- g_ffn_in: float32 [1024, 4096], P('seq')
- g_ffn_out: float32 [4096, 1024], P('seq')
- g_biases: float32 [6, 1024], P(None, 'seq')
- g_out_bias: float32 [1024], P('seq')
- g_ffn_bias: float32 [4096], P('seq')
- g_gain: float32 [3, 1024], P(None, 'seq')
- g_shift: float32 [3, 1024], P(None, 'seq')
The draws below stay inside these ranges and needn't reach their ends.
Inputs may be any that keep to these rules, and one draw needn't show every extreme that they name: Memory slots 0 to mem_len - 1 of a row are live. With tiles of 128 slots a row has ceil(mem_len / 128) live tiles; the 24 rows together have exactly 96, and in every draw the 3 rows of some index of dp have 3 * 7. Decoder slots 0 to dec_len - 1 of a row are live; every index of dp holds a row with dec_len = 128. `mem_seg`: along a row's slots (tile, then position) never falling, from 0 to the row's pair count minus 1, each of these values on some live slot; slots past mem_len hold the last. `dec_seg`: along a row never falling, with the same pair count as the row's mem_seg, each value on some live slot; slots past dec_len hold the last. Every index of dp holds a row whose dec_seg is 0 throughout and whose dec_len is 128.
All inputs are finite; a program needn't handle non-finite values.
Results may differ from the reference program's by a relative error of at most 0.023.
Values may be sent and summed in bfloat16 or wider, within the bound.
No kernel may reach another device: no remote copies, remote signals or barrier semaphores. Data moves between devices by JAX's collectives and lax.ppermute only.
A program may use at most 320 MiB of HBM per device.

```python
import jax
import jax.numpy as jnp
from jax import lax

D = 1024
HEADS = 16
HEAD_DIM = 64
FF = 4096
MEM = 896
DEC = 128
TILE = 128
ROWS = 3
ROWS_ALL = 24
MEM_TILES = 7
N_DP = 8


def row_plan(key):
    half_rows = ROWS_ALL // 2
    half_groups = N_DP // 2
    keys = jax.random.split(key, 7)
    bucket = jax.random.randint(keys[0], (half_groups,), 1, MEM_TILES + 1)
    jitter = jax.random.randint(keys[1], (half_rows,), -1, 2)
    group_of = jnp.arange(half_rows, dtype=jnp.int32) // ROWS
    full_group = jax.random.randint(keys[2], (), 0, half_groups)
    onehot = (group_of[:, None] == jnp.arange(half_groups, dtype=jnp.int32)[None, :]).astype(jnp.int32)
    first_tiles = jnp.clip(jnp.sum(onehot * bucket[None, :], 1) + jitter, 1, MEM_TILES)
    is_full = group_of == full_group
    first_tiles = jnp.where(is_full, MEM_TILES, first_tiles)
    tile_counts = jnp.concatenate([first_tiles, MEM_TILES + 1 - first_tiles])
    remainder = jax.random.randint(keys[3], (ROWS_ALL,), 4, TILE + 1)
    full_rows = jnp.concatenate([is_full, jnp.zeros((half_rows,), dtype=jnp.bool_)])
    remainder = jnp.where(full_rows, TILE, remainder)
    mem_length = TILE * (tile_counts - 1) + remainder
    pair_count = jax.random.randint(keys[4], (ROWS_ALL,), 1, 5)
    chosen = jax.random.randint(keys[5], (N_DP,), 0, ROWS)
    row_in_group = jnp.arange(ROWS_ALL, dtype=jnp.int32) % ROWS
    span_rows = row_in_group == jnp.repeat(chosen, ROWS)
    pair_count = jnp.where(span_rows, 1, pair_count)
    dec_length = jax.random.randint(keys[6], (ROWS_ALL,), DEC // 2, DEC + 1)
    dec_length = jnp.where(span_rows, DEC, dec_length)
    return (mem_length.astype(jnp.int32), dec_length.astype(jnp.int32), pair_count.astype(jnp.int32))


def segment_ids(key, lengths, pair_count, slot_count):
    reach = lengths // (2 * pair_count)
    jitter = jax.random.randint(key, (lengths.shape[0], 3), 0, 1 << 20) % (reach[:, None] + 1)
    steps_in = jnp.arange(1, 4, dtype=jnp.int32)
    cuts = steps_in[None, :] * lengths[:, None] // pair_count[:, None] + jitter
    used = steps_in[None, :] < pair_count[:, None]
    places = jnp.arange(slot_count, dtype=jnp.int32)
    passed = used[:, None, :] & (places[None, :, None] >= cuts[:, None, :])
    return jnp.sum(passed.astype(jnp.int32), -1).astype(jnp.int32)


def draw_mem_len(key, part):
    plan = row_plan(key)
    return plan[0]


def draw_dec_len(key, part):
    plan = row_plan(key)
    return plan[1]


def draw_mem_seg(key, part):
    plan = row_plan(key)
    own_key = jax.random.fold_in(key, 3)
    segments = segment_ids(own_key, plan[0], plan[2], MEM)
    return segments.reshape(ROWS_ALL, MEM_TILES, TILE)


def draw_dec_seg(key, part):
    plan = row_plan(key)
    own_key = jax.random.fold_in(key, 4)
    return segment_ids(own_key, plan[1], plan[2], DEC)


def steps_of(rng, dims, pieces, smallest, largest):
    def one(position, shards_of):
        steps = jax.random.uniform(jax.random.fold_in(jax.random.fold_in(rng, 6), position), (shards_of,), jnp.float32, smallest / len(pieces), largest / len(pieces))
        return jnp.repeat(jnp.exp(steps), dims[position] // shards_of).reshape((-1,) + (1,) * (len(dims) - position - 1))

    level = one(*pieces[0])
    for cut in pieces[1:]:
        level = level * one(*cut)
    return level


def centred(key, dims, scale, most, cuts=(), kind=jnp.bfloat16):
    entries = scale * jax.random.normal(key, dims, jnp.float32)
    if cuts:
        entries = entries * steps_of(key, dims, cuts, -0.22, 0.18)
    return jnp.clip(entries, -most, most).astype(kind)


def setup_inputs(seed: int = 0) -> dict:
    key_list = jax.random.split(jax.random.key(seed), 17)
    dec_in = centred(key_list[0], (ROWS_ALL, DEC, D), 1.0, 6.0, ((0, 8), (1, 4)))
    memory = centred(key_list[1], (ROWS_ALL, MEM_TILES, TILE, D), 1.0, 6.0, ((0, 8), (2, 4)))
    proj_w = centred(key_list[2], (6, D, D), D ** -0.5, 0.1875, ((1, 32),))
    out_w = centred(key_list[3], (2, D, D), (D // 48) ** -0.5, 1.25, ((1, 32),))
    ffn_in = centred(key_list[4], (D, FF), D ** -0.5, 0.1875, ((0, 32),))
    ffn_out = centred(key_list[5], (FF, D), FF ** -0.5, 0.09375, ((0, 32),))
    biases = centred(key_list[6], (6, D), 0.3, 2.0, (), jnp.float32)
    out_bias = centred(key_list[7], (D,), 0.3, 2.0, (), jnp.float32)
    ffn_bias = centred(key_list[8], (FF,), 0.3, 2.0, (), jnp.float32)
    norm_gain = jnp.clip(1.0 + 0.1 * jax.random.normal(key_list[9], (3, D), jnp.float32), 0.5, 1.5)
    norm_bias = centred(key_list[10], (3, D), 0.3, 2.0, (), jnp.float32)
    mem_len = draw_mem_len(jax.random.fold_in(key_list[16], 71), 0)
    dec_len = draw_dec_len(jax.random.fold_in(key_list[16], 71), 0)
    mem_seg = draw_mem_seg(jax.random.fold_in(key_list[16], 71), 0)
    dec_seg = draw_dec_seg(jax.random.fold_in(key_list[16], 71), 0)
    cotangent = centred(key_list[15], (ROWS_ALL, DEC, D), 1.0, 6.0, ((0, 8), (1, 4)))
    return {"dec_in": dec_in, "memory": memory, "proj_w": proj_w, "out_w": out_w, "ffn_in": ffn_in, "ffn_out": ffn_out, "biases": biases, "out_bias": out_bias, "ffn_bias": ffn_bias, "norm_gain": norm_gain, "norm_bias": norm_bias, "mem_len": mem_len, "dec_len": dec_len, "mem_seg": mem_seg, "dec_seg": dec_seg, "cotangent": cotangent}


EPS = 1e-05
NEG = -1e+30
HIGH = lax.Precision.HIGHEST

@jax.custom_vjp
def low(v):
    return lax.optimization_barrier(v.astype(jnp.bfloat16)).astype(jnp.float32)

@jax.custom_vjp
def low_back(v):
    return v

def low_keep(v):
    return (low(v), None)

def low_pass(kept, grad):
    return (grad,)

def back_keep(v):
    return (v, None)

def back_low(kept, grad):
    return (low(grad),)
low.defvjp(low_keep, low_pass)
low_back.defvjp(back_keep, back_low)

def norm_rows(values, gain, shift):
    centre = values - lax.optimization_barrier(jnp.mean(values, -1, keepdims=True))
    spread = lax.optimization_barrier(jnp.mean(centre * centre, -1, keepdims=True))
    return centre * lax.rsqrt(spread + EPS) * gain + shift

def product(left, weight):
    return jnp.einsum('...i,ij->...j', left, weight, precision=HIGH)

def attend(query, key_rows, value_rows, allowed):
    batch, count_q, width = query.shape
    count_k = key_rows.shape[1]
    query_h = query.reshape(batch, count_q, HEADS, HEAD_DIM)
    key_h = key_rows.reshape(batch, count_k, HEADS, HEAD_DIM)
    value_h = value_rows.reshape(batch, count_k, HEADS, HEAD_DIM)
    scores = low_back(jnp.einsum('bqhd,bkhd->bhqk', query_h, key_h, precision=HIGH) * HEAD_DIM ** (-0.5))
    scores = jnp.where(allowed[:, None], scores, NEG)
    expo = jnp.exp(scores - lax.optimization_barrier(jnp.max(scores, -1, keepdims=True)))
    probs = low(expo / lax.optimization_barrier(jnp.sum(expo, -1, keepdims=True)))
    mixed_h = jnp.einsum('bhqk,bkhd->bqhd', probs, value_h, precision=HIGH)
    return mixed_h.reshape(batch, count_q, width)

def layer_rows(params, tokens, memory, dseg, mseg, dlen, mlen):
    proj_w, out_w, ffn_in, ffn_out, biases, out_bias, ffn_bias, norm_gain, norm_bias = params
    batch = tokens.shape[0]
    memory = memory.reshape(batch, MEM, D)
    mseg = mseg.reshape(batch, MEM)
    places = jnp.arange(DEC, dtype=jnp.int32)
    mplaces = jnp.arange(MEM, dtype=jnp.int32)
    qlive = places[None, :] < dlen[:, None]
    same_pair = dseg[:, :, None] == dseg[:, None, :]
    self_mask = same_pair & (places[None, None, :] <= places[None, :, None]) & qlive[:, None, :] | (places[None, None, :] == places[None, :, None])
    mlive = mplaces[None, :] < mlen[:, None]
    cross_mask = mlive[:, None, :] & ((dseg[:, :, None] == mseg[:, None, :]) | ~qlive[:, :, None])
    query = low_back(low(product(tokens, proj_w[0]) + biases[0]))
    key_rows = low_back(low(product(tokens, proj_w[1])))
    value_rows = low_back(low(product(tokens, proj_w[2]) + biases[1]))
    mixed_self = low_back(low(attend(query, key_rows, value_rows, self_mask)))
    branch_self = low_back(product(mixed_self, out_w[0]) + out_bias)
    hidden_one = norm_rows(tokens + branch_self, norm_gain[0], norm_bias[0])
    query_two = low_back(low(product(low(hidden_one), proj_w[3]) + biases[2]))
    mem_keys = low_back(low(product(memory, proj_w[4])))
    mem_values = low_back(low(product(memory, proj_w[5]) + biases[3]))
    mixed_cross = low_back(low(attend(query_two, mem_keys, mem_values, cross_mask)))
    branch_cross = low_back(product(mixed_cross, out_w[1]) + biases[4])
    hidden_two = norm_rows(hidden_one + branch_cross, norm_gain[1], norm_bias[1])
    inner = low_back(product(low(hidden_two), ffn_in) + ffn_bias)
    active = low(jax.nn.gelu(inner, approximate=False))
    branch_ffn = low_back(product(active, ffn_out) + biases[5])
    normed = norm_rows(hidden_two + branch_ffn, norm_gain[2], norm_bias[2])
    return normed * qlive[:, :, None].astype(jnp.float32)

def reference(dec_in, memory, proj_w, out_w, ffn_in, ffn_out, biases, out_bias, ffn_bias, norm_gain, norm_bias, mem_len, dec_len, mem_seg, dec_seg, cotangent):
    params = tuple((item.astype(jnp.float32) for item in (proj_w, out_w, ffn_in, ffn_out, biases, out_bias, ffn_bias, norm_gain, norm_bias)))
    blocks = ROWS_ALL // 4

    def blocked(array):
        return array.reshape((blocks, 4) + array.shape[1:])
    int_parts = (blocked(dec_seg), blocked(mem_seg), blocked(dec_len), blocked(mem_len))

    def forward(weights, tokens, memory_in):

        def one_block(item):
            return layer_rows(weights, item[0], item[1], item[2], item[3], item[4], item[5])
        outputs = lax.map(jax.checkpoint(one_block), (blocked(tokens), blocked(memory_in)) + int_parts)
        return outputs.reshape(ROWS_ALL, DEC, D)
    output, pullback = jax.vjp(forward, params, dec_in.astype(jnp.float32), memory.astype(jnp.float32))
    grads, grad_dec, grad_mem = pullback(cotangent.astype(jnp.float32))
    return (output.astype(jnp.bfloat16), grad_dec, grad_mem.astype(jnp.bfloat16), grads[0], grads[1], grads[2], grads[3], grads[4], grads[5], grads[6], grads[7], grads[8])
```

```python
import functools

import jax
import jax.numpy as jnp
from jax import lax
from jax.experimental import pallas as pl
from jax.experimental.pallas import tpu as pltpu
from jax.sharding import Mesh
from jax.sharding import PartitionSpec as P

HEADS = 16
HEAD_DIM = 64
LOCAL_HEADS = 4
EPS = 1e-05
NEG = -1e30
F32 = jnp.float32
BF16 = jnp.bfloat16
AXES = ("hi", "x", "core", "z")
ORDER = (0, 2, 1, 3)
VMEM_LIMIT = 60 * 1024 * 1024


def mm(left, right):
    return jnp.dot(left, right, preferred_element_type=F32)


def mm_t(left, right):
    return lax.dot_general(left, right, (((1,), (1,)), ((), ())), preferred_element_type=F32)


def t_mm(left, right):
    return lax.dot_general(left, right, (((0,), (0,)), ((), ())), preferred_element_type=F32)


def pick(array, index, axis=0):
    return lax.dynamic_index_in_dim(array, index, axis, False)


def swap(values, axis):
    return lax.ppermute(values, axis, [(0, 1), (1, 0)])


def head_masks(width):
    lane = lax.broadcasted_iota(jnp.int32, (1, width), 1)
    return [(lane // HEAD_DIM) == h for h in range(LOCAL_HEADS)]


def stack_heads(values, masks):
    zero = jnp.zeros_like(values)
    return jnp.concatenate([jnp.where(m, values, zero) for m in masks], 0)


def join_heads(stacked, masks, rows):
    out = jnp.zeros((rows, stacked.shape[1]), stacked.dtype)
    for h, m in enumerate(masks):
        out = jnp.where(m, stacked[h * rows : (h + 1) * rows], out)
    return out


def softmax_parts(scores, allowed):
    scores = jnp.where(allowed, scores * HEAD_DIM**-0.5, NEG)
    top = jnp.max(scores, -1, keepdims=True)
    expo = jnp.exp(scores - top)
    return expo * (1.0 / jnp.sum(expo, -1, keepdims=True))


def attend_core(q, k, v, allowed):
    rows, width = q.shape
    masks = head_masks(width)
    scores = mm_t(stack_heads(q, masks), k)
    probs = [
        softmax_parts(scores[h * rows : (h + 1) * rows], allowed).astype(BF16)
        for h in range(LOCAL_HEADS)
    ]
    mixed = mm(jnp.concatenate(probs, 0), v)
    return join_heads(mixed, masks, rows).astype(BF16)


def attend_back_core(q, k, v, allowed, grad):
    rows, width = q.shape
    masks = head_masks(width)
    q_heads = stack_heads(q, masks)
    grad_heads = stack_heads(grad, masks)
    scores = mm_t(q_heads, k)
    grad_probs = mm_t(grad_heads, v)
    probs, grad_scores = [], []
    for h in range(LOCAL_HEADS):
        part = slice(h * rows, (h + 1) * rows)
        p = softmax_parts(scores[part], allowed)
        gp = grad_probs[part]
        centre = jnp.sum(p * gp, -1, keepdims=True)
        grad_scores.append((p * (gp - centre)).astype(BF16))
        probs.append(p.astype(BF16))
    probs = jnp.concatenate(probs, 0)
    grad_scores = jnp.concatenate(grad_scores, 0)
    scale = HEAD_DIM**-0.5
    dq = join_heads(mm(grad_scores, k), masks, rows) * scale
    dk = t_mm(grad_scores, q_heads) * scale
    dv = t_mm(probs, grad_heads)
    return dq.astype(BF16), dk.astype(BF16), dv.astype(BF16)


def run(kernel, args, outs, scratch=(), aliases=None, any_args=(), any_outs=()):
    single = not isinstance(outs, (list, tuple))
    out_list = [outs] if single else list(outs)
    vmem = pl.BlockSpec(memory_space=pltpu.VMEM)
    anywhere = pl.BlockSpec(memory_space=pl.ANY)
    base = getattr(kernel, "func", kernel)
    result = pl.pallas_call(
        kernel,
        name=base.__name__,
        in_specs=[anywhere if i in any_args else vmem for i in range(len(args))],
        out_specs=[anywhere if i in any_outs else vmem for i in range(len(out_list))],
        out_shape=out_list,
        scratch_shapes=list(scratch),
        input_output_aliases=aliases or {},
        compiler_params=pltpu.CompilerParams(vmem_limit_bytes=VMEM_LIMIT),
    )(*args)
    return result[0] if single else result


def shaped(shape, dtype):
    return jax.ShapeDtypeStruct(shape, dtype)


def group_place():
    return lax.axis_index("x") * 2 + lax.axis_index("core")


def lanes(start, size):
    return pl.ds(pl.multiple_of(start, 128), size)


def local_bias(ref, row, j):
    n = ref.shape[1]
    return jnp.concatenate(
        [ref[pl.ds(row, 1), lanes(h * (n // 2) + j * (n // 8), n // 8)] for h in range(2)], 1
    )


def whole(refs):
    return jnp.concatenate([r[...] for r in refs], 0)


def halves(product, act, sent_ref, kept_ref):
    half = act.shape[0] // 2
    sent_ref[...] = product(act[half:]).astype(BF16)
    kept_ref[...] = product(act[:half])


def flat_row(ref, r):
    block = ref[:, r]
    return block.reshape(block.shape[0] * block.shape[1], block.shape[2])


def self_fwd_kernel(x0, x1, x2, x3, w, wo, biases, mask, qkv_out, o_out, sent, kept):
    j = group_place()
    tokens = whole([x0, x1, x2, x3])
    width = wo.shape[0]
    bq = local_bias(biases, 0, j)
    bias = jnp.concatenate([bq, jnp.zeros_like(bq), local_bias(biases, 1, j)], 1)
    qkv = (mm(tokens, w[...]) + bias).astype(BF16)
    qkv_out[...] = qkv.reshape(qkv_out.shape)
    for r in range(qkv_out.shape[1]):
        row = flat_row(qkv_out, r)
        out = attend_core(
            row[:, :width], row[:, width : 2 * width], row[:, 2 * width :], mask[r] > 0.5
        )
        o_out[:, r] = out.reshape(o_out.shape[0], o_out.shape[2], width)
    mixed = o_out[...].reshape(tokens.shape[0], width)
    halves(lambda a: mm(a, wo[...]), mixed, sent, kept)


def cross_allowed(qc, kc):
    return (kc >= 0.0) & ((kc == qc) | (qc < -1.5))


def kv_row(kv_refs, r):
    return jnp.concatenate([ref[r] for ref in kv_refs], 0)


def cross_fwd_kernel(
    h0, h1, h2, h3, w, wo, biases, kv0, kv1, kv2, kv3, q_code, k_code, q_out, o_out, sent, kept
):
    j = group_place()
    tokens = whole([h0, h1, h2, h3])
    width = wo.shape[0]
    query = (mm(tokens, w[:, :width]) + local_bias(biases, 2, j)).astype(BF16)
    q_out[...] = query.reshape(q_out.shape)

    def one_row(r, carry):
        kv = kv_row([kv0, kv1, kv2, kv3], r)
        allowed = cross_allowed(q_code[r], k_code[r])
        out = attend_core(flat_row(q_out, r), kv[:, :width], kv[:, width:], allowed)
        o_out[:, r] = out.reshape(o_out.shape[0], o_out.shape[2], width)
        return carry

    lax.fori_loop(0, q_out.shape[1], one_row, 0)
    mixed = o_out[...].reshape(tokens.shape[0], width)
    halves(lambda a: mm(a, wo[...]), mixed, sent, kept)


def ffn_fwd_kernel(h0, h1, h2, h3, w1, w2, bias, g_out, slope_out, sent, kept):
    j = group_place()
    tokens = whole([h0, h1, h2, h3])
    u = mm(tokens, w1[...]) + local_bias(bias, 0, j)
    normal = 0.5 * (1.0 + lax.erf(u * 0.7071067811865476))
    slope_out[...] = normal + u * (0.3989422804014327 * jnp.exp(-0.5 * u * u))
    g_out[...] = (u * normal).astype(BF16)
    halves(lambda a: mm(a, w2[...]), g_out[...], sent, kept)


def ffn_bwd_kernel(f0, f1, f2, f3, w1, w2, slope, du_out, bias_out, sent, kept):
    grads = whole([f0, f1, f2, f3])
    du = (mm_t(grads, w2[...]) * slope[...]).astype(BF16)
    du_out[...] = du
    bias_out[...] = jnp.sum(du.astype(F32), 0, keepdims=True)
    halves(lambda a: mm_t(a, w1[...]), du, sent, kept)


def cross_bwd_kernel(
    f0, f1, f2, f3, w, wo, q, kv0, kv1, kv2, kv3, q_code, k_code,
    dq_out, dkv0, dkv1, dkv2, dkv3, sums, sent, kept, do_ref,
):
    grads = whole([f0, f1, f2, f3])
    width = wo.shape[0]
    do_ref[...] = mm_t(grads, wo[...]).astype(BF16).reshape(do_ref.shape)
    slots = kv0.shape[1]
    sums[...] = jnp.zeros_like(sums)

    def one_row(r, carry):
        kv = kv_row([kv0, kv1, kv2, kv3], r)
        allowed = cross_allowed(q_code[r], k_code[r])
        dq, dk, dv = attend_back_core(
            flat_row(q, r), kv[:, :width], kv[:, width:], allowed, flat_row(do_ref, r)
        )
        dq_out[:, r] = dq.reshape(dq_out.shape[0], dq_out.shape[2], width)
        dkv = jnp.concatenate([dk, dv], 1)
        for d, ref in enumerate([dkv0, dkv1, dkv2, dkv3]):
            ref[r] = dkv[d * slots : (d + 1) * slots]
        sums[1:2, :] += jnp.sum(dv.astype(F32), 0, keepdims=True)
        return carry

    lax.fori_loop(0, q.shape[1], one_row, 0)
    dq = dq_out[...].reshape(grads.shape[0], width)
    sums[0:1, :] = jnp.sum(dq.astype(F32), 0, keepdims=True)
    halves(lambda a: mm_t(a, w[:, :width]), dq, sent, kept)


def self_bwd_kernel(f0, f1, f2, f3, w, wo, qkv, mask, dqkv_out, sums, sent, kept):
    grads = whole([f0, f1, f2, f3])
    width = wo.shape[0]
    shape = (qkv.shape[0], qkv.shape[1], qkv.shape[2], width)
    do = mm_t(grads, wo[...]).astype(BF16).reshape(shape)
    for r in range(shape[1]):
        row = flat_row(qkv, r)
        grad = do[:, r].reshape(row.shape[0], width)
        parts = attend_back_core(
            row[:, :width], row[:, width : 2 * width], row[:, 2 * width :], mask[r] > 0.5, grad
        )
        dqkv_out[:, r] = jnp.concatenate(parts, 1).reshape(shape[0], shape[2], 3 * width)
    dqkv = dqkv_out[...].reshape(grads.shape[0], 3 * width)
    sums[...] = jnp.sum(dqkv.astype(F32), 0, keepdims=True)
    halves(lambda a: mm_t(a, w[...]), dqkv, sent, kept)


def branch_sum(kept, arrived, crossed):
    n = crossed.shape[0]
    return kept[:n] + arrived[:n].astype(F32) + crossed[...].astype(F32)


def normalise(v):
    centre = v - jnp.mean(v, -1, keepdims=True)
    rstd = lax.rsqrt(jnp.mean(centre * centre, -1, keepdims=True) + EPS)
    return centre * rstd, rstd


def denormalise(e, gain, n, rstd):
    a = e * gain
    return rstd * (a - jnp.mean(a, -1, keepdims=True) - n * jnp.mean(a * n, -1, keepdims=True))


def norm_one_kernel(kept, arrived, crossed, own, bias, gains, shifts, n_out, rstd_out, low_out):
    v = branch_sum(kept, arrived, crossed) + bias[...] + own[...].astype(F32)
    n, rstd = normalise(v)
    n_out[...] = n
    rstd_out[...] = jnp.broadcast_to(rstd, rstd_out.shape)
    low_out[...] = (n * gains[0:1] + shifts[0:1]).astype(BF16)


def norm_two_kernel(kept, arrived, crossed, n_one, biases, gains, shifts, n_out, rstd_out, low_out):
    resid = n_one[...] * gains[0:1] + shifts[0:1]
    n, rstd = normalise(branch_sum(kept, arrived, crossed) + biases[4:5] + resid)
    n_out[...] = n
    rstd_out[...] = jnp.broadcast_to(rstd, rstd_out.shape)
    low_out[...] = (n * gains[1:2] + shifts[1:2]).astype(BF16)


def sums_of(e, n, low):
    return jnp.concatenate(
        [
            jnp.sum(e * n, 0, keepdims=True),
            jnp.sum(e, 0, keepdims=True),
            jnp.sum(low.astype(F32), 0, keepdims=True),
            jnp.zeros((5, e.shape[1]), F32),
        ],
        0,
    )


def norm_three_kernel(
    kept, arrived, crossed, n_two, biases, gains, shifts, cot, live, mixed_out, d_out, low_out, sums
):
    resid = n_two[...] * gains[1:2] + shifts[1:2]
    n, rstd = normalise(branch_sum(kept, arrived, crossed) + biases[5:6] + resid)
    mixed_out[...] = ((n * gains[2:3] + shifts[2:3]) * live[...]).astype(BF16)
    e = cot[...].astype(F32) * live[...]
    d = denormalise(e, gains[2:3], n, rstd)
    low = d.astype(BF16)
    d_out[...] = d
    low_out[...] = low
    sums[...] = sums_of(e, n, low)


def norm_back_kernel(which, kept, arrived, crossed, d_in, n, rstd, gains, d_out, low_out, sums):
    e = branch_sum(kept, arrived, crossed) + d_in[...]
    d = denormalise(e, gains[which : which + 1], n[...], rstd[:, 0:1])
    low = d.astype(BF16)
    d_out[...] = d
    low_out[...] = low
    sums[...] = sums_of(e, n[...], low)


def cut_cols_kernel(proj, first, *outs):
    j = group_place()
    n, _, width = proj.shape
    ff = first.shape[1]
    for d, out in enumerate(outs):
        target = jnp.bitwise_xor(j, d)
        at = 0
        for m in range(n):
            for h in range(2):
                out[:, at : at + width // 8] = proj[
                    m, :, lanes(h * (width // 2) + target * (width // 8), width // 8)
                ]
                at += width // 8
        for h in range(2):
            out[:, at : at + ff // 8] = first[:, lanes(h * (ff // 2) + target * (ff // 8), ff // 8)]
            at += ff // 8


def pack_kernel(e0, e1, e2, e3, out_w, second, buf_a, buf_b, buf_c):
    j = group_place()
    quarter = out_w.shape[2] // 4
    three = 3 * quarter
    rows = e0.shape[0]
    for d, e in enumerate([e0, e1, e2, e3]):
        at = jnp.bitwise_xor(j, d)
        buf_a[at, :, :three] = e[:, :three]
        buf_b[at, :, :three] = e[:, three : 2 * three]
        buf_c[at] = e[:, 2 * three :]
    for i in range(4):
        buf_a[i, :, three:] = out_w[0, :, i * quarter : (i + 1) * quarter]
        buf_b[i, :, three:] = out_w[1, :, i * quarter : (i + 1) * quarter]
        buf_c[4 + i] = second[i * rows : (i + 1) * rows]


def place_kernel(n_z, ffn, *refs):
    blocks, wcol, wrow = refs[: 2 * n_z], refs[2 * n_z], refs[2 * n_z + 1]
    hi = lax.axis_index("hi")
    z = lax.axis_index("z")
    cols = wcol.shape[-1]
    rows = wcol.shape[-2]
    for half in range(2):
        h = hi if half == 0 else 1 - hi
        for k in range(n_z):
            zz = lax.rem(z + k, n_z)
            block = blocks[half * n_z + k]
            for i in range(4):
                if ffn:
                    wcol[h, i, zz] = block[i]
                    wrow[h, zz, i * rows : (i + 1) * rows] = block[4 + i]
                else:
                    wcol[h, i, zz] = block[i, :, :cols]
                    quarter = block.shape[2] - cols
                    wrow[h, zz, :, i * quarter : (i + 1) * quarter] = block[i, :, cols:]


def select_rows(dst, pieces, n_z, half_index):
    z = lax.axis_index("z")
    at = 0
    for piece in pieces:
        count, width = piece.shape
        for k in range(n_z):
            start = lax.rem(z + k, n_z) * (width // n_z) + half_index * (width // n_z // 2)
            dst[at : at + count, k * 128 : (k + 1) * 128] = piece[:, lanes(start, 128)]
        at += count


def select_cols(dst, pieces, n_z):
    z = lax.axis_index("z")
    at = 0
    for piece in pieces:
        count, width = piece.shape
        size = width // n_z
        for k in range(n_z):
            start = lax.rem(z + k, n_z) * size
            dst[at : at + count, k * size : (k + 1) * size] = piece[:, lanes(start, size)]
        at += count


def put_cols(out, at, block):
    n_z, rows = out.shape[0], out.shape[1]
    cols = block.shape[1]
    out[:, :, at : at + cols] = block.astype(BF16).reshape(n_z, rows, cols)


def put_rows(out, at, block):
    n_z, rows = out.shape[0], out.shape[1]
    size = block.shape[1] // n_z
    for k in range(n_z):
        for i in range(block.shape[0] // rows):
            out[k, :, at + i * size : at + (i + 1) * size] = block[
                i * rows : (i + 1) * rows, k * size : (k + 1) * size
            ].astype(BF16)


def half_of(ref, h):
    size = ref.shape[1] // 2
    return ref[:, lanes(h * size, size)]


def ffn_grad_kernel(n_z, a0, a1, a2, a3, du, g, f0, f1, f2, f3, kept, sent, left, right):
    hi = lax.axis_index("hi")
    select_cols(right, [f0, f1, f2, f3], n_z)
    for out, h in ((sent, 1 - hi), (kept, hi)):
        select_rows(left, [a0, a1, a2, a3], n_z, h)
        put_cols(out, 0, t_mm(left[...], du[...]))
        put_rows(out, du.shape[1], t_mm(half_of(g, h), right[...]))


def memory_grad_kernel(n_z, *refs):
    mems, dkvs, kept, sent, left, right, total = refs[:4], refs[4:8], *refs[8:]
    hi = lax.axis_index("hi")
    row = pl.program_id(0)
    slots = mems[0].shape[1]
    for d in range(4):
        right[d * slots : (d + 1) * slots] = dkvs[d][0]
    for s, h in ((0, hi), (1, 1 - hi)):
        select_rows(left, [m.at[0] for m in mems], n_z, h)
        part = t_mm(left[...], right[...])

        @pl.when(row == 0)
        def _():
            total[s] = part

        @pl.when(row > 0)
        def _():
            total[s] += part

    @pl.when(row == pl.num_programs(0) - 1)
    def _():
        put_cols(kept, 0, total[0])
        put_cols(sent, 0, total[1])


def cross_grad_kernel(
    n_z, h0, h1, h2, h3, dq, kv_kept, kv_sent, o2, f20, f21, f22, f23, o1, f10, f11, f12, f13,
    kept, sent, left, right,
):
    hi = lax.axis_index("hi")
    c_q, c_kv = dq.shape[1], kv_kept.shape[2]
    for out, h, kv in ((sent, 1 - hi, kv_sent), (kept, hi, kv_kept)):
        select_rows(left, [h0, h1, h2, h3], n_z, h)
        put_cols(out, 0, t_mm(left[...], dq[...]))
        out[:, :, c_q : c_q + c_kv] = kv[...]
    at = c_q + c_kv
    for o, f in ((o1, [f10, f11, f12, f13]), (o2, [f20, f21, f22, f23])):
        select_cols(right, f, n_z)
        for out, h in ((sent, 1 - hi), (kept, hi)):
            put_rows(out, at, t_mm(half_of(o, h), right[...]))
        at += right.shape[1] // n_z


def self_grad_kernel(n_z, x0, x1, x2, x3, dqkv, sums, kept, sent, left):
    hi = lax.axis_index("hi")
    rows = kept.shape[1] - 16
    cols = dqkv.shape[1]
    lower = jnp.broadcast_to(sums[...], (16, cols)).astype(BF16)
    for out, h in ((sent, 1 - hi), (kept, hi)):
        select_rows(left, [x0, x1, x2, x3], n_z, h)
        block = t_mm(left[...], dqkv[...]).astype(BF16)
        for k in range(n_z):
            out[k, :rows] = block[k * rows : (k + 1) * rows]
            out[k, rows:] = lower


def pair_sum_kernel(kept, arrived, own, *sent):
    own[...] = kept[0].astype(F32) + arrived[0].astype(F32)
    for k, out in enumerate(sent):
        out[...] = (kept[k + 1].astype(F32) + arrived[k + 1].astype(F32)).astype(BF16)


def final_sum_kernel(cols, own, *refs):
    total = own[...]
    arrived, outs = refs[: -len(cols)], refs[-len(cols) :]
    for a in arrived:
        total = total + a[...].astype(F32)
    at = 0
    for out, size in zip(outs, cols):
        out[...] = total[:, at : at + size].astype(BF16)
        at += size


def places(index):
    h = jnp.bitwise_xor(lax.axis_index("hi"), (index >> 2) & 1)
    return h, jnp.bitwise_xor(group_place(), index & 3)


def ffn_out_kernel(*refs):
    pieces, first, second = refs[:8], refs[8], refs[9]
    rows = pieces[0].shape[0]
    ff = first.shape[1]
    width = second.shape[1]
    size = width // 4
    for index, piece in enumerate(pieces):
        h, j = places(index)
        for half in range(2):
            first[
                pl.ds(pl.multiple_of(h * rows, 8), rows),
                lanes(half * (ff // 2) + j * (ff // 8), ff // 8),
            ] = piece[:, half * (ff // 8) : (half + 1) * (ff // 8)].astype(F32)
        for i in range(4):
            at = ff // 4 + i * size
            second[
                pl.ds(pl.multiple_of(h * 4 * rows + i * rows, 8), rows), lanes(j * size, size)
            ] = piece[:, at : at + size].astype(F32)


def place_cols(out, m, rows, piece, at):
    width = out.shape[2]
    for index, p in enumerate(piece):
        h, j = places(index)
        for half in range(2):
            lo = at + half * (width // 8)
            out[
                m,
                pl.ds(pl.multiple_of(h * rows, 8), rows),
                lanes(half * (width // 2) + j * (width // 8), width // 8),
            ] = p[:rows, lo : lo + width // 8].astype(F32)


def cross_out_kernel(*refs):
    pieces, g_proj, g_out, work, sem = refs[:8], *refs[8:]
    rows = pieces[0].shape[0]
    width = work.shape[2]
    for m in range(3):
        place_cols(work, m, rows, pieces, m * (width // 4))
    copy = pltpu.make_async_copy(work, g_proj.at[pl.ds(3, 3)], sem)
    copy.start()
    for index, piece in enumerate(pieces):
        h, j = places(index)
        for m in range(2):
            at = 3 * (width // 4) + m * (width // 4)
            g_out[
                m, pl.ds(pl.multiple_of(h * rows, 8), rows), lanes(j * (width // 4), width // 4)
            ] = piece[:, at : at + width // 4].astype(F32)
    copy.wait()


def self_out_kernel(*refs):
    pieces, _, g_proj, sums, work, sem = refs[:8], *refs[8:]
    rows = pieces[0].shape[0] - 16
    width = work.shape[2]
    for m in range(3):
        place_cols(work, m, rows, pieces, m * (width // 4))
    copy = pltpu.make_async_copy(work, g_proj.at[pl.ds(0, 3)], sem)
    copy.start()
    sums[...] = jnp.zeros_like(sums)
    for index in range(4):
        _, j = places(index)
        for m in range(3):
            for half in range(2):
                lo = m * (width // 4) + half * (width // 8)
                sums[m : m + 1, lanes(half * (width // 2) + j * (width // 8), width // 8)] = (
                    pieces[index][rows : rows + 16, lo : lo + width // 8].astype(F32)[0:1]
                )
    copy.wait()


def small_kernel(s3, s2, s1, cross_sums, ff_sum, out):
    j = group_place()
    width = out.shape[1]
    ff = ff_sum.shape[1] * 4
    out[...] = jnp.zeros_like(out)
    for half in range(2):
        at = lanes(half * (width // 2) + j * (width // 8), width // 8)
        part = slice(half * (width // 8), (half + 1) * (width // 8))
        out[0:1, at] = cross_sums[0:1, part]
        out[1:2, at] = cross_sums[1:2, part]
    out[2:3] = s2[2:3]
    out[3:4] = s3[2:3]
    out[4:5] = s1[2:3]
    ff_rows = ff // width
    per = ff // 8
    for half in range(2):
        flat_at = half * (ff // 2) + j * per
        row = 5 + flat_at // width
        out[pl.ds(row, 1), lanes(lax.rem(flat_at, width), per)] = ff_sum[
            0:1, half * per : (half + 1) * per
        ]
    at = 5 + ff_rows
    for i, s in enumerate([s1, s2, s3]):
        out[at + i : at + i + 1] = s[0:1]
        out[at + 3 + i : at + 4 + i] = s[1:2]


def per_device(
    dec_in,
    memory,
    proj_w,
    out_w,
    ffn_in,
    ffn_out,
    biases,
    out_bias,
    ffn_bias,
    norm_gain,
    norm_bias,
    mem_len,
    dec_len,
    mem_seg,
    dec_seg,
    cotangent,
):
    n_hi = lax.axis_size("hi")
    n_z = lax.axis_size("z")
    hi = lax.axis_index("hi")
    zi = lax.axis_index("z")
    j = group_place()
    fast = n_hi == 2 and n_z == 4
    row_count, query_count, width = dec_in.shape
    tile_count, tile_part = memory.shape[1], memory.shape[2]
    own_tokens = row_count * query_count
    all_tokens = 4 * own_tokens
    slots = tile_count * tile_part
    ff_width = ffn_in.shape[1]
    local = width // 4
    ff_local = ff_width // 4

    def turned(index):
        return (index & 1) * 2 + (index >> 1)

    to_rows = [
        ((h * 4 + a) * 4 + b, (h * 4 + turned(b)) * 4 + turned(a))
        for h in range(n_hi)
        for a in range(4)
        for b in range(4)
    ]

    def transpose(values):
        return lax.ppermute(values, AXES, to_rows)

    def shift_z(values, k):
        return lax.ppermute(values, "z", [(i, (i + k) % n_z) for i in range(n_z)])

    def gather_j(values):
        across = swap(values, "x")
        return [values, across, swap(values, "core"), swap(across, "core")]

    def cross_links(sent, kept):
        arrived = swap(sent, "core")
        half = kept.shape[0] // 2
        middle = (kept[half:] + arrived[half:].astype(F32)).astype(BF16)
        return kept, arrived, swap(middle, "x")

    def split_cols(full):
        n, total, cols = full.shape
        split = pick(full.reshape(n, total, 2, 4, cols // 8), j, 3)
        return split.transpose(1, 0, 2, 3).reshape(total, n * cols // 4)

    def split_rows(full):
        total, cols = full.shape
        return pick(full.reshape(2, 4, total // 8, cols), j, 1).reshape(total // 4, cols)

    def near_blocks(block):
        return [block] + [shift_z(block, -k) for k in range(1, n_z)]

    def after(values, *others):
        return lax.optimization_barrier((values, *others))[0]

    segs = transpose(jnp.concatenate([mem_seg.reshape(row_count, -1), dec_seg], 1))
    own_in = transpose(dec_in).reshape(own_tokens, width)
    tokens = gather_j(own_in)
    if fast:
        rows = proj_w.shape[1]
        cut = shaped((rows, 6 * local + ff_local), BF16)
        e = run(cut_cols_kernel, [proj_w, ffn_in], [cut] * 4)
        diag = [(0, 3), (1, 2), (2, 1), (3, 0)]
        e = [e[0], swap(e[1], "core"), swap(e[2], "x"), lax.ppermute(e[3], ("x", "core"), diag)]
        buf_a, buf_b, buf_c = run(
            pack_kernel,
            e + [out_w, ffn_out],
            [shaped((4, rows, width), BF16)] * 2 + [shaped((8, rows, ff_local), BF16)],
        )

        def placed(near, cols, row_rows, ffn):
            wcol, wrow = run(
                functools.partial(place_kernel, n_z, ffn),
                near + [swap(b, "hi") for b in near],
                [
                    shaped((2, 4, n_z, rows, cols), BF16),
                    shaped((2, n_z, row_rows, width), BF16),
                ],
            )
            return wcol.reshape(-1, cols), wrow.reshape(-1, width)

        near_a = near_blocks(buf_a)
        w_qkv, w_out = placed(near_a, 3 * local, rows, False)
        memory = after(memory, near_a[1])
        near_b = near_blocks(after(buf_b, near_a[1]))
        w_two, w_out2 = placed(near_b, 3 * local, rows, False)
        near_c = near_blocks(after(buf_c, near_b[1]))
        w_first, w_second = placed(near_c, ff_local, ffn_out.shape[0], True)
    else:
        proj_full = lax.all_gather(proj_w, AXES, axis=1, tiled=True)
        out_full = lax.all_gather(out_w, AXES, axis=1, tiled=True)
        w_qkv, w_two = split_cols(proj_full[:3]), split_cols(proj_full[3:])
        w_out, w_out2 = split_rows(out_full[0]), split_rows(out_full[1])
        w_first = split_cols(lax.all_gather(ffn_in, AXES, axis=0, tiled=True)[None])
        w_second = split_rows(lax.all_gather(ffn_out, AXES, axis=0, tiled=True))

    mems = gather_j(transpose(memory).reshape(row_count * slots, width))
    own_cot = transpose(after(cotangent, mems[1])).reshape(own_tokens, width)
    mem_full = mem_seg.shape[1] * mem_seg.shape[2]
    group = hi * 4 + turned(zi)
    own_dlen = lax.dynamic_slice_in_dim(dec_len, group * row_count, row_count)
    own_mlen = lax.dynamic_slice_in_dim(mem_len, group * row_count, row_count)
    parts = [turned(j ^ d) for d in ORDER]
    mem_parts = segs[:, :mem_full].reshape(row_count, tile_count, 4, tile_part)
    dec_parts = segs[:, mem_full:].reshape(row_count, 4, query_count)
    dseg = jnp.concatenate([pick(dec_parts, p, 1) for p in parts], 1)
    mseg = jnp.concatenate([pick(mem_parts, p, 2).reshape(row_count, slots) for p in parts], 1)
    dpos = jnp.concatenate([p * query_count + jnp.arange(query_count) for p in parts])
    in_tile = jnp.arange(tile_count)[:, None] * (4 * tile_part) + jnp.arange(tile_part)[None, :]
    mpos = jnp.concatenate([(in_tile + p * tile_part).reshape(-1) for p in parts])
    dlive = dpos[None, :] < own_dlen[:, None]
    mlive = mpos[None, :] < own_mlen[:, None]
    self_mask = (
        (dseg[:, :, None] == dseg[:, None, :])
        & (dpos[None, None, :] <= dpos[None, :, None])
        & dlive[:, None, :]
    ) | (dpos[None, None, :] == dpos[None, :, None])
    self_mask = self_mask.astype(F32)
    q_code = jnp.where(dlive, dseg.astype(F32), -2.0)[:, :, None]
    k_code = jnp.where(mlive, mseg.astype(F32), -1.0)[:, None, :]
    own_pos = parts[0] * query_count + jnp.arange(query_count)
    own_live = (own_pos[None, :] < own_dlen[:, None]).astype(F32).reshape(own_tokens, 1)
    bias_v2 = pick(biases[3].reshape(2, 4, width // 8), j, 1).reshape(local)
    bias_kv = jnp.concatenate([jnp.zeros((local,), F32), bias_v2])

    part = width // n_z // 2

    def sum_rep(kept, sent, cols):
        arrived = swap(sent, "hi")
        shape = kept.shape[1:]
        own, *out = run(
            pair_sum_kernel,
            [kept, arrived],
            [shaped(shape, F32)] + [shaped(shape, BF16)] * (n_z - 1),
        )
        arrived = [shift_z(block, i + 1) for i, block in enumerate(out)]
        return run(
            functools.partial(final_sum_kernel, cols),
            [own, *arrived],
            [shaped((shape[0], c), BF16) for c in cols],
        )

    to_plane = [
        ((h * 4 + 2 * a + b) * 4 + z, (b * 4 + z) * 4 + 2 * h + a)
        for h in range(2)
        for a in range(2)
        for b in range(2)
        for z in range(4)
    ]

    def gather_dp(block):
        pieces = [block, swap(block, "x")]
        pieces = pieces + [swap(p, "hi") for p in pieces]
        return [q for p in pieces for q in (p, swap(p, "core"))]

    def spread(blocks):
        return gather_dp(
            jnp.concatenate([blocks[0], lax.ppermute(blocks[1], AXES, to_plane)], 1)
        )

    def both(cols, rows=part):
        return [shaped((n_z, rows, cols), BF16)] * 2

    def tokens_scratch(cols):
        return pltpu.VMEM((all_tokens, cols), BF16)


    heads = shaped((4, row_count, query_count, local), BF16)
    sent = shaped((all_tokens // 2, width), BF16)
    kept = shaped((all_tokens // 2, width), F32)
    own_f32 = shaped((own_tokens, width), F32)
    own_low = shaped((own_tokens, width), BF16)
    rstd_shape = shaped((own_tokens, 128), F32)
    sums_shape = shaped((8, width), F32)
    qkv, mixed_self, s, k = run(
        self_fwd_kernel,
        [*tokens, w_qkv, w_out, biases, self_mask],
        [shaped((4, row_count, query_count, 3 * local), BF16), heads, sent, kept],
    )
    n_one, rstd_one, one_low = run(
        norm_one_kernel,
        [*cross_links(s, k), own_in, out_bias[None], norm_gain, norm_bias],
        [own_f32, rstd_shape, own_low],
    )
    ones = gather_j(one_low)
    w_kv2 = w_two[:, local:]
    kv2 = [(mm(m, w_kv2) + bias_kv).astype(BF16).reshape(row_count, slots, -1) for m in mems]
    query_two, mixed_cross, s, k = run(
        cross_fwd_kernel,
        [*ones, w_two, w_out2, biases, *kv2, q_code, k_code],
        [heads, heads, sent, kept],
    )
    n_two, rstd_two, two_low = run(
        norm_two_kernel,
        [*cross_links(s, k), n_one, biases, norm_gain, norm_bias],
        [own_f32, rstd_shape, own_low],
    )
    twos = gather_j(two_low)
    active, slope, s, k = run(
        ffn_fwd_kernel,
        [*twos, w_first, w_second, ffn_bias[None]],
        [shaped((all_tokens, ff_local), BF16), shaped((all_tokens, ff_local), F32), sent, kept],
    )
    mixed_out, d_three, own_f3, sums_three = run(
        norm_three_kernel,
        [*cross_links(s, k), n_two, biases, norm_gain, norm_bias, own_cot, own_live],
        [own_low, own_f32, own_low, sums_shape],
    )
    mixed_out = transpose(mixed_out.reshape(dec_in.shape))

    f3 = gather_j(own_f3)
    du, ff_sum, s, k = run(
        ffn_bwd_kernel,
        [*f3, w_first, w_second, slope],
        [shaped((all_tokens, ff_local), BF16), shaped((1, ff_local), F32), sent, kept],
    )
    k, arrived, crossed = cross_links(s, k)
    if fast:
        ffn_cols = (ff_local, width)
        kept_c, sent_c = run(
            functools.partial(ffn_grad_kernel, n_z),
            [*twos, du, active, *f3],
            both(sum(ffn_cols)),
            scratch=[tokens_scratch(width // 2), tokens_scratch(width)],
        )
        crossed = after(crossed, sent_c)
        ffn_gradients = run(
            ffn_out_kernel,
            spread(sum_rep(kept_c, sent_c, ffn_cols)),
            [shaped((width // n_z, ff_width), F32), shaped((ff_width // n_z, width), F32)],
        )

    d_two, own_f2, sums_two = run(
        functools.partial(norm_back_kernel, 1),
        [k, arrived, crossed, d_three, n_two, rstd_two, norm_gain],
        [own_f32, own_low, sums_shape],
    )
    f2 = gather_j(own_f2)
    memory_rows = shaped((row_count, slots, 2 * local), BF16)
    dq2, *dkv2, cross_sums, s, k = run(
        cross_bwd_kernel,
        [*f2, w_two, w_out2, query_two, *kv2, q_code, k_code],
        [heads] + [memory_rows] * 4 + [shaped((8, local), F32), sent, kept],
        scratch=[pltpu.VMEM(heads.shape, BF16)],
    )
    d_one, own_f1, sums_one = run(
        functools.partial(norm_back_kernel, 0),
        [*cross_links(s, k), d_two, n_one, rstd_one, norm_gain],
        [own_f32, own_low, sums_shape],
    )
    f1 = gather_j(own_f1)
    dqkv, sum_qkv, s, k = run(
        self_bwd_kernel,
        [*f1, w_qkv, w_out, qkv, self_mask],
        [
            shaped((4, row_count, query_count, 3 * local), BF16),
            shaped((1, 3 * local), F32),
            sent,
            kept,
        ],
    )
    k, arrived, crossed = cross_links(s, k)
    own_d = k[:own_tokens] + arrived[:own_tokens].astype(F32) + crossed.astype(F32) + d_one
    d_dec = transpose(own_d.astype(BF16).reshape(dec_in.shape)).astype(F32)

    flat_kv = [d.reshape(row_count * slots, -1) for d in dkv2]
    far = [swap(mm_t(d, w_kv2).astype(BF16), "core") for d in flat_kv[2:]]
    across = (mm_t(flat_kv[1], w_kv2) + far[1].astype(F32)).astype(BF16)
    near = mm_t(flat_kv[0], w_kv2) + far[0].astype(F32)
    d_memory = (near + swap(across, "x").astype(F32)).astype(BF16)
    d_memory = transpose(d_memory.reshape(memory.shape))

    ff_rows = ff_width // width
    n_small = -(-(11 + ff_rows) // 8) * 8
    small = run(
        small_kernel,
        [sums_three, sums_two, sums_one, cross_sums, ff_sum],
        shaped((n_small, width), F32),
    )
    if fast:
        for axis in ("core", "x", "hi"):
            small = small + swap(small, axis)
        for step in (1, 2):
            small = small + lax.ppermute(small, "z", [(i, i ^ step) for i in range(n_z)])
    else:
        small = lax.psum(small, AXES)

    dq2 = dq2.reshape(all_tokens, local)
    dqkv = dqkv.reshape(all_tokens, -1)
    o1 = mixed_self.reshape(all_tokens, local)
    o2 = mixed_cross.reshape(all_tokens, local)
    if fast:
        g_first, g_second = ffn_gradients

        def row_block(cols):
            return pl.BlockSpec((1, slots, cols), lambda r: (r, 0, 0))

        def fixed(array):
            return pl.BlockSpec(array.shape, lambda r: (0, 0, 0))

        outs = both(2 * local)
        kept_m, sent_m = pl.pallas_call(
            functools.partial(memory_grad_kernel, n_z),
            grid=(row_count,),
            in_specs=[row_block(width)] * 4 + [row_block(2 * local)] * 4,
            out_specs=[fixed(o) for o in outs],
            out_shape=outs,
            scratch_shapes=[
                pltpu.VMEM((4 * slots, width // 2), BF16),
                pltpu.VMEM((4 * slots, 2 * local), BF16),
                pltpu.VMEM((2, width // 2, 2 * local), F32),
            ],
            compiler_params=pltpu.CompilerParams(vmem_limit_bytes=VMEM_LIMIT),
        )(*[m.reshape(row_count, slots, width) for m in mems], *dkv2)
        kept_b, sent_b = run(
            functools.partial(cross_grad_kernel, n_z),
            [*ones, dq2, kept_m, sent_m, o2, *f2, o1, *f1],
            both(5 * local),
            scratch=[tokens_scratch(width // 2), tokens_scratch(width)],
        )
        g_proj, g_out = run(
            cross_out_kernel,
            spread(sum_rep(kept_b, sent_b, (3 * local, 2 * local))),
            [shaped((6, width // n_z, width), F32), shaped((2, width // n_z, width), F32)],
            scratch=[pltpu.VMEM((3, width // n_z, width), F32), pltpu.SemaphoreType.DMA],
            any_outs=(0,),
        )
        kept_a, sent_a = run(
            functools.partial(self_grad_kernel, n_z),
            [*tokens, dqkv, sum_qkv],
            both(3 * local, part + 16),
            scratch=[tokens_scratch(width // 2)],
        )
        g_proj, sums_qkv = run(
            self_out_kernel,
            gather_dp(sum_rep(kept_a, sent_a, (3 * local,))[0]) + [g_proj],
            [shaped(g_proj.shape, F32), shaped((8, width), F32)],
            scratch=[pltpu.VMEM((3, width // n_z, width), F32), pltpu.SemaphoreType.DMA],
            aliases={8: 0},
            any_args=(8,),
            any_outs=(0,),
        )
    else:
        mine = (jnp.arange(4) == j).astype(F32)[:, None]

        def col_grads(left, grads, n):
            cols = grads.shape[1] // n * 4
            total = t_mm(left, grads).reshape(-1, n, 2, 1, cols // 8)
            full = (total * mine).reshape(-1, n, cols).transpose(1, 0, 2)
            out = lax.psum_scatter(full.astype(BF16), "z", scatter_dimension=1, tiled=True)
            return lax.psum(out.astype(F32), ("hi", "x", "core"))

        def row_grads(left, grads):
            total = t_mm(left, grads).reshape(2, 1, -1, width)
            full = (total * mine[:, :, None]).reshape(-1, width)
            out = lax.psum_scatter(full.astype(BF16), "z", scatter_dimension=0, tiled=True)
            return lax.psum(out.astype(F32), ("hi", "x", "core"))

        def joined(pieces):
            return jnp.concatenate(pieces, 0)

        g_first = col_grads(joined(twos), du, 1)[0]
        g_second = row_grads(active, joined(f3))
        g_qkv = col_grads(joined(tokens), dqkv, 3)
        g_q2 = col_grads(joined(ones), dq2, 1)
        g_kv2 = col_grads(joined(mems), joined(flat_kv), 2)
        g_proj = jnp.concatenate([g_qkv, g_q2, g_kv2], 0)
        g_out = jnp.stack([row_grads(o1, joined(f1)), row_grads(o2, joined(f2))])
        sums_qkv = (sum_qkv.reshape(3, 2, 1, width // 8) * mine).reshape(3, width)
        sums_qkv = lax.psum(sums_qkv, AXES)

    n_part = width // n_z
    cut = lax.dynamic_slice_in_dim(small, zi * n_part, n_part, 1)
    cut_qkv = lax.dynamic_slice_in_dim(sums_qkv, zi * n_part, n_part, 1)
    g_biases = jnp.concatenate([cut_qkv[0:1], cut_qkv[2:3], cut[0:4]], 0)
    g_out_bias = cut[4]
    g_ffn_bias = lax.dynamic_slice_in_dim(
        small[5 : 5 + ff_rows].reshape(-1), zi * (ff_width // n_z), ff_width // n_z
    )
    g_gain = cut[5 + ff_rows : 8 + ff_rows]
    g_shift = cut[8 + ff_rows : 11 + ff_rows]
    return (
        mixed_out,
        d_dec,
        d_memory,
        g_proj,
        g_out,
        g_first,
        g_second,
        g_biases,
        g_out_bias,
        g_ffn_bias,
        g_gain,
        g_shift,
    )


def solution(mesh):
    devices = mesh.devices
    inner = Mesh(devices.reshape(devices.shape[0] // 4, 2, 2, devices.shape[1]), AXES)
    dp = ("hi", "x", "core")
    in_specs = (
        P(dp, "z", None),
        P(dp, None, "z", None),
        P(None, AXES, None),
        P(None, AXES, None),
        P(AXES, None),
        P(AXES, None),
        P(),
        P(),
        P(),
        P(),
        P(),
        P(),
        P(),
        P(dp, None, None),
        P(dp, None),
        P(dp, "z", None),
    )
    out_specs = (
        P(dp, "z", None),
        P(dp, "z", None),
        P(dp, None, "z", None),
        P(None, "z", None),
        P(None, "z", None),
        P("z", None),
        P("z", None),
        P(None, "z"),
        P("z"),
        P("z"),
        P(None, "z"),
        P(None, "z"),
    )
    return jax.shard_map(
        per_device, mesh=inner, in_specs=in_specs, out_specs=out_specs, check_vma=False
    )
```

```python
import functools

import jax
import jax.numpy as jnp
from jax import lax
from jax.experimental import pallas as pl
from jax.experimental.pallas import tpu as pltpu
from jax.sharding import Mesh
from jax.sharding import PartitionSpec as P

HEADS = 16
HEAD_DIM = 64
LOCAL_HEADS = 4
EPS = 1e-05
NEG = -1e30
F32 = jnp.float32
BF16 = jnp.bfloat16
AXES = ("hi", "x", "core", "z")
ORDER = (0, 2, 1, 3)
VMEM_LIMIT = 60 * 1024 * 1024


def mm(left, right):
    return jnp.dot(left, right, preferred_element_type=F32)


def mm_t(left, right):
    return lax.dot_general(left, right, (((1,), (1,)), ((), ())), preferred_element_type=F32)


def t_mm(left, right):
    return lax.dot_general(left, right, (((0,), (0,)), ((), ())), preferred_element_type=F32)


def pick(array, index, axis=0):
    return lax.dynamic_index_in_dim(array, index, axis, False)


def swap(values, axis):
    return lax.ppermute(values, axis, [(0, 1), (1, 0)])


def head_masks(width):
    lane = lax.broadcasted_iota(jnp.int32, (1, width), 1)
    return [(lane // HEAD_DIM) == h for h in range(LOCAL_HEADS)]


def stack_heads(values, masks):
    zero = jnp.zeros_like(values)
    return jnp.concatenate([jnp.where(m, values, zero) for m in masks], 0)


def join_heads(stacked, masks, rows):
    out = jnp.zeros((rows, stacked.shape[1]), stacked.dtype)
    for h, m in enumerate(masks):
        out = jnp.where(m, stacked[h * rows : (h + 1) * rows], out)
    return out


def softmax_parts(scores, allowed):
    scores = jnp.where(allowed, scores * HEAD_DIM**-0.5, NEG)
    top = jnp.max(scores, -1, keepdims=True)
    expo = jnp.exp(scores - top)
    return expo * (1.0 / jnp.sum(expo, -1, keepdims=True))


def attend_core(q, k, v, allowed):
    rows, width = q.shape
    masks = head_masks(width)
    scores = mm_t(stack_heads(q, masks), k)
    probs = [
        softmax_parts(scores[h * rows : (h + 1) * rows], allowed).astype(BF16)
        for h in range(LOCAL_HEADS)
    ]
    mixed = mm(jnp.concatenate(probs, 0), v)
    return join_heads(mixed, masks, rows).astype(BF16)


def attend_back_core(q, k, v, allowed, grad):
    rows, width = q.shape
    masks = head_masks(width)
    q_heads = stack_heads(q, masks)
    grad_heads = stack_heads(grad, masks)
    scores = mm_t(q_heads, k)
    grad_probs = mm_t(grad_heads, v)
    probs, grad_scores = [], []
    for h in range(LOCAL_HEADS):
        part = slice(h * rows, (h + 1) * rows)
        p = softmax_parts(scores[part], allowed)
        gp = grad_probs[part]
        centre = jnp.sum(p * gp, -1, keepdims=True)
        grad_scores.append((p * (gp - centre)).astype(BF16))
        probs.append(p.astype(BF16))
    probs = jnp.concatenate(probs, 0)
    grad_scores = jnp.concatenate(grad_scores, 0)
    scale = HEAD_DIM**-0.5
    dq = join_heads(mm(grad_scores, k), masks, rows) * scale
    dk = t_mm(grad_scores, q_heads) * scale
    dv = t_mm(probs, grad_heads)
    return dq.astype(BF16), dk.astype(BF16), dv.astype(BF16)


KERNEL_US = {
    "cut_cols_kernel": 2,
    "pack_kernel": 2,
    "place_kernel": 4,
    "self_fwd_kernel": 5,
    "norm_one_kernel": 3,
    "memory_kv_kernel": 7,
    "cross_fwd_kernel": 8,
    "norm_two_kernel": 3,
    "place_ffn_kernel": 5,
    "ffn_fwd_kernel": 6,
    "norm_three_kernel": 3,
    "ffn_bwd_kernel": 6,
    "ffn_grad_kernel": 6,
    "norm_back_kernel": 3,
    "cross_bwd_kernel": 11,
    "memory_grad_kernel": 9,
    "cross_grad_kernel": 4,
    "self_bwd_kernel": 6,
    "self_grad_kernel": 5,
    "memory_back_kernel": 8,
    "pair_sum_kernel": 3,
    "final_sum_kernel": 2,
    "cross_out_kernel": 4,
    "self_out_kernel": 5,
    "ffn_out_kernel": 6,
    "small_kernel": 1,
}


def run(kernel, args, outs, scratch=(), aliases=None, any_args=(), any_outs=()):
    single = not isinstance(outs, (list, tuple))
    out_list = [outs] if single else list(outs)
    vmem = pl.BlockSpec(memory_space=pltpu.VMEM)
    anywhere = pl.BlockSpec(memory_space=pl.ANY)
    base = getattr(kernel, "func", kernel)
    result = pl.pallas_call(
        kernel,
        name=base.__name__,
        in_specs=[anywhere if i in any_args else vmem for i in range(len(args))],
        out_specs=[anywhere if i in any_outs else vmem for i in range(len(out_list))],
        out_shape=out_list,
        scratch_shapes=list(scratch),
        input_output_aliases=aliases or {},
        cost_estimate=pl.CostEstimate(
            flops=KERNEL_US[base.__name__] * 1_100_000_000, bytes_accessed=0, transcendentals=0
        ),
        compiler_params=pltpu.CompilerParams(vmem_limit_bytes=VMEM_LIMIT),
    )(*args)
    return result[0] if single else result


def shaped(shape, dtype):
    return jax.ShapeDtypeStruct(shape, dtype)


def group_place():
    return lax.axis_index("x") * 2 + lax.axis_index("core")


def lanes(start, size):
    return pl.ds(pl.multiple_of(start, 128), size)


def local_bias(ref, row, j):
    n = ref.shape[1]
    return jnp.concatenate(
        [ref[pl.ds(row, 1), lanes(h * (n // 2) + j * (n // 8), n // 8)] for h in range(2)], 1
    )


def whole(refs):
    return jnp.concatenate([r[...] for r in refs], 0)


def halves(product, act, sent_ref, kept_ref):
    half = act.shape[0] // 2
    sent_ref[...] = product(act[half:]).astype(BF16)
    kept_ref[...] = product(act[:half])


def flat_row(ref, r):
    block = ref[:, r]
    return block.reshape(block.shape[0] * block.shape[1], block.shape[2])


def self_fwd_kernel(x0, x1, x2, x3, w, wo, biases, mask, qkv_out, o_out, sent, kept):
    j = group_place()
    tokens = whole([x0, x1, x2, x3])
    width = wo.shape[0]
    bq = local_bias(biases, 0, j)
    bias = jnp.concatenate([bq, jnp.zeros_like(bq), local_bias(biases, 1, j)], 1)
    qkv = (mm(tokens, w[...]) + bias).astype(BF16)
    qkv_out[...] = qkv.reshape(qkv_out.shape)
    for r in range(qkv_out.shape[1]):
        row = flat_row(qkv_out, r)
        out = attend_core(
            row[:, :width], row[:, width : 2 * width], row[:, 2 * width :], mask[r] > 0.5
        )
        o_out[:, r] = out.reshape(o_out.shape[0], o_out.shape[2], width)
    mixed = o_out[...].reshape(tokens.shape[0], width)
    halves(lambda a: mm(a, wo[...]), mixed, sent, kept)


def cross_allowed(qc, kc):
    return (kc >= 0.0) & ((kc == qc) | (qc < -1.5))


def memory_kv_kernel(m0, m1, m2, m3, w, biases, *outs):
    j = group_place()
    width = w.shape[1] // 3
    bv = local_bias(biases, 3, j)
    bias = jnp.concatenate([jnp.zeros_like(bv), bv], 1)
    for r, out in enumerate(outs):
        mem = jnp.concatenate([m[r] for m in (m0, m1, m2, m3)], 0)
        out[...] = (mm(mem, w[:, width:]) + bias).astype(BF16)


def memory_back_kernel(*refs):
    dkvs, (w, sent, kept) = refs[:-3], refs[-3:]
    width = w.shape[1] // 3
    for r, dkv in enumerate(dkvs):
        slots = dkv.shape[0] // 4
        far = mm_t(dkv[2 * slots :], w[:, width:]).astype(BF16)
        near = mm_t(dkv[: 2 * slots], w[:, width:])
        for d in range(2):
            sent[d, r] = far[d * slots : (d + 1) * slots]
            kept[d, r] = near[d * slots : (d + 1) * slots]


def cross_fwd_kernel(rows, *refs):
    h, (w, wo, biases), kvs = refs[:4], refs[4:7], refs[7 : 7 + rows]
    q_code, k_code, q_out, o_out, sent, kept = refs[7 + rows :]
    tokens = whole(h)
    width = wo.shape[0]
    query = (mm(tokens, w[:, :width]) + local_bias(biases, 2, group_place())).astype(BF16)
    q_out[...] = query.reshape(q_out.shape)
    for r, kv in enumerate(kvs):
        allowed = cross_allowed(q_code[r], k_code[r])
        out = attend_core(flat_row(q_out, r), kv[:, :width], kv[:, width:], allowed)
        o_out[:, r] = out.reshape(o_out.shape[0], o_out.shape[2], width)
    mixed = o_out[...].reshape(tokens.shape[0], width)
    halves(lambda a: mm(a, wo[...]), mixed, sent, kept)


def ffn_fwd_kernel(h0, h1, h2, h3, w1, w2, bias, g_out, slope_out, sent, kept):
    j = group_place()
    tokens = whole([h0, h1, h2, h3])
    u = mm(tokens, w1[...]) + local_bias(bias, 0, j)
    normal = 0.5 * (1.0 + lax.erf(u * 0.7071067811865476))
    slope_out[...] = normal + u * (0.3989422804014327 * jnp.exp(-0.5 * u * u))
    g_out[...] = (u * normal).astype(BF16)
    halves(lambda a: mm(a, w2[...]), g_out[...], sent, kept)


def ffn_bwd_kernel(f0, f1, f2, f3, w1, w2, slope, du_out, bias_out, sent, kept):
    grads = whole([f0, f1, f2, f3])
    du = (mm_t(grads, w2[...]) * slope[...]).astype(BF16)
    du_out[...] = du
    bias_out[...] = jnp.sum(du.astype(F32), 0, keepdims=True)
    halves(lambda a: mm_t(a, w1[...]), du, sent, kept)


def cross_bwd_kernel(rows, *refs):
    f, (w, wo, q), kvs = refs[:4], refs[4:7], refs[7 : 7 + rows]
    q_code, k_code, dq_out = refs[7 + rows : 10 + rows]
    dkvs = refs[10 + rows : 10 + 2 * rows]
    sums, sent, kept, do_ref = refs[10 + 2 * rows :]
    grads = whole(f)
    width = wo.shape[0]
    do_ref[...] = mm_t(grads, wo[...]).astype(BF16).reshape(do_ref.shape)
    total_v = jnp.zeros((1, width), F32)
    for r, (kv, dkv) in enumerate(zip(kvs, dkvs)):
        allowed = cross_allowed(q_code[r], k_code[r])
        dq, dk, dv = attend_back_core(
            flat_row(q, r), kv[:, :width], kv[:, width:], allowed, flat_row(do_ref, r)
        )
        dq_out[:, r] = dq.reshape(dq_out.shape[0], dq_out.shape[2], width)
        dkv[:, :width] = dk
        dkv[:, width:] = dv
        total_v = total_v + jnp.sum(dv.astype(F32), 0, keepdims=True)
    dq = dq_out[...].reshape(grads.shape[0], width)
    total_q = jnp.sum(dq.astype(F32), 0, keepdims=True)
    sums[...] = jnp.concatenate([total_q, total_v, jnp.zeros((6, width), F32)], 0)
    halves(lambda a: mm_t(a, w[:, :width]), dq, sent, kept)


def self_bwd_kernel(f0, f1, f2, f3, w, wo, qkv, mask, dqkv_out, sums, sent, kept):
    grads = whole([f0, f1, f2, f3])
    width = wo.shape[0]
    shape = (qkv.shape[0], qkv.shape[1], qkv.shape[2], width)
    do = mm_t(grads, wo[...]).astype(BF16).reshape(shape)
    for r in range(shape[1]):
        row = flat_row(qkv, r)
        grad = do[:, r].reshape(row.shape[0], width)
        parts = attend_back_core(
            row[:, :width], row[:, width : 2 * width], row[:, 2 * width :], mask[r] > 0.5, grad
        )
        dqkv_out[:, r] = jnp.concatenate(parts, 1).reshape(shape[0], shape[2], 3 * width)
    dqkv = dqkv_out[...].reshape(grads.shape[0], 3 * width)
    sums[...] = jnp.sum(dqkv.astype(F32), 0, keepdims=True)
    halves(lambda a: mm_t(a, w[...]), dqkv, sent, kept)


def branch_sum(kept, arrived, crossed):
    n = crossed.shape[0]
    return kept[:n] + arrived[:n].astype(F32) + crossed[...].astype(F32)


def normalise(v):
    centre = v - jnp.mean(v, -1, keepdims=True)
    rstd = lax.rsqrt(jnp.mean(centre * centre, -1, keepdims=True) + EPS)
    return centre * rstd, rstd


def denormalise(e, gain, n, rstd):
    a = e * gain
    return rstd * (a - jnp.mean(a, -1, keepdims=True) - n * jnp.mean(a * n, -1, keepdims=True))


def norm_one_kernel(kept, arrived, crossed, own, bias, gains, shifts, n_out, rstd_out, low_out):
    v = branch_sum(kept, arrived, crossed) + bias[...] + own[...].astype(F32)
    n, rstd = normalise(v)
    n_out[...] = n
    rstd_out[...] = jnp.broadcast_to(rstd, rstd_out.shape)
    low_out[...] = (n * gains[0:1] + shifts[0:1]).astype(BF16)


def norm_two_kernel(kept, arrived, crossed, n_one, biases, gains, shifts, n_out, rstd_out, low_out):
    resid = n_one[...] * gains[0:1] + shifts[0:1]
    n, rstd = normalise(branch_sum(kept, arrived, crossed) + biases[4:5] + resid)
    n_out[...] = n
    rstd_out[...] = jnp.broadcast_to(rstd, rstd_out.shape)
    low_out[...] = (n * gains[1:2] + shifts[1:2]).astype(BF16)


def sums_of(e, n, low):
    return jnp.concatenate(
        [
            jnp.sum(e * n, 0, keepdims=True),
            jnp.sum(e, 0, keepdims=True),
            jnp.sum(low.astype(F32), 0, keepdims=True),
            jnp.zeros((5, e.shape[1]), F32),
        ],
        0,
    )


def norm_three_kernel(
    kept, arrived, crossed, n_two, biases, gains, shifts, cot, live, mixed_out, d_out, low_out, sums
):
    resid = n_two[...] * gains[1:2] + shifts[1:2]
    n, rstd = normalise(branch_sum(kept, arrived, crossed) + biases[5:6] + resid)
    mixed_out[...] = ((n * gains[2:3] + shifts[2:3]) * live[...]).astype(BF16)
    e = cot[...].astype(F32) * live[...]
    d = denormalise(e, gains[2:3], n, rstd)
    low = d.astype(BF16)
    d_out[...] = d
    low_out[...] = low
    sums[...] = sums_of(e, n, low)


def norm_back_kernel(which, kept, arrived, crossed, d_in, n, rstd, gains, d_out, low_out, sums):
    e = branch_sum(kept, arrived, crossed) + d_in[...]
    d = denormalise(e, gains[which : which + 1], n[...], rstd[:, 0:1])
    low = d.astype(BF16)
    d_out[...] = d
    low_out[...] = low
    sums[...] = sums_of(e, n[...], low)


def cut_cols_kernel(proj, first, *outs):
    j = group_place()
    n, _, width = proj.shape
    ff = first.shape[1]
    for d, out in enumerate(outs):
        target = jnp.bitwise_xor(j, d)
        at = 0
        for m in range(n):
            for h in range(2):
                out[:, at : at + width // 8] = proj[
                    m, :, lanes(h * (width // 2) + target * (width // 8), width // 8)
                ]
                at += width // 8
        for h in range(2):
            out[:, at : at + ff // 8] = first[:, lanes(h * (ff // 2) + target * (ff // 8), ff // 8)]
            at += ff // 8


def pack_kernel(e0, e1, e2, e3, out_w, second, buf_ab, buf_c):
    j = group_place()
    quarter = out_w.shape[2] // 4
    three = 3 * quarter
    rows = e0.shape[0]
    for d, e in enumerate([e0, e1, e2, e3]):
        at = jnp.bitwise_xor(j, d)
        buf_ab[at, :, :three] = e[:, :three]
        buf_ab[at, :, three : 2 * three] = e[:, three : 2 * three]
        buf_c[at] = e[:, 2 * three :]
    for i in range(4):
        for m in range(2):
            at = 2 * three + m * quarter
            buf_ab[i, :, at : at + quarter] = out_w[m, :, i * quarter : (i + 1) * quarter]
        buf_c[4 + i] = second[i * rows : (i + 1) * rows]


def place_kernel(blocks, w_qkv, w_two, w_out, w_out2):
    cols = w_qkv.shape[-1]
    quarter = cols // 3
    for h in range(blocks.shape[0]):
        for z in range(blocks.shape[1]):
            for i in range(4):
                w_qkv[h, i, z] = blocks[h, z, i, :, :cols]
                w_two[h, i, z] = blocks[h, z, i, :, cols : 2 * cols]
                for m, out in enumerate([w_out, w_out2]):
                    at = 2 * cols + m * quarter
                    out[h, z, :, i * quarter : (i + 1) * quarter] = blocks[
                        h, z, i, :, at : at + quarter
                    ]


def place_ffn_kernel(blocks, wcol, wrow):
    rows = wcol.shape[-2]
    for h in range(blocks.shape[0]):
        for z in range(blocks.shape[1]):
            for i in range(4):
                wcol[h, i, z] = blocks[h, z, i]
                wrow[h, z, i * rows : (i + 1) * rows] = blocks[h, z, 4 + i]


def select_rows(dst, pieces, n_z, half_index):
    z = lax.axis_index("z")
    at = 0
    for piece in pieces:
        count, width = piece.shape
        for k in range(n_z):
            start = lax.rem(z + k, n_z) * (width // n_z) + half_index * (width // n_z // 2)
            dst[at : at + count, k * 128 : (k + 1) * 128] = piece[:, lanes(start, 128)]
        at += count


def select_cols(dst, pieces, n_z):
    z = lax.axis_index("z")
    at = 0
    for piece in pieces:
        count, width = piece.shape
        size = width // n_z
        for k in range(n_z):
            start = lax.rem(z + k, n_z) * size
            dst[at : at + count, k * size : (k + 1) * size] = piece[:, lanes(start, size)]
        at += count


def put_cols(out, at, block):
    n_z, rows = out.shape[0], out.shape[1]
    cols = block.shape[1]
    out[:, :, at : at + cols] = block.astype(BF16).reshape(n_z, rows, cols)


def put_rows(out, at, block):
    n_z, rows = out.shape[0], out.shape[1]
    size = block.shape[1] // n_z
    for k in range(n_z):
        for i in range(block.shape[0] // rows):
            out[k, :, at + i * size : at + (i + 1) * size] = block[
                i * rows : (i + 1) * rows, k * size : (k + 1) * size
            ].astype(BF16)


def half_of(ref, h):
    size = ref.shape[1] // 2
    return ref[:, lanes(h * size, size)]


def ffn_grad_kernel(a0, a1, a2, a3, du, g, f0, f1, f2, f3, out):
    n_hi, n_z, rows = out.shape[0], out.shape[1], out.shape[2]
    cols = du.shape[1]
    block = t_mm(whole([a0, a1, a2, a3]), du[...]).astype(BF16)
    for z in range(n_z):
        for h in range(n_hi):
            at = (z * n_hi + h) * rows
            out[h, z, :, :cols] = block[at : at + rows]
    block = t_mm(g[...], whole([f0, f1, f2, f3])).astype(BF16)
    size = block.shape[1] // n_z
    per = block.shape[0] // n_hi
    for h in range(n_hi):
        for z in range(n_z):
            for i in range(per // rows):
                at = h * per + i * rows
                out[h, z, :, cols + i * size : cols + (i + 1) * size] = block[
                    at : at + rows, z * size : (z + 1) * size
                ]


def memory_grad_kernel(n_z, rows, *refs):
    mems, dkvs, (kept, sent, left) = refs[:4], refs[4 : 4 + rows], refs[4 + rows :]
    hi = lax.axis_index("hi")
    for out, h in ((sent, 1 - hi), (kept, hi)):
        total = 0.0
        for r in range(rows):
            select_rows(left, [m.at[r] for m in mems], n_z, h)
            total = total + t_mm(left[...], dkvs[r][...])
        put_cols(out, 0, total)


def cross_grad_kernel(
    n_z, h0, h1, h2, h3, dq, kv_kept, kv_sent, o2, f0, f1, f2, f3, kept, sent, left, right
):
    hi = lax.axis_index("hi")
    c_q, c_kv = dq.shape[1], kv_kept.shape[2]
    select_cols(right, [f0, f1, f2, f3], n_z)
    for out, h, kv in ((sent, 1 - hi, kv_sent), (kept, hi, kv_kept)):
        select_rows(left, [h0, h1, h2, h3], n_z, h)
        put_cols(out, 0, t_mm(left[...], dq[...]))
        out[:, :, c_q : c_q + c_kv] = kv[...]
        put_rows(out, c_q + c_kv, t_mm(half_of(o2, h), right[...]))


def self_grad_kernel(
    n_z, x0, x1, x2, x3, dqkv, sums, small, o1, f0, f1, f2, f3, kept, sent, left, right
):
    hi = lax.axis_index("hi")
    rows = kept.shape[1] - 16
    cols = dqkv.shape[1]
    last = jnp.concatenate([sums[...], jnp.zeros((1, right.shape[1] - cols), F32)], 1)
    at_last = lax.broadcasted_iota(jnp.int32, small.shape, 0) == small.shape[0] - 1
    lower = jnp.where(at_last, last, small[...]).astype(BF16)
    select_cols(right, [f0, f1, f2, f3], n_z)
    size = right.shape[1] // n_z
    for out, h in ((sent, 1 - hi), (kept, hi)):
        select_rows(left, [x0, x1, x2, x3], n_z, h)
        block = t_mm(left[...], dqkv[...]).astype(BF16)
        other = t_mm(half_of(o1, h), right[...]).astype(BF16)
        for k in range(n_z):
            out[k, :rows, :cols] = block[k * rows : (k + 1) * rows]
            out[k, rows:] = lower
            out[k, :rows, cols:] = other[:, k * size : (k + 1) * size]


def pair_sum_kernel(kept, arrived, own, *sent):
    own[...] = kept[0].astype(F32) + arrived[0].astype(F32)
    for k, out in enumerate(sent):
        out[...] = (kept[k + 1].astype(F32) + arrived[k + 1].astype(F32)).astype(BF16)


def final_sum_kernel(cols, own, *refs):
    total = own[...]
    arrived, outs = refs[: -len(cols)], refs[-len(cols) :]
    for a in arrived:
        total = total + a[...].astype(F32)
    at = 0
    for out, size in zip(outs, cols):
        out[...] = total[:, at : at + size].astype(BF16)
        at += size


def places(index):
    h = jnp.bitwise_xor(lax.axis_index("hi"), (index >> 2) & 1)
    return h, jnp.bitwise_xor(group_place(), index & 3)


def ffn_out_kernel(pieces, first, second):
    rows = pieces.shape[1]
    ff = first.shape[1]
    width = second.shape[1]
    size = width // 4
    for index in range(8):
        h, j = index // 4, index % 4
        for half in range(2):
            at = half * (ff // 2) + j * (ff // 8)
            first[h * rows : (h + 1) * rows, at : at + ff // 8] = pieces[
                index, :, half * (ff // 8) : (half + 1) * (ff // 8)
            ].astype(F32)
        for i in range(4):
            at = ff // 4 + i * size
            row = h * 4 * rows + i * rows
            second[row : row + rows, j * size : (j + 1) * size] = pieces[
                index, :, at : at + size
            ].astype(F32)


def place_cols(out, m, rows, piece, at):
    width = out.shape[2]
    for index, p in enumerate(piece):
        h, j = places(index)
        for half in range(2):
            lo = at + half * (width // 8)
            out[
                m,
                pl.ds(pl.multiple_of(h * rows, 8), rows),
                lanes(half * (width // 2) + j * (width // 8), width // 8),
            ] = p[:rows, lo : lo + width // 8].astype(F32)


def place_rows(out, m, rows, pieces, at):
    size = out.shape[2] // 4
    for index, piece in enumerate(pieces):
        h, j = places(index)
        out[m, pl.ds(pl.multiple_of(h * rows, 8), rows), lanes(j * size, size)] = piece[
            :rows, at : at + size
        ].astype(F32)


def cross_out_kernel(*refs):
    pieces, g_proj, g_out, work, work_out, sems = refs[:8], *refs[8:]
    rows = pieces[0].shape[0]
    width = work.shape[2]
    for m in range(3):
        place_cols(work, m, rows, pieces, m * (width // 4))
    copy = pltpu.make_async_copy(work, g_proj.at[pl.ds(3, 3)], sems.at[0])
    copy.start()
    place_rows(work_out, 0, rows, pieces, 3 * (width // 4))
    second = pltpu.make_async_copy(work_out, g_out.at[pl.ds(1, 1)], sems.at[1])
    second.start()
    copy.wait()
    second.wait()


def self_out_kernel(*refs):
    pieces, _, _, g_proj, g_out, sums, small, work, work_out, sems = refs[:8], *refs[8:]
    rows = pieces[0].shape[0] - 16
    width = work.shape[2]
    for m in range(3):
        place_cols(work, m, rows, pieces, m * (width // 4))
    copy = pltpu.make_async_copy(work, g_proj.at[pl.ds(0, 3)], sems.at[0])
    copy.start()
    place_rows(work_out, 0, rows, pieces, 3 * (width // 4))
    second = pltpu.make_async_copy(work_out, g_out.at[pl.ds(0, 1)], sems.at[1])
    second.start()
    sums[...] = jnp.zeros_like(sums)
    lowers = [pieces[index][rows : rows + 16].astype(F32) for index in range(4)]
    small[...] = (lowers[0] + lowers[1]) + (lowers[2] + lowers[3])
    for index, lower in enumerate(lowers):
        _, j = places(index)
        for m in range(3):
            for half in range(2):
                lo = m * (width // 4) + half * (width // 8)
                sums[m : m + 1, lanes(half * (width // 2) + j * (width // 8), width // 8)] = lower[
                    15:16, lo : lo + width // 8
                ]
    copy.wait()
    second.wait()


def small_kernel(s3, s2, s1, cross_sums, ff_sum, out):
    j = group_place()
    width = out.shape[1]
    ff = ff_sum.shape[1] * 4
    out[...] = jnp.zeros_like(out)
    for half in range(2):
        at = lanes(half * (width // 2) + j * (width // 8), width // 8)
        part = slice(half * (width // 8), (half + 1) * (width // 8))
        out[0:1, at] = cross_sums[0:1, part]
        out[1:2, at] = cross_sums[1:2, part]
    out[2:3] = s2[2:3]
    out[3:4] = s3[2:3]
    out[4:5] = s1[2:3]
    ff_rows = ff // width
    per = ff // 8
    for half in range(2):
        flat_at = half * (ff // 2) + j * per
        row = 5 + flat_at // width
        out[pl.ds(row, 1), lanes(lax.rem(flat_at, width), per)] = ff_sum[
            0:1, half * per : (half + 1) * per
        ]
    at = 5 + ff_rows
    for i, s in enumerate([s1, s2, s3]):
        out[at + i : at + i + 1] = s[0:1]
        out[at + 3 + i : at + 4 + i] = s[1:2]


def per_device(
    dec_in,
    memory,
    proj_w,
    out_w,
    ffn_in,
    ffn_out,
    biases,
    out_bias,
    ffn_bias,
    norm_gain,
    norm_bias,
    mem_len,
    dec_len,
    mem_seg,
    dec_seg,
    cotangent,
):
    n_hi = lax.axis_size("hi")
    n_z = lax.axis_size("z")
    hi = lax.axis_index("hi")
    zi = lax.axis_index("z")
    j = group_place()
    fast = n_hi == 2 and n_z == 4
    row_count, query_count, width = dec_in.shape
    tile_count, tile_part = memory.shape[1], memory.shape[2]
    own_tokens = row_count * query_count
    all_tokens = 4 * own_tokens
    slots = tile_count * tile_part
    ff_width = ffn_in.shape[1]
    local = width // 4
    ff_local = ff_width // 4

    def turned(index):
        return (index & 1) * 2 + (index >> 1)

    to_rows = [
        ((h * 4 + a) * 4 + b, (h * 4 + turned(b)) * 4 + turned(a))
        for h in range(n_hi)
        for a in range(4)
        for b in range(4)
    ]

    def transpose(values):
        return lax.ppermute(values, AXES, to_rows)

    def shift_z(values, k):
        return lax.ppermute(values, "z", [(i, (i + k) % n_z) for i in range(n_z)])

    def gather_j(values):
        across = swap(values, "x")
        return [values, across, swap(values, "core"), swap(across, "core")]

    def cross_links(sent, kept):
        arrived = swap(sent, "core")
        half = kept.shape[0] // 2
        middle = (kept[half:] + arrived[half:].astype(F32)).astype(BF16)
        return kept, arrived, swap(middle, "x")

    def add_crossed(kept, arrived, crossed, other=0.0):
        n = crossed.shape[0]
        total = kept[:n] + arrived[:n].astype(F32) + crossed.astype(F32) + other
        return total.astype(BF16)

    def split_cols(full):
        n, total, cols = full.shape
        split = pick(full.reshape(n, total, 2, 4, cols // 8), j, 3)
        return split.transpose(1, 0, 2, 3).reshape(total, n * cols // 4)

    def split_rows(full):
        total, cols = full.shape
        return pick(full.reshape(2, 4, total // 8, cols), j, 1).reshape(total // 4, cols)

    def near_blocks(block):
        return [block] + [shift_z(block, -k) for k in range(1, n_z)]

    def after(values, *others):
        return lax.optimization_barrier((values, *others))[0]

    segs = transpose(jnp.concatenate([mem_seg.reshape(row_count, -1), dec_seg], 1))
    own_in = transpose(dec_in).reshape(own_tokens, width)
    tokens = gather_j(own_in)
    own_memory = transpose(after(memory, own_in, segs)).reshape(row_count, slots, width)
    mems = gather_j(own_memory)
    if fast:
        rows = proj_w.shape[1]
        cut = shaped((rows, 6 * local + ff_local), BF16)
        e = run(cut_cols_kernel, [proj_w, ffn_in], [cut] * 4)
        diag = [(0, 3), (1, 2), (2, 1), (3, 0)]
        e = [e[0], swap(e[1], "core"), swap(e[2], "x"), lax.ppermute(e[3], ("x", "core"), diag)]
        buf_ab, buf_c = run(
            pack_kernel,
            e + [out_w, ffn_out],
            [shaped((4, rows, 2 * width), BF16), shaped((8, rows, ff_local), BF16)],
        )
        all_ab = lax.all_gather(after(buf_ab, own_memory), ("hi", "z"), axis=0)
        col_shape = shaped((2, 4, n_z, rows, 3 * local), BF16)
        row_shape = shaped((2, n_z, rows, width), BF16)
        placed = run(
            place_kernel,
            [all_ab.reshape((2, n_z) + buf_ab.shape)],
            [col_shape, col_shape, row_shape, row_shape],
        )
        w_qkv, w_two = (w.reshape(-1, 3 * local) for w in placed[:2])
        w_out, w_out2 = (w.reshape(-1, width) for w in placed[2:])
        all_c = lax.all_gather(after(buf_c, all_ab), ("hi", "z"), axis=0)
        w_first, w_second = run(
            place_ffn_kernel,
            [all_c.reshape((2, n_z) + buf_c.shape)],
            [
                shaped((2, 4, n_z, rows, ff_local), BF16),
                shaped((2, n_z, ffn_out.shape[0], width), BF16),
            ],
        )
        w_first = w_first.reshape(-1, ff_local)
        w_second = w_second.reshape(-1, width)
    else:
        proj_full = lax.all_gather(proj_w, AXES, axis=1, tiled=True)
        out_full = lax.all_gather(out_w, AXES, axis=1, tiled=True)
        w_qkv, w_two = split_cols(proj_full[:3]), split_cols(proj_full[3:])
        w_out, w_out2 = split_rows(out_full[0]), split_rows(out_full[1])
        w_first = split_cols(lax.all_gather(ffn_in, AXES, axis=0, tiled=True)[None])
        w_second = split_rows(lax.all_gather(ffn_out, AXES, axis=0, tiled=True))

    own_cot = transpose(after(cotangent, mems[3])).reshape(own_tokens, width)
    mem_full = mem_seg.shape[1] * mem_seg.shape[2]
    group = hi * 4 + turned(zi)
    own_dlen = lax.dynamic_slice_in_dim(dec_len, group * row_count, row_count)
    own_mlen = lax.dynamic_slice_in_dim(mem_len, group * row_count, row_count)
    parts = [turned(j ^ d) for d in ORDER]
    mem_parts = segs[:, :mem_full].reshape(row_count, tile_count, 4, tile_part)
    dec_parts = segs[:, mem_full:].reshape(row_count, 4, query_count)
    dseg = jnp.concatenate([pick(dec_parts, p, 1) for p in parts], 1)
    mseg = jnp.concatenate([pick(mem_parts, p, 2).reshape(row_count, slots) for p in parts], 1)
    dpos = jnp.concatenate([p * query_count + jnp.arange(query_count) for p in parts])
    in_tile = jnp.arange(tile_count)[:, None] * (4 * tile_part) + jnp.arange(tile_part)[None, :]
    mpos = jnp.concatenate([(in_tile + p * tile_part).reshape(-1) for p in parts])
    dlive = dpos[None, :] < own_dlen[:, None]
    mlive = mpos[None, :] < own_mlen[:, None]
    self_mask = (
        (dseg[:, :, None] == dseg[:, None, :])
        & (dpos[None, None, :] <= dpos[None, :, None])
        & dlive[:, None, :]
    ) | (dpos[None, None, :] == dpos[None, :, None])
    self_mask = self_mask.astype(F32)
    q_code = jnp.where(dlive, dseg.astype(F32), -2.0)[:, :, None]
    k_code = jnp.where(mlive, mseg.astype(F32), -1.0)[:, None, :]
    own_pos = parts[0] * query_count + jnp.arange(query_count)
    own_live = (own_pos[None, :] < own_dlen[:, None]).astype(F32).reshape(own_tokens, 1)
    part = width // n_z // 2

    def pair_sums(kept, arrived):
        shape = kept.shape[1:]
        return run(
            pair_sum_kernel,
            [kept, arrived],
            [shaped(shape, F32)] + [shaped(shape, BF16)] * (n_z - 1),
        )

    def sum_z(own, out, cols):
        arrived = [shift_z(block, i + 1) for i, block in enumerate(out)]
        return run(
            functools.partial(final_sum_kernel, cols),
            [own, *arrived],
            [shaped((own.shape[0], c), BF16) for c in cols],
        )

    to_plane = [
        ((h * 4 + 2 * a + b) * 4 + z, (b * 4 + z) * 4 + 2 * h + a)
        for h in range(2)
        for a in range(2)
        for b in range(2)
        for z in range(4)
    ]

    def gather_dp(block):
        pieces = [block, swap(block, "x")]
        pieces = pieces + [swap(p, "hi") for p in pieces]
        return [q for p in pieces for q in (p, swap(p, "core"))]

    def to_planes(rows):
        return lax.ppermute(rows, AXES, to_plane)

    def beside(cols, rows):
        return jnp.concatenate([cols, rows], 1)

    def both(cols, rows=part):
        return [shaped((n_z, rows, cols), BF16)] * 2

    def tokens_scratch(cols):
        return pltpu.VMEM((all_tokens, cols), BF16)


    heads = shaped((4, row_count, query_count, local), BF16)
    sent = shaped((all_tokens // 2, width), BF16)
    kept = shaped((all_tokens // 2, width), F32)
    own_f32 = shaped((own_tokens, width), F32)
    own_low = shaped((own_tokens, width), BF16)
    rstd_shape = shaped((own_tokens, 128), F32)
    sums_shape = shaped((8, width), F32)
    qkv, mixed_self, s, k = run(
        self_fwd_kernel,
        [*[after(t, mems[3]) for t in tokens], w_qkv, w_out, biases, self_mask],
        [shaped((4, row_count, query_count, 3 * local), BF16), heads, sent, kept],
    )
    n_one, rstd_one, one_low = run(
        norm_one_kernel,
        [*cross_links(s, k), own_in, out_bias[None], norm_gain, norm_bias],
        [own_f32, rstd_shape, own_low],
    )
    ones = gather_j(one_low)
    kv_shape = shaped((4 * slots, 2 * local), BF16)
    kv2 = run(memory_kv_kernel, [*mems, w_two, biases], [kv_shape] * row_count)
    query_two, mixed_cross, s, k = run(
        functools.partial(cross_fwd_kernel, row_count),
        [*ones, w_two, w_out2, biases, *kv2, q_code, k_code],
        [heads, heads, sent, kept],
    )
    n_two, rstd_two, two_low = run(
        norm_two_kernel,
        [*cross_links(s, k), n_one, biases, norm_gain, norm_bias],
        [own_f32, rstd_shape, own_low],
    )
    twos = gather_j(two_low)
    active, slope, s, k = run(
        ffn_fwd_kernel,
        [*twos, w_first, w_second, ffn_bias[None]],
        [shaped((all_tokens, ff_local), BF16), shaped((all_tokens, ff_local), F32), sent, kept],
    )
    mixed_out, d_three, own_f3, sums_three = run(
        norm_three_kernel,
        [*cross_links(s, k), n_two, biases, norm_gain, norm_bias, own_cot, own_live],
        [own_low, own_f32, own_low, sums_shape],
    )
    own_out = mixed_out.reshape(dec_in.shape)

    f3 = gather_j(own_f3)
    du, ff_sum, s, k = run(
        ffn_bwd_kernel,
        [*f3, w_first, w_second, slope],
        [shaped((all_tokens, ff_local), BF16), shaped((1, ff_local), F32), sent, kept],
    )
    k, arrived, crossed = cross_links(s, k)
    mixed_out = transpose(after(own_out, crossed))
    if fast:
        g_ffn = run(
            ffn_grad_kernel,
            [*twos, du, active, *f3],
            shaped((2, n_z, part, ff_local + width), BF16),
        )
        crossed = after(crossed, g_ffn)
        g_ffn = lax.psum_scatter(
            g_ffn.reshape(2 * n_z * part, -1), ("hi", "z"), scatter_dimension=0, tiled=True
        )
    d_two, own_f2, sums_two = run(
        functools.partial(norm_back_kernel, 1),
        [k, arrived, crossed, d_three, n_two, rstd_two, norm_gain],
        [own_f32, own_low, sums_shape],
    )
    f2 = gather_j(own_f2)
    dq2, *dkv2, cross_sums, s, k = run(
        functools.partial(cross_bwd_kernel, row_count),
        [*f2, w_two, w_out2, query_two, *kv2, q_code, k_code],
        [heads] + [kv_shape] * row_count + [shaped((8, local), F32), sent, kept],
        scratch=[pltpu.VMEM(heads.shape, BF16)],
    )
    d_one, own_f1, sums_one = run(
        functools.partial(norm_back_kernel, 0),
        [*cross_links(s, k), d_two, n_one, rstd_one, norm_gain],
        [own_f32, own_low, sums_shape],
    )
    f1 = gather_j(own_f1)
    dq2 = dq2.reshape(all_tokens, local)
    o2 = mixed_cross.reshape(all_tokens, local)
    if fast:
        kept_m, sent_m = run(
            functools.partial(memory_grad_kernel, n_z, row_count),
            mems + dkv2,
            both(2 * local),
            scratch=[pltpu.VMEM((4 * slots, width // 2), BF16)],
        )
        kept_b, sent_b = run(
            functools.partial(cross_grad_kernel, n_z),
            [*ones, dq2, kept_m, sent_m, o2, *f2],
            both(4 * local),
            scratch=[tokens_scratch(width // 2), tokens_scratch(width)],
        )
        f1 = [after(f, sent_b) for f in f1]
    dqkv, sum_qkv, s, k = run(
        self_bwd_kernel,
        [*f1, w_qkv, w_out, qkv, self_mask],
        [
            shaped((4, row_count, query_count, 3 * local), BF16),
            shaped((1, 3 * local), F32),
            sent,
            kept,
        ],
    )
    own_d = add_crossed(*cross_links(s, k), d_one)

    ff_rows = ff_width // width
    n_small = 16
    small = run(
        small_kernel,
        [sums_three, sums_two, sums_one, cross_sums, ff_sum],
        shaped((n_small, width), F32),
    )
    dqkv = dqkv.reshape(all_tokens, -1)
    o1 = mixed_self.reshape(all_tokens, local)
    half_slots = (2, row_count, slots, width)
    memory_outs = [shaped(half_slots, BF16), shaped(half_slots, F32)]
    if fast:
        g_shapes = [shaped((6, width // n_z, width), F32), shaped((2, width // n_z, width), F32)]
        work = [
            pltpu.VMEM((3, width // n_z, width), F32),
            pltpu.VMEM((1, width // n_z, width), F32),
            pltpu.SemaphoreType.DMA((2,)),
        ]
        arrived_b = swap(sent_b, "hi")
        kept_a, sent_a = run(
            functools.partial(self_grad_kernel, n_z),
            [*tokens, dqkv, sum_qkv, small, o1, *f1],
            both(4 * local, part + 16),
            scratch=[tokens_scratch(width // 2), tokens_scratch(width)],
        )
        s_m, k_m = run(
            memory_back_kernel, [after(dkv, sent_a) for dkv in dkv2] + [w_two], memory_outs
        )
        links_m = cross_links(s_m, k_m)
        sums_c = after(g_ffn, s_m)
        rows_c = to_planes(sums_c[:, ff_local:])
        arrived_a = swap(after(sent_a, rows_c, links_m[1]), "hi")
        own_b, *out_b = pair_sums(kept_b, after(arrived_b, rows_c))
        cols_b, rows_b = sum_z(own_b, out_b, (3 * local, local))
        rows_b = to_planes(rows_b)
        own_a, *out_a = pair_sums(kept_a, after(arrived_a, rows_b))
        g_ffn = lax.all_gather(
            beside(sums_c[:, :ff_local], after(rows_c, own_a)), ("hi", "x", "core"), axis=0
        )
        cols_a, rows_a = sum_z(own_a, out_a, (3 * local, local))
        pieces_b = gather_dp(beside(cols_b, rows_b))
        rows_a = jnp.concatenate([to_planes(rows_a[:part]), rows_a[part:]], 0)
        g_proj, g_out = run(cross_out_kernel, pieces_b, g_shapes, scratch=work, any_outs=(0, 1))
        g_proj, g_out, sums_qkv, small = run(
            self_out_kernel,
            gather_dp(beside(cols_a, rows_a)) + [g_proj, g_out],
            g_shapes + [shaped((8, width), F32), shaped(small.shape, F32)],
            scratch=work,
            aliases={8: 0, 9: 1},
            any_args=(8, 9),
            any_outs=(0, 1),
        )
        g_first, g_second = run(
            ffn_out_kernel,
            [g_ffn],
            [shaped((width // n_z, ff_width), F32), shaped((ff_width // n_z, width), F32)],
        )
        d_memory = add_crossed(*(t.reshape((-1, width)) for t in links_m))
        d_memory = after(d_memory, rows_a)
        own_d = after(own_d, rows_a)
    else:
        mine = (jnp.arange(4) == j).astype(F32)[:, None]

        small = lax.psum(small, AXES)
        d_memory = add_crossed(
            *(
                t.reshape((-1, width))
                for t in cross_links(*run(memory_back_kernel, list(dkv2) + [w_two], memory_outs))
            )
        )

        def col_grads(left, grads, n):
            cols = grads.shape[1] // n * 4
            total = t_mm(left, grads).reshape(-1, n, 2, 1, cols // 8)
            full = (total * mine).reshape(-1, n, cols).transpose(1, 0, 2)
            out = lax.psum_scatter(full.astype(BF16), "z", scatter_dimension=1, tiled=True)
            return lax.psum(out.astype(F32), ("hi", "x", "core"))

        def row_grads(left, grads):
            total = t_mm(left, grads).reshape(2, 1, -1, width)
            full = (total * mine[:, :, None]).reshape(-1, width)
            out = lax.psum_scatter(full.astype(BF16), "z", scatter_dimension=0, tiled=True)
            return lax.psum(out.astype(F32), ("hi", "x", "core"))

        def joined(pieces):
            return jnp.concatenate(pieces, 0)

        g_first = col_grads(joined(twos), du, 1)[0]
        g_second = row_grads(active, joined(f3))
        g_qkv = col_grads(joined(tokens), dqkv, 3)
        g_q2 = col_grads(joined(ones), dq2, 1)
        rows_of = jnp.concatenate(mems, 1).reshape(-1, width)
        g_kv2 = col_grads(rows_of, joined(dkv2), 2)
        g_proj = jnp.concatenate([g_qkv, g_q2, g_kv2], 0)
        g_out = jnp.stack([row_grads(o1, joined(f1)), row_grads(o2, joined(f2))])
        sums_qkv = (sum_qkv.reshape(3, 2, 1, width // 8) * mine).reshape(3, width)
        sums_qkv = lax.psum(sums_qkv, AXES)

    d_memory = transpose(d_memory.reshape(memory.shape))
    d_dec = transpose(own_d.reshape(dec_in.shape)).astype(F32)
    n_part = width // n_z
    cut = lax.dynamic_slice_in_dim(small, zi * n_part, n_part, 1)
    cut_qkv = lax.dynamic_slice_in_dim(sums_qkv, zi * n_part, n_part, 1)
    g_biases = jnp.concatenate([cut_qkv[0:1], cut_qkv[2:3], cut[0:4]], 0)
    g_out_bias = cut[4]
    g_ffn_bias = lax.dynamic_slice_in_dim(
        small[5 : 5 + ff_rows].reshape(-1), zi * (ff_width // n_z), ff_width // n_z
    )
    g_gain = cut[5 + ff_rows : 8 + ff_rows]
    g_shift = cut[8 + ff_rows : 11 + ff_rows]
    return (
        mixed_out,
        d_dec,
        d_memory,
        g_proj,
        g_out,
        g_first,
        g_second,
        g_biases,
        g_out_bias,
        g_ffn_bias,
        g_gain,
        g_shift,
    )


def solution(mesh):
    devices = mesh.devices
    inner = Mesh(devices.reshape(devices.shape[0] // 4, 2, 2, devices.shape[1]), AXES)
    dp = ("hi", "x", "core")
    in_specs = (
        P(dp, "z", None),
        P(dp, None, "z", None),
        P(None, AXES, None),
        P(None, AXES, None),
        P(AXES, None),
        P(AXES, None),
        P(),
        P(),
        P(),
        P(),
        P(),
        P(),
        P(),
        P(dp, None, None),
        P(dp, None),
        P(dp, "z", None),
    )
    out_specs = (
        P(dp, "z", None),
        P(dp, "z", None),
        P(dp, None, "z", None),
        P(None, "z", None),
        P(None, "z", None),
        P("z", None),
        P("z", None),
        P(None, "z"),
        P("z"),
        P("z"),
        P(None, "z"),
        P(None, "z"),
    )
    return jax.shard_map(
        per_device, mesh=inner, in_specs=in_specs, out_specs=out_specs, check_vma=False
    )
```

```python
import functools

import jax
import jax.numpy as jnp
from jax import lax
from jax.experimental import pallas as pl
from jax.experimental.pallas import tpu as pltpu
from jax.sharding import Mesh
from jax.sharding import PartitionSpec as P

HEADS = 16
HEAD_DIM = 64
LOCAL_HEADS = 4
EPS = 1e-05
NEG = -1e30
F32 = jnp.float32
BF16 = jnp.bfloat16
AXES = ("hi", "x", "core", "z")
ORDER = (0, 2, 1, 3)
VMEM_LIMIT = 60 * 1024 * 1024


def mm(left, right):
    return jnp.dot(left, right, preferred_element_type=F32)


def mm_t(left, right):
    return lax.dot_general(left, right, (((1,), (1,)), ((), ())), preferred_element_type=F32)


def t_mm(left, right):
    return lax.dot_general(left, right, (((0,), (0,)), ((), ())), preferred_element_type=F32)


def pick(array, index, axis=0):
    return lax.dynamic_index_in_dim(array, index, axis, False)


def swap(values, axis):
    return lax.ppermute(values, axis, [(0, 1), (1, 0)])


def head_masks(width):
    lane = lax.broadcasted_iota(jnp.int32, (1, width), 1)
    return [(lane // HEAD_DIM) == h for h in range(LOCAL_HEADS)]


def stack_heads(values, masks):
    zero = jnp.zeros_like(values)
    return jnp.concatenate([jnp.where(m, values, zero) for m in masks], 0)


def join_heads(stacked, masks, rows):
    out = jnp.zeros((rows, stacked.shape[1]), stacked.dtype)
    for h, m in enumerate(masks):
        out = jnp.where(m, stacked[h * rows : (h + 1) * rows], out)
    return out


def softmax_parts(scores, allowed):
    scores = jnp.where(allowed, scores * HEAD_DIM**-0.5, NEG)
    top = jnp.max(scores, -1, keepdims=True)
    expo = jnp.exp(scores - top)
    return expo * (1.0 / jnp.sum(expo, -1, keepdims=True))


def attend_core(q, k, v, allowed):
    rows, width = q.shape
    masks = head_masks(width)
    scores = mm_t(stack_heads(q, masks), k)
    probs = [
        softmax_parts(scores[h * rows : (h + 1) * rows], allowed).astype(BF16)
        for h in range(LOCAL_HEADS)
    ]
    mixed = mm(jnp.concatenate(probs, 0), v)
    return join_heads(mixed, masks, rows).astype(BF16)


def attend_back_core(q, k, v, allowed, grad):
    rows, width = q.shape
    masks = head_masks(width)
    q_heads = stack_heads(q, masks)
    grad_heads = stack_heads(grad, masks)
    scores = mm_t(q_heads, k)
    grad_probs = mm_t(grad_heads, v)
    probs, grad_scores = [], []
    for h in range(LOCAL_HEADS):
        part = slice(h * rows, (h + 1) * rows)
        p = softmax_parts(scores[part], allowed)
        gp = grad_probs[part]
        centre = jnp.sum(p * gp, -1, keepdims=True)
        grad_scores.append((p * (gp - centre)).astype(BF16))
        probs.append(p.astype(BF16))
    probs = jnp.concatenate(probs, 0)
    grad_scores = jnp.concatenate(grad_scores, 0)
    scale = HEAD_DIM**-0.5
    dq = join_heads(mm(grad_scores, k), masks, rows) * scale
    dk = t_mm(grad_scores, q_heads) * scale
    dv = t_mm(probs, grad_heads)
    return dq.astype(BF16), dk.astype(BF16), dv.astype(BF16)


KERNEL_US = {
    "cut_cols_kernel": 2,
    "pack_kernel": 2,
    "pack_ffn_kernel": 2,
    "place_kernel": 4,
    "self_fwd_kernel": 5,
    "norm_one_kernel": 3,
    "memory_kv_kernel": 7,
    "cross_fwd_kernel": 8,
    "norm_two_kernel": 3,
    "place_ffn_kernel": 5,
    "ffn_fwd_kernel": 6,
    "norm_three_kernel": 3,
    "ffn_bwd_kernel": 6,
    "ffn_grad_kernel": 6,
    "norm_back_kernel": 3,
    "cross_bwd_kernel": 11,
    "memory_grad_kernel": 9,
    "cross_grad_kernel": 4,
    "self_bwd_kernel": 6,
    "self_grad_kernel": 5,
    "memory_back_kernel": 8,
    "pair_sum_kernel": 3,
    "final_sum_kernel": 2,
    "join_kernel": 1,
    "proj_out_kernel": 7,
    "ffn_out_kernel": 6,
    "small_kernel": 1,
}


def run(kernel, args, outs, scratch=(), aliases=None, any_args=(), any_outs=()):
    single = not isinstance(outs, (list, tuple))
    out_list = [outs] if single else list(outs)
    vmem = pl.BlockSpec(memory_space=pltpu.VMEM)
    anywhere = pl.BlockSpec(memory_space=pl.ANY)
    base = getattr(kernel, "func", kernel)
    result = pl.pallas_call(
        kernel,
        name=base.__name__,
        in_specs=[anywhere if i in any_args else vmem for i in range(len(args))],
        out_specs=[anywhere if i in any_outs else vmem for i in range(len(out_list))],
        out_shape=out_list,
        scratch_shapes=list(scratch),
        input_output_aliases=aliases or {},
        cost_estimate=pl.CostEstimate(
            flops=KERNEL_US[base.__name__] * 1_100_000_000, bytes_accessed=0, transcendentals=0
        ),
        compiler_params=pltpu.CompilerParams(vmem_limit_bytes=VMEM_LIMIT),
    )(*args)
    return result[0] if single else result


def shaped(shape, dtype):
    return jax.ShapeDtypeStruct(shape, dtype)


def group_place():
    return lax.axis_index("x") * 2 + lax.axis_index("core")


def lanes(start, size):
    return pl.ds(pl.multiple_of(start, 128), size)


def local_bias(ref, row, j, parts=2):
    n = ref.shape[1]
    size = n // (4 * parts)
    return jnp.concatenate(
        [ref[pl.ds(row, 1), lanes(p * 4 * size + j * size, size)] for p in range(parts)], 1
    )


def whole(refs):
    return jnp.concatenate([r[...] for r in refs], 0)


def halves(product, act, sent_ref, kept_ref):
    half = act.shape[0] // 2
    sent_ref[...] = product(act[half:]).astype(BF16)
    kept_ref[...] = product(act[:half])


def flat_row(ref, r):
    block = ref[:, r]
    return block.reshape(block.shape[0] * block.shape[1], block.shape[2])


def self_fwd_kernel(x0, x1, x2, x3, w, wo, biases, mask, qkv_out, o_out, sent, kept):
    j = group_place()
    tokens = whole([x0, x1, x2, x3])
    width = wo.shape[0]
    bq = local_bias(biases, 0, j)
    bias = jnp.concatenate([bq, jnp.zeros_like(bq), local_bias(biases, 1, j)], 1)
    qkv = (mm(tokens, w[...]) + bias).astype(BF16)
    qkv_out[...] = qkv.reshape(qkv_out.shape)
    for r in range(qkv_out.shape[1]):
        row = flat_row(qkv_out, r)
        out = attend_core(
            row[:, :width], row[:, width : 2 * width], row[:, 2 * width :], mask[r] > 0.5
        )
        o_out[:, r] = out.reshape(o_out.shape[0], o_out.shape[2], width)
    mixed = o_out[...].reshape(tokens.shape[0], width)
    halves(lambda a: mm(a, wo[...]), mixed, sent, kept)


def cross_allowed(qc, kc):
    return (kc >= 0.0) & ((kc == qc) | (qc < -1.5))


def memory_kv_kernel(m0, m1, m2, m3, w, biases, *outs):
    j = group_place()
    width = w.shape[1] // 3
    bv = local_bias(biases, 3, j)
    bias = jnp.concatenate([jnp.zeros_like(bv), bv], 1)
    for r, out in enumerate(outs):
        mem = jnp.concatenate([m[r] for m in (m0, m1, m2, m3)], 0)
        out[...] = (mm(mem, w[:, width:]) + bias).astype(BF16)


def memory_back_kernel(*refs):
    dkvs, (w, sent, kept) = refs[:-3], refs[-3:]
    width = w.shape[1] // 3
    for r, dkv in enumerate(dkvs):
        slots = dkv.shape[0] // 4
        far = mm_t(dkv[2 * slots :], w[:, width:]).astype(BF16)
        near = mm_t(dkv[: 2 * slots], w[:, width:])
        for d in range(2):
            sent[d, r] = far[d * slots : (d + 1) * slots]
            kept[d, r] = near[d * slots : (d + 1) * slots]


def cross_fwd_kernel(rows, *refs):
    h, (w, wo, biases), kvs = refs[:4], refs[4:7], refs[7 : 7 + rows]
    q_code, k_code, q_out, o_out, sent, kept = refs[7 + rows :]
    tokens = whole(h)
    width = wo.shape[0]
    query = (mm(tokens, w[:, :width]) + local_bias(biases, 2, group_place())).astype(BF16)
    q_out[...] = query.reshape(q_out.shape)
    for r, kv in enumerate(kvs):
        allowed = cross_allowed(q_code[r], k_code[r])
        out = attend_core(flat_row(q_out, r), kv[:, :width], kv[:, width:], allowed)
        o_out[:, r] = out.reshape(o_out.shape[0], o_out.shape[2], width)
    mixed = o_out[...].reshape(tokens.shape[0], width)
    halves(lambda a: mm(a, wo[...]), mixed, sent, kept)


def ffn_fwd_kernel(h0, h1, h2, h3, w1, w2, bias, g_out, slope_out, sent, kept):
    j = group_place()
    tokens = whole([h0, h1, h2, h3])
    u = mm(tokens, w1[...]) + local_bias(bias, 0, j, 4)
    normal = 0.5 * (1.0 + lax.erf(u * 0.7071067811865476))
    slope_out[...] = normal + u * (0.3989422804014327 * jnp.exp(-0.5 * u * u))
    g_out[...] = (u * normal).astype(BF16)
    halves(lambda a: mm(a, w2[...]), g_out[...], sent, kept)


def ffn_bwd_kernel(f0, f1, f2, f3, w1, w2, slope, du_out, bias_out, sent, kept):
    grads = whole([f0, f1, f2, f3])
    du = (mm_t(grads, w2[...]) * slope[...]).astype(BF16)
    du_out[...] = du
    bias_out[...] = jnp.sum(du.astype(F32), 0, keepdims=True)
    halves(lambda a: mm_t(a, w1[...]), du, sent, kept)


def cross_bwd_kernel(rows, *refs):
    f, (w, wo, q), kvs = refs[:4], refs[4:7], refs[7 : 7 + rows]
    q_code, k_code, dq_out = refs[7 + rows : 10 + rows]
    dkvs = refs[10 + rows : 10 + 2 * rows]
    sums, sent, kept, do_ref = refs[10 + 2 * rows :]
    grads = whole(f)
    width = wo.shape[0]
    do_ref[...] = mm_t(grads, wo[...]).astype(BF16).reshape(do_ref.shape)
    total_v = jnp.zeros((1, width), F32)
    for r, (kv, dkv) in enumerate(zip(kvs, dkvs)):
        allowed = cross_allowed(q_code[r], k_code[r])
        dq, dk, dv = attend_back_core(
            flat_row(q, r), kv[:, :width], kv[:, width:], allowed, flat_row(do_ref, r)
        )
        dq_out[:, r] = dq.reshape(dq_out.shape[0], dq_out.shape[2], width)
        dkv[:, :width] = dk
        dkv[:, width:] = dv
        total_v = total_v + jnp.sum(dv.astype(F32), 0, keepdims=True)
    dq = dq_out[...].reshape(grads.shape[0], width)
    total_q = jnp.sum(dq.astype(F32), 0, keepdims=True)
    sums[...] = jnp.concatenate([total_q, total_v, jnp.zeros((6, width), F32)], 0)
    halves(lambda a: mm_t(a, w[:, :width]), dq, sent, kept)


def self_bwd_kernel(f0, f1, f2, f3, w, wo, qkv, mask, dqkv_out, sums, sent, kept):
    grads = whole([f0, f1, f2, f3])
    width = wo.shape[0]
    shape = (qkv.shape[0], qkv.shape[1], qkv.shape[2], width)
    do = mm_t(grads, wo[...]).astype(BF16).reshape(shape)
    for r in range(shape[1]):
        row = flat_row(qkv, r)
        grad = do[:, r].reshape(row.shape[0], width)
        parts = attend_back_core(
            row[:, :width], row[:, width : 2 * width], row[:, 2 * width :], mask[r] > 0.5, grad
        )
        dqkv_out[:, r] = jnp.concatenate(parts, 1).reshape(shape[0], shape[2], 3 * width)
    dqkv = dqkv_out[...].reshape(grads.shape[0], 3 * width)
    sums[...] = jnp.sum(dqkv.astype(F32), 0, keepdims=True)
    halves(lambda a: mm_t(a, w[...]), dqkv, sent, kept)


def branch_sum(kept, arrived, crossed):
    n = crossed.shape[0]
    return kept[:n] + arrived[:n].astype(F32) + crossed[...].astype(F32)


def normalise(v):
    centre = v - jnp.mean(v, -1, keepdims=True)
    rstd = lax.rsqrt(jnp.mean(centre * centre, -1, keepdims=True) + EPS)
    return centre * rstd, rstd


def denormalise(e, gain, n, rstd):
    a = e * gain
    return rstd * (a - jnp.mean(a, -1, keepdims=True) - n * jnp.mean(a * n, -1, keepdims=True))


def norm_one_kernel(kept, arrived, crossed, own, bias, gains, shifts, n_out, rstd_out, low_out):
    v = branch_sum(kept, arrived, crossed) + bias[...] + own[...].astype(F32)
    n, rstd = normalise(v)
    n_out[...] = n
    rstd_out[...] = jnp.broadcast_to(rstd, rstd_out.shape)
    low_out[...] = (n * gains[0:1] + shifts[0:1]).astype(BF16)


def norm_two_kernel(kept, arrived, crossed, n_one, biases, gains, shifts, n_out, rstd_out, low_out):
    resid = n_one[...] * gains[0:1] + shifts[0:1]
    n, rstd = normalise(branch_sum(kept, arrived, crossed) + biases[4:5] + resid)
    n_out[...] = n
    rstd_out[...] = jnp.broadcast_to(rstd, rstd_out.shape)
    low_out[...] = (n * gains[1:2] + shifts[1:2]).astype(BF16)


def sums_of(e, n, low):
    return jnp.concatenate(
        [
            jnp.sum(e * n, 0, keepdims=True),
            jnp.sum(e, 0, keepdims=True),
            jnp.sum(low.astype(F32), 0, keepdims=True),
            jnp.zeros((5, e.shape[1]), F32),
        ],
        0,
    )


def norm_three_kernel(
    kept, arrived, crossed, n_two, biases, gains, shifts, cot, live, mixed_out, d_out, low_out, sums
):
    resid = n_two[...] * gains[1:2] + shifts[1:2]
    n, rstd = normalise(branch_sum(kept, arrived, crossed) + biases[5:6] + resid)
    mixed_out[...] = ((n * gains[2:3] + shifts[2:3]) * live[...]).astype(BF16)
    e = cot[...].astype(F32) * live[...]
    d = denormalise(e, gains[2:3], n, rstd)
    low = d.astype(BF16)
    d_out[...] = d
    low_out[...] = low
    sums[...] = sums_of(e, n, low)


def norm_back_kernel(which, kept, arrived, crossed, d_in, n, rstd, gains, d_out, low_out, sums):
    e = branch_sum(kept, arrived, crossed) + d_in[...]
    d = denormalise(e, gains[which : which + 1], n[...], rstd[:, 0:1])
    low = d.astype(BF16)
    d_out[...] = d
    low_out[...] = low
    sums[...] = sums_of(e, n[...], low)


def cut_cols_kernel(proj, first, *outs):
    j = group_place()
    n, _, width = proj.shape
    ff = first.shape[1]
    for d, out in enumerate(outs):
        target = jnp.bitwise_xor(j, d)
        at = 0
        for m in range(n):
            for h in range(2):
                out[:, at : at + width // 8] = proj[
                    m, :, lanes(h * (width // 2) + target * (width // 8), width // 8)
                ]
                at += width // 8
        for q in range(4):
            size = ff // 16
            out[:, at : at + size] = first[:, lanes(q * (ff // 4) + target * size, size)]
            at += size


def pack_kernel(e0, e1, e2, e3, out_w, buf_ab):
    j = group_place()
    quarter = out_w.shape[2] // 4
    six = 6 * quarter
    for d, e in enumerate([e0, e1, e2, e3]):
        buf_ab[jnp.bitwise_xor(j, d), :, :six] = e[:, :six]
    for i in range(4):
        for m in range(2):
            at = six + m * quarter
            buf_ab[i, :, at : at + quarter] = out_w[m, :, i * quarter : (i + 1) * quarter]


def pack_ffn_kernel(e0, e1, e2, e3, second, buf_c):
    j = group_place()
    rows, cols = buf_c.shape[1], buf_c.shape[2]
    for d, e in enumerate([e0, e1, e2, e3]):
        buf_c[jnp.bitwise_xor(j, d)] = e[:, e.shape[1] - cols :]
    for i in range(4):
        buf_c[4 + i] = second[i * rows : (i + 1) * rows]


def place_kernel(blocks, w_qkv, w_two, w_out, w_out2):
    cols = w_qkv.shape[-1]
    quarter = cols // 3
    for h in range(blocks.shape[0]):
        for z in range(blocks.shape[1]):
            for i in range(4):
                w_qkv[h, i, z] = blocks[h, z, i, :, :cols]
                w_two[h, i, z] = blocks[h, z, i, :, cols : 2 * cols]
                for m, out in enumerate([w_out, w_out2]):
                    at = 2 * cols + m * quarter
                    out[h, z, :, i * quarter : (i + 1) * quarter] = blocks[
                        h, z, i, :, at : at + quarter
                    ]


def place_ffn_kernel(blocks, wcol, wrow):
    rows = wcol.shape[-2]
    for h in range(blocks.shape[0]):
        for z in range(blocks.shape[1]):
            for i in range(4):
                wcol[h, i, z] = blocks[h, z, i]
                wrow[h, z, i * rows : (i + 1) * rows] = blocks[h, z, 4 + i]


def select_rows(dst, pieces, n_z, half_index):
    z = lax.axis_index("z")
    at = 0
    for piece in pieces:
        count, width = piece.shape
        for k in range(n_z):
            start = lax.rem(z + k, n_z) * (width // n_z) + half_index * (width // n_z // 2)
            dst[at : at + count, k * 128 : (k + 1) * 128] = piece[:, lanes(start, 128)]
        at += count


def select_cols(dst, pieces, n_z):
    z = lax.axis_index("z")
    at = 0
    for piece in pieces:
        count, width = piece.shape
        size = width // n_z
        for k in range(n_z):
            start = lax.rem(z + k, n_z) * size
            dst[at : at + count, k * size : (k + 1) * size] = piece[:, lanes(start, size)]
        at += count


def put_cols(out, at, block):
    n_z, rows = out.shape[0], out.shape[1]
    cols = block.shape[1]
    out[:, :, at : at + cols] = block.astype(BF16).reshape(n_z, rows, cols)


def put_rows(out, at, block):
    n_z, rows = out.shape[0], out.shape[1]
    size = block.shape[1] // n_z
    for k in range(n_z):
        for i in range(block.shape[0] // rows):
            out[k, :, at + i * size : at + (i + 1) * size] = block[
                i * rows : (i + 1) * rows, k * size : (k + 1) * size
            ].astype(BF16)


def half_of(ref, h):
    size = ref.shape[1] // 2
    return ref[:, lanes(h * size, size)]


def ffn_grad_kernel(a0, a1, a2, a3, du, g, f0, f1, f2, f3, out):
    n_hi, n_z, rows = out.shape[0], out.shape[1], out.shape[2]
    cols = du.shape[1]
    first = t_mm(whole([a0, a1, a2, a3]), du[...]).astype(BF16)
    second = t_mm(g[...], whole([f0, f1, f2, f3])).astype(BF16)
    for z in range(n_z):
        for h in range(n_hi):
            at = (z * n_hi + h) * rows
            out[h, z, :, :cols] = first[at : at + rows]
            out[h, z, :, cols:] = second[at : at + rows]


def memory_grad_kernel(n_z, rows, *refs):
    mems, dkvs, (kept, sent, left) = refs[:4], refs[4 : 4 + rows], refs[4 + rows :]
    hi = lax.axis_index("hi")
    for out, h in ((sent, 1 - hi), (kept, hi)):
        total = 0.0
        for r in range(rows):
            select_rows(left, [m.at[r] for m in mems], n_z, h)
            total = total + t_mm(left[...], dkvs[r][...])
        put_cols(out, 0, total)


def cross_grad_kernel(
    n_z, h0, h1, h2, h3, dq, kv_kept, kv_sent, o2, f0, f1, f2, f3, kept, sent, left, right
):
    hi = lax.axis_index("hi")
    c_q, c_kv = dq.shape[1], kv_kept.shape[2]
    select_cols(right, [f0, f1, f2, f3], n_z)
    for out, h, kv in ((sent, 1 - hi, kv_sent), (kept, hi, kv_kept)):
        select_rows(left, [h0, h1, h2, h3], n_z, h)
        put_cols(out, 0, t_mm(left[...], dq[...]))
        out[:, :, c_q : c_q + c_kv] = kv[...]
        put_rows(out, c_q + c_kv, t_mm(half_of(o2, h), right[...]))


def self_grad_kernel(
    n_z, x0, x1, x2, x3, dqkv, sums, small, o1, f0, f1, f2, f3, kept, sent, left, right
):
    hi = lax.axis_index("hi")
    rows = kept.shape[1] - 16
    cols = dqkv.shape[1]
    last = jnp.concatenate([sums[...], jnp.zeros((1, right.shape[1] - cols), F32)], 1)
    at_last = lax.broadcasted_iota(jnp.int32, small.shape, 0) == small.shape[0] - 1
    lower = jnp.where(at_last, last, small[...]).astype(BF16)
    select_cols(right, [f0, f1, f2, f3], n_z)
    size = right.shape[1] // n_z
    for out, h in ((sent, 1 - hi), (kept, hi)):
        select_rows(left, [x0, x1, x2, x3], n_z, h)
        block = t_mm(left[...], dqkv[...]).astype(BF16)
        other = t_mm(half_of(o1, h), right[...]).astype(BF16)
        for k in range(n_z):
            out[k, :rows, :cols] = block[k * rows : (k + 1) * rows]
            out[k, rows:] = lower
            out[k, :rows, cols:] = other[:, k * size : (k + 1) * size]


def pair_sum_kernel(kept, arrived, own, *sent):
    own[...] = kept[0].astype(F32) + arrived[0].astype(F32)
    for k, out in enumerate(sent):
        out[...] = (kept[k + 1].astype(F32) + arrived[k + 1].astype(F32)).astype(BF16)


def final_sum_kernel(cols, own, *refs):
    total = own[...]
    arrived, outs = refs[: -len(cols)], refs[-len(cols) :]
    for a in arrived:
        total = total + a[...].astype(F32)
    at = 0
    for out, size in zip(outs, cols):
        out[...] = total[:, at : at + size].astype(BF16)
        at += size


def places(index):
    h = jnp.bitwise_xor(lax.axis_index("hi"), (index >> 2) & 1)
    return h, jnp.bitwise_xor(group_place(), index & 3)


def ffn_out_kernel(*refs):
    pieces, first, second = refs[:8], refs[8], refs[9]
    rows = pieces[0].shape[0]
    ff = first.shape[1]
    size = ff // 16
    for index, piece in enumerate(pieces):
        h, j = places(index)
        at_rows = pl.ds(pl.multiple_of(h * rows, 8), rows)
        for q in range(4):
            first[at_rows, lanes(q * 4 * size + j * size, size)] = piece[
                :, q * size : (q + 1) * size
            ].astype(F32)
        second[pl.ds(pl.multiple_of((j * 2 + h) * rows, 8), rows), :] = piece[
            :, 4 * size :
        ].astype(F32)


def place_cols(out, m, rows, piece, at):
    width = out.shape[2]
    for index, p in enumerate(piece):
        h, j = places(index)
        for half in range(2):
            lo = at + half * (width // 8)
            out[
                m,
                pl.ds(pl.multiple_of(h * rows, 8), rows),
                lanes(half * (width // 2) + j * (width // 8), width // 8),
            ] = p[:rows, lo : lo + width // 8].astype(F32)


def place_rows(out, m, rows, pieces, at):
    size = out.shape[2] // 4
    for index, piece in enumerate(pieces):
        h, j = places(index)
        out[m, pl.ds(pl.multiple_of(h * rows, 8), rows), lanes(j * size, size)] = piece[
            :rows, at : at + size
        ].astype(F32)


def join_kernel(cols_b, cols_a, planed, rows_a, out):
    rows = cols_b.shape[0]
    c, r = cols_b.shape[1], rows_a.shape[1]
    out[...] = jnp.zeros_like(out)
    out[:rows, :c] = cols_b[...]
    out[:, c : 2 * c] = cols_a[...]
    out[:rows, 2 * c :] = planed[...]
    out[rows:, 2 * c : 2 * c + r] = rows_a[rows:, :]


def proj_out_kernel(n_z, *refs):
    pieces, (g_proj, g_out, g_biases, g_out_bias, g_ffn_bias, g_norms, sums, small) = (
        refs[:8],
        refs[8:],
    )
    rows = pieces[0].shape[0] - 16
    width = g_proj.shape[2]
    quarter = width // 4
    for m in range(3):
        place_cols(g_proj, m + 3, rows, pieces, m * quarter)
        place_cols(g_proj, m, rows, pieces, (3 + m) * quarter)
    place_rows(g_out, 1, rows, pieces, 6 * quarter)
    place_rows(g_out, 0, rows, pieces, 7 * quarter)
    lowers = [p[rows:, 3 * quarter : 7 * quarter].astype(F32) for p in pieces[:4]]
    small[...] = (lowers[0] + lowers[1]) + (lowers[2] + lowers[3])
    for index, lower in enumerate(lowers):
        _, j = places(index)
        for m in range(3):
            for half in range(2):
                lo = m * quarter + half * (width // 8)
                sums[m : m + 1, lanes(half * (width // 2) + j * (width // 8), width // 8)] = lower[
                    15:16, lo : lo + width // 8
                ]
    z = lax.axis_index("z")
    own = lanes(z * (width // n_z), width // n_z)
    ff_rows = n_z * g_ffn_bias.shape[1] // width
    g_biases[0:1] = sums[0:1, own]
    g_biases[1:2] = sums[2:3, own]
    g_biases[2:6] = small[0:4, own]
    g_out_bias[...] = small[4:5, own]
    g_ffn_bias[...] = small[pl.ds(5 + z * (ff_rows // n_z), 1), :]
    g_norms[...] = small[5 + ff_rows : 11 + ff_rows, own]


def small_kernel(s3, s2, s1, cross_sums, ff_sum, out):
    j = group_place()
    width = out.shape[1]
    ff = ff_sum.shape[1] * 4
    out[...] = jnp.zeros_like(out)
    for half in range(2):
        at = lanes(half * (width // 2) + j * (width // 8), width // 8)
        part = slice(half * (width // 8), (half + 1) * (width // 8))
        out[0:1, at] = cross_sums[0:1, part]
        out[1:2, at] = cross_sums[1:2, part]
    out[2:3] = s2[2:3]
    out[3:4] = s3[2:3]
    out[4:5] = s1[2:3]
    ff_rows = ff // width
    per = ff // 16
    for q in range(4):
        flat_at = q * (ff // 4) + j * per
        row = 5 + flat_at // width
        out[pl.ds(row, 1), lanes(lax.rem(flat_at, width), per)] = ff_sum[
            0:1, q * per : (q + 1) * per
        ]
    at = 5 + ff_rows
    for i, s in enumerate([s1, s2, s3]):
        out[at + i : at + i + 1] = s[0:1]
        out[at + 3 + i : at + 4 + i] = s[1:2]


def per_device(
    dec_in,
    memory,
    proj_w,
    out_w,
    ffn_in,
    ffn_out,
    biases,
    out_bias,
    ffn_bias,
    norm_gain,
    norm_bias,
    mem_len,
    dec_len,
    mem_seg,
    dec_seg,
    cotangent,
):
    n_hi = lax.axis_size("hi")
    n_z = lax.axis_size("z")
    hi = lax.axis_index("hi")
    zi = lax.axis_index("z")
    j = group_place()
    fast = n_hi == 2 and n_z == 4
    row_count, query_count, width = dec_in.shape
    tile_count, tile_part = memory.shape[1], memory.shape[2]
    own_tokens = row_count * query_count
    all_tokens = 4 * own_tokens
    slots = tile_count * tile_part
    ff_width = ffn_in.shape[1]
    local = width // 4
    ff_local = ff_width // 4

    def turned(index):
        return (index & 1) * 2 + (index >> 1)

    to_rows = [
        ((h * 4 + a) * 4 + b, (h * 4 + turned(b)) * 4 + turned(a))
        for h in range(n_hi)
        for a in range(4)
        for b in range(4)
    ]

    def transpose(values):
        return lax.ppermute(values, AXES, to_rows)

    def shift_z(values, k):
        return lax.ppermute(values, "z", [(i, (i + k) % n_z) for i in range(n_z)])

    def gather_j(values):
        across = swap(values, "x")
        return [values, across, swap(values, "core"), swap(across, "core")]

    def cross_links(sent, kept):
        arrived = swap(sent, "core")
        half = kept.shape[0] // 2
        middle = (kept[half:] + arrived[half:].astype(F32)).astype(BF16)
        return kept, arrived, swap(middle, "x")

    def add_crossed(kept, arrived, crossed, other=0.0):
        n = crossed.shape[0]
        total = kept[:n] + arrived[:n].astype(F32) + crossed.astype(F32) + other
        return total.astype(BF16)

    def split_cols(full, parts=2):
        n, total, cols = full.shape
        split = pick(full.reshape(n, total, parts, 4, cols // (4 * parts)), j, 3)
        return split.transpose(1, 0, 2, 3).reshape(total, n * cols // 4)

    def split_rows(full, parts=2):
        total, cols = full.shape
        split = full.reshape(parts, 4, total // (4 * parts), cols)
        return pick(split, j, 1).reshape(total // 4, cols)

    def near_blocks(block):
        return [block] + [shift_z(block, -k) for k in range(1, n_z)]

    def after(values, *others):
        return lax.optimization_barrier((values, *others))[0]

    segs = transpose(jnp.concatenate([mem_seg.reshape(row_count, -1), dec_seg], 1))
    own_in = transpose(dec_in).reshape(own_tokens, width)
    tokens = gather_j(own_in)
    own_memory = transpose(after(memory, own_in, segs)).reshape(row_count, slots, width)
    mems = gather_j(own_memory)
    if fast:
        rows = proj_w.shape[1]
        cut = shaped((rows, 6 * local + ff_local), BF16)
        e = run(cut_cols_kernel, [proj_w, ffn_in], [cut] * 4)
        diag = [(0, 3), (1, 2), (2, 1), (3, 0)]
        e = [e[0], swap(e[1], "core"), swap(e[2], "x"), lax.ppermute(e[3], ("x", "core"), diag)]
        to_quarter = [
            ((h * 4 + a) * 4 + b, (h * 4 + 2 * (a % 2) + b // 2) * 4 + 2 * (a // 2) + b % 2)
            for h in range(2)
            for a in range(4)
            for b in range(4)
        ]
        buf_ab = run(pack_kernel, e + [out_w], shaped((4, rows, 2 * width), BF16))
        second = lax.ppermute(after(ffn_out, own_memory), AXES, to_quarter)
        buf_c = run(pack_ffn_kernel, e + [second], shaped((8, rows, ff_local), BF16))
        all_ab = lax.all_gather(after(buf_ab, own_memory), ("hi", "z"), axis=0)
        col_shape = shaped((2, 4, n_z, rows, 3 * local), BF16)
        row_shape = shaped((2, n_z, rows, width), BF16)
        placed = run(
            place_kernel,
            [all_ab.reshape((2, n_z) + buf_ab.shape)],
            [col_shape, col_shape, row_shape, row_shape],
        )
        w_qkv, w_two = (w.reshape(-1, 3 * local) for w in placed[:2])
        w_out, w_out2 = (w.reshape(-1, width) for w in placed[2:])
        all_c = lax.all_gather(after(buf_c, all_ab), ("hi", "z"), axis=0)
        w_first, w_second = run(
            place_ffn_kernel,
            [all_c.reshape((2, n_z) + buf_c.shape)],
            [
                shaped((2, 4, n_z, rows, ff_local), BF16),
                shaped((2, n_z, ffn_out.shape[0], width), BF16),
            ],
        )
        w_first = w_first.reshape(-1, ff_local)
        w_second = w_second.reshape(-1, width)
    else:
        proj_full = lax.all_gather(proj_w, AXES, axis=1, tiled=True)
        out_full = lax.all_gather(out_w, AXES, axis=1, tiled=True)
        w_qkv, w_two = split_cols(proj_full[:3]), split_cols(proj_full[3:])
        w_out, w_out2 = split_rows(out_full[0]), split_rows(out_full[1])
        w_first = split_cols(lax.all_gather(ffn_in, AXES, axis=0, tiled=True)[None], 4)
        w_second = split_rows(lax.all_gather(ffn_out, AXES, axis=0, tiled=True), 4)

    own_cot = transpose(after(cotangent, mems[3])).reshape(own_tokens, width)
    mem_full = mem_seg.shape[1] * mem_seg.shape[2]
    group = hi * 4 + turned(zi)
    own_dlen = lax.dynamic_slice_in_dim(dec_len, group * row_count, row_count)
    own_mlen = lax.dynamic_slice_in_dim(mem_len, group * row_count, row_count)
    parts = [turned(j ^ d) for d in ORDER]
    mem_parts = segs[:, :mem_full].reshape(row_count, tile_count, 4, tile_part)
    dec_parts = segs[:, mem_full:].reshape(row_count, 4, query_count)
    dseg = jnp.concatenate([pick(dec_parts, p, 1) for p in parts], 1)
    mseg = jnp.concatenate([pick(mem_parts, p, 2).reshape(row_count, slots) for p in parts], 1)
    dpos = jnp.concatenate([p * query_count + jnp.arange(query_count) for p in parts])
    in_tile = jnp.arange(tile_count)[:, None] * (4 * tile_part) + jnp.arange(tile_part)[None, :]
    mpos = jnp.concatenate([(in_tile + p * tile_part).reshape(-1) for p in parts])
    dlive = dpos[None, :] < own_dlen[:, None]
    mlive = mpos[None, :] < own_mlen[:, None]
    self_mask = (
        (dseg[:, :, None] == dseg[:, None, :])
        & (dpos[None, None, :] <= dpos[None, :, None])
        & dlive[:, None, :]
    ) | (dpos[None, None, :] == dpos[None, :, None])
    self_mask = self_mask.astype(F32)
    q_code = jnp.where(dlive, dseg.astype(F32), -2.0)[:, :, None]
    k_code = jnp.where(mlive, mseg.astype(F32), -1.0)[:, None, :]
    own_pos = parts[0] * query_count + jnp.arange(query_count)
    own_live = (own_pos[None, :] < own_dlen[:, None]).astype(F32).reshape(own_tokens, 1)
    part = width // n_z // 2

    def pair_sums(kept, arrived):
        shape = kept.shape[1:]
        return run(
            pair_sum_kernel,
            [kept, arrived],
            [shaped(shape, F32)] + [shaped(shape, BF16)] * (n_z - 1),
        )

    def sum_z(own, out, cols):
        arrived = [shift_z(block, i + 1) for i, block in enumerate(out)]
        return run(
            functools.partial(final_sum_kernel, cols),
            [own, *arrived],
            [shaped((own.shape[0], c), BF16) for c in cols],
        )

    to_plane = [
        ((h * 4 + 2 * a + b) * 4 + z, (b * 4 + z) * 4 + 2 * h + a)
        for h in range(2)
        for a in range(2)
        for b in range(2)
        for z in range(4)
    ]

    def gather_dp(block):
        pieces = [block, swap(block, "x")]
        pieces = pieces + [swap(p, "hi") for p in pieces]
        return [q for p in pieces for q in (p, swap(p, "core"))]

    def to_planes(rows):
        return lax.ppermute(rows, AXES, to_plane)

    def beside(cols, rows):
        return jnp.concatenate([cols, rows], 1)

    def both(cols, rows=part):
        return [shaped((n_z, rows, cols), BF16)] * 2

    def tokens_scratch(cols):
        return pltpu.VMEM((all_tokens, cols), BF16)


    heads = shaped((4, row_count, query_count, local), BF16)
    sent = shaped((all_tokens // 2, width), BF16)
    kept = shaped((all_tokens // 2, width), F32)
    own_f32 = shaped((own_tokens, width), F32)
    own_low = shaped((own_tokens, width), BF16)
    rstd_shape = shaped((own_tokens, 128), F32)
    sums_shape = shaped((8, width), F32)
    qkv, mixed_self, s, k = run(
        self_fwd_kernel,
        [*[after(t, mems[3]) for t in tokens], w_qkv, w_out, biases, self_mask],
        [shaped((4, row_count, query_count, 3 * local), BF16), heads, sent, kept],
    )
    n_one, rstd_one, one_low = run(
        norm_one_kernel,
        [*cross_links(s, k), own_in, out_bias[None], norm_gain, norm_bias],
        [own_f32, rstd_shape, own_low],
    )
    ones = gather_j(one_low)
    kv_shape = shaped((4 * slots, 2 * local), BF16)
    kv2 = run(memory_kv_kernel, [*mems, w_two, biases], [kv_shape] * row_count)
    query_two, mixed_cross, s, k = run(
        functools.partial(cross_fwd_kernel, row_count),
        [*ones, w_two, w_out2, biases, *kv2, q_code, k_code],
        [heads, heads, sent, kept],
    )
    n_two, rstd_two, two_low = run(
        norm_two_kernel,
        [*cross_links(s, k), n_one, biases, norm_gain, norm_bias],
        [own_f32, rstd_shape, own_low],
    )
    twos = gather_j(two_low)
    active, slope, s, k = run(
        ffn_fwd_kernel,
        [*twos, w_first, w_second, ffn_bias[None]],
        [shaped((all_tokens, ff_local), BF16), shaped((all_tokens, ff_local), F32), sent, kept],
    )
    mixed_out, d_three, own_f3, sums_three = run(
        norm_three_kernel,
        [*cross_links(s, k), n_two, biases, norm_gain, norm_bias, own_cot, own_live],
        [own_low, own_f32, own_low, sums_shape],
    )
    own_out = mixed_out.reshape(dec_in.shape)

    f3 = gather_j(own_f3)
    du, ff_sum, s, k = run(
        ffn_bwd_kernel,
        [*f3, w_first, w_second, slope],
        [shaped((all_tokens, ff_local), BF16), shaped((1, ff_local), F32), sent, kept],
    )
    k, arrived, crossed = cross_links(s, k)
    if fast:
        g_ffn = run(
            ffn_grad_kernel,
            [*twos, du, active, *f3],
            shaped((2, n_z, part, ff_local + width), BF16),
        )
        crossed = after(crossed, g_ffn)
        g_ffn = lax.psum_scatter(
            g_ffn.reshape(2 * n_z * part, -1), ("hi", "z"), scatter_dimension=0, tiled=True
        )
    d_two, own_f2, sums_two = run(
        functools.partial(norm_back_kernel, 1),
        [k, arrived, crossed, d_three, n_two, rstd_two, norm_gain],
        [own_f32, own_low, sums_shape],
    )
    f2 = gather_j(own_f2)
    dq2, *dkv2, cross_sums, s, k = run(
        functools.partial(cross_bwd_kernel, row_count),
        [*f2, w_two, w_out2, query_two, *kv2, q_code, k_code],
        [heads] + [kv_shape] * row_count + [shaped((8, local), F32), sent, kept],
        scratch=[pltpu.VMEM(heads.shape, BF16)],
    )
    d_one, own_f1, sums_one = run(
        functools.partial(norm_back_kernel, 0),
        [*cross_links(s, k), d_two, n_one, rstd_one, norm_gain],
        [own_f32, own_low, sums_shape],
    )
    f1 = gather_j(own_f1)
    dq2 = dq2.reshape(all_tokens, local)
    o2 = mixed_cross.reshape(all_tokens, local)
    if fast:
        kept_m, sent_m = run(
            functools.partial(memory_grad_kernel, n_z, row_count),
            mems + dkv2,
            both(2 * local),
            scratch=[pltpu.VMEM((4 * slots, width // 2), BF16)],
        )
        kept_b, sent_b = run(
            functools.partial(cross_grad_kernel, n_z),
            [*ones, dq2, kept_m, sent_m, o2, *f2],
            both(4 * local),
            scratch=[tokens_scratch(width // 2), tokens_scratch(width)],
        )
        f1 = [after(f, sent_b) for f in f1]
    dqkv, sum_qkv, s, k = run(
        self_bwd_kernel,
        [*f1, w_qkv, w_out, qkv, self_mask],
        [
            shaped((4, row_count, query_count, 3 * local), BF16),
            shaped((1, 3 * local), F32),
            sent,
            kept,
        ],
    )
    own_d = add_crossed(*cross_links(s, k), d_one)

    ff_rows = ff_width // width
    n_small = 16
    small = run(
        small_kernel,
        [sums_three, sums_two, sums_one, cross_sums, ff_sum],
        shaped((n_small, width), F32),
    )
    dqkv = dqkv.reshape(all_tokens, -1)
    o1 = mixed_self.reshape(all_tokens, local)
    half_slots = (2, row_count, slots, width)
    memory_outs = [shaped(half_slots, BF16), shaped(half_slots, F32)]
    if fast:
        arrived_b = swap(sent_b, "hi")
        kept_a, sent_a = run(
            functools.partial(self_grad_kernel, n_z),
            [*tokens, dqkv, sum_qkv, small, o1, *f1],
            both(4 * local, part + 16),
            scratch=[tokens_scratch(width // 2), tokens_scratch(width)],
        )
        sums_c = after(g_ffn, sent_a)
        arrived_a = swap(after(sent_a, arrived_b), "hi")
        own_b, *out_b = pair_sums(kept_b, after(arrived_b, sums_c))
        s_m, k_m = run(
            memory_back_kernel, [after(dkv, out_b[0]) for dkv in dkv2] + [w_two], memory_outs
        )
        links_m = cross_links(s_m, k_m)
        cols_b, rows_b = sum_z(own_b, out_b, (3 * local, local))
        own_a, *out_a = pair_sums(kept_a, after(arrived_a, rows_b, links_m[2]))
        pieces_c = gather_dp(after(sums_c, arrived_a))
        cols_a, rows_a = sum_z(own_a, out_a, (3 * local, local))
        planed = to_planes(beside(rows_b, rows_a[:part]))
        d_memory = add_crossed(*(t.reshape((-1, width)) for t in links_m))
        d_memory = after(d_memory, planed)
        block = run(
            join_kernel,
            [cols_b, cols_a, after(planed, d_memory), rows_a],
            shaped((part + 16, 8 * local), BF16),
        )
        mixed_out = transpose(after(own_out, planed))
        d_dec = transpose(after(own_d, planed).reshape(dec_in.shape))
        d_memory = transpose(after(d_memory, d_dec, mixed_out).reshape(memory.shape))
        g_first, g_second = run(
            ffn_out_kernel,
            pieces_c,
            [shaped((width // n_z, ff_width), F32), shaped((ff_width // n_z, width), F32)],
        )
        n_part = width // n_z
        g_proj, g_out, g_biases, g_out_bias, g_ffn_bias, g_norms = run(
            functools.partial(proj_out_kernel, n_z),
            gather_dp(block),
            [
                shaped((6, n_part, width), F32),
                shaped((2, n_part, width), F32),
                shaped((6, n_part), F32),
                shaped((1, n_part), F32),
                shaped((1, ff_width // n_z), F32),
                shaped((6, n_part), F32),
            ],
            scratch=[pltpu.VMEM((8, width), F32), pltpu.VMEM(small.shape, F32)],
        )
        g_out_bias, g_ffn_bias = g_out_bias[0], g_ffn_bias[0]
        g_gain, g_shift = g_norms[:3], g_norms[3:]
    else:
        mine = (jnp.arange(4) == j).astype(F32)[:, None]

        small = lax.psum(small, AXES)
        d_memory = add_crossed(
            *(
                t.reshape((-1, width))
                for t in cross_links(*run(memory_back_kernel, list(dkv2) + [w_two], memory_outs))
            )
        )

        d_memory = transpose(d_memory.reshape(memory.shape))
        d_dec = transpose(own_d.reshape(dec_in.shape))
        mixed_out = transpose(own_out)

        def col_grads(left, grads, n, parts=2):
            cols = grads.shape[1] // n * 4
            total = t_mm(left, grads).reshape(-1, n, parts, 1, cols // (4 * parts))
            full = (total * mine).reshape(-1, n, cols).transpose(1, 0, 2)
            out = lax.psum_scatter(full.astype(BF16), "z", scatter_dimension=1, tiled=True)
            return lax.psum(out.astype(F32), ("hi", "x", "core"))

        def row_grads(left, grads, parts=2):
            total = t_mm(left, grads).reshape(parts, 1, -1, width)
            full = (total * mine[:, :, None]).reshape(-1, width)
            out = lax.psum_scatter(full.astype(BF16), "z", scatter_dimension=0, tiled=True)
            return lax.psum(out.astype(F32), ("hi", "x", "core"))

        def joined(pieces):
            return jnp.concatenate(pieces, 0)

        g_first = col_grads(joined(twos), du, 1, 4)[0]
        g_second = row_grads(active, joined(f3), 4)
        g_qkv = col_grads(joined(tokens), dqkv, 3)
        g_q2 = col_grads(joined(ones), dq2, 1)
        rows_of = jnp.concatenate(mems, 1).reshape(-1, width)
        g_kv2 = col_grads(rows_of, joined(dkv2), 2)
        g_proj = jnp.concatenate([g_qkv, g_q2, g_kv2], 0)
        g_out = jnp.stack([row_grads(o1, joined(f1)), row_grads(o2, joined(f2))])
        sums_qkv = (sum_qkv.reshape(3, 2, 1, width // 8) * mine).reshape(3, width)
        sums_qkv = lax.psum(sums_qkv, AXES)

        n_part = width // n_z
        cut = lax.dynamic_slice_in_dim(small, zi * n_part, n_part, 1)
        cut_qkv = lax.dynamic_slice_in_dim(sums_qkv, zi * n_part, n_part, 1)
        g_biases = jnp.concatenate([cut_qkv[0:1], cut_qkv[2:3], cut[0:4]], 0)
        g_out_bias = cut[4]
        g_ffn_bias = lax.dynamic_slice_in_dim(
            small[5 : 5 + ff_rows].reshape(-1), zi * (ff_width // n_z), ff_width // n_z
        )
        g_gain = cut[5 + ff_rows : 8 + ff_rows]
        g_shift = cut[8 + ff_rows : 11 + ff_rows]
    d_dec = d_dec.astype(F32)
    return (
        mixed_out,
        d_dec,
        d_memory,
        g_proj,
        g_out,
        g_first,
        g_second,
        g_biases,
        g_out_bias,
        g_ffn_bias,
        g_gain,
        g_shift,
    )


def solution(mesh):
    devices = mesh.devices
    inner = Mesh(devices.reshape(devices.shape[0] // 4, 2, 2, devices.shape[1]), AXES)
    dp = ("hi", "x", "core")
    in_specs = (
        P(dp, "z", None),
        P(dp, None, "z", None),
        P(None, AXES, None),
        P(None, AXES, None),
        P(AXES, None),
        P(AXES, None),
        P(),
        P(),
        P(),
        P(),
        P(),
        P(),
        P(),
        P(dp, None, None),
        P(dp, None),
        P(dp, "z", None),
    )
    out_specs = (
        P(dp, "z", None),
        P(dp, "z", None),
        P(dp, None, "z", None),
        P(None, "z", None),
        P(None, "z", None),
        P("z", None),
        P("z", None),
        P(None, "z"),
        P("z"),
        P("z"),
        P(None, "z"),
        P(None, "z"),
    )
    return jax.shard_map(
        per_device, mesh=inner, in_specs=in_specs, out_specs=out_specs, check_vma=False
    )
```

```python
import functools

import jax
import jax.numpy as jnp
from jax import lax
from jax.experimental import pallas as pl
from jax.experimental.pallas import tpu as pltpu
from jax.sharding import Mesh
from jax.sharding import PartitionSpec as P

HEADS = 16
HEAD_DIM = 64
LOCAL_HEADS = 4
EPS = 1e-05
NEG = -1e30
F32 = jnp.float32
BF16 = jnp.bfloat16
AXES = ("hi", "x", "core", "z")
ORDER = (0, 2, 1, 3)
VMEM_LIMIT = 60 * 1024 * 1024


def mm(left, right):
    return jnp.dot(left, right, preferred_element_type=F32)


def mm_t(left, right):
    return lax.dot_general(left, right, (((1,), (1,)), ((), ())), preferred_element_type=F32)


def t_mm(left, right):
    return lax.dot_general(left, right, (((0,), (0,)), ((), ())), preferred_element_type=F32)


def pick(array, index, axis=0):
    return lax.dynamic_index_in_dim(array, index, axis, False)


def swap(values, axis):
    return lax.ppermute(values, axis, [(0, 1), (1, 0)])


def head_masks(width):
    lane = lax.broadcasted_iota(jnp.int32, (1, width), 1)
    return [(lane // HEAD_DIM) == h for h in range(LOCAL_HEADS)]


def stack_heads(values, masks):
    zero = jnp.zeros_like(values)
    return jnp.concatenate([jnp.where(m, values, zero) for m in masks], 0)


def join_heads(stacked, masks, rows):
    out = jnp.zeros((rows, stacked.shape[1]), stacked.dtype)
    for h, m in enumerate(masks):
        out = jnp.where(m, stacked[h * rows : (h + 1) * rows], out)
    return out


def softmax_parts(scores, allowed):
    scores = jnp.where(allowed, scores * HEAD_DIM**-0.5, NEG)
    top = jnp.max(scores, -1, keepdims=True)
    expo = jnp.exp(scores - top)
    return expo * (1.0 / jnp.sum(expo, -1, keepdims=True))


def attend_core(q, k, v, allowed):
    rows, width = q.shape
    masks = head_masks(width)
    scores = mm_t(stack_heads(q, masks), k)
    probs = [
        softmax_parts(scores[h * rows : (h + 1) * rows], allowed).astype(BF16)
        for h in range(LOCAL_HEADS)
    ]
    mixed = mm(jnp.concatenate(probs, 0), v)
    return join_heads(mixed, masks, rows).astype(BF16)


def attend_back_core(q, k, v, allowed, grad):
    rows, width = q.shape
    masks = head_masks(width)
    q_heads = stack_heads(q, masks)
    grad_heads = stack_heads(grad, masks)
    scores = mm_t(q_heads, k)
    grad_probs = mm_t(grad_heads, v)
    probs, grad_scores = [], []
    for h in range(LOCAL_HEADS):
        part = slice(h * rows, (h + 1) * rows)
        p = softmax_parts(scores[part], allowed)
        gp = grad_probs[part]
        centre = jnp.sum(p * gp, -1, keepdims=True)
        grad_scores.append((p * (gp - centre)).astype(BF16))
        probs.append(p.astype(BF16))
    probs = jnp.concatenate(probs, 0)
    grad_scores = jnp.concatenate(grad_scores, 0)
    scale = HEAD_DIM**-0.5
    dq = join_heads(mm(grad_scores, k), masks, rows) * scale
    dk = t_mm(grad_scores, q_heads) * scale
    dv = t_mm(probs, grad_heads)
    return dq.astype(BF16), dk.astype(BF16), dv.astype(BF16)


KERNEL_US = {
    "cut_cols_kernel": 2,
    "pack_kernel": 2,
    "pack_ffn_kernel": 2,
    "place_kernel": 4,
    "self_fwd_kernel": 5,
    "norm_one_kernel": 3,
    "memory_kv_kernel": 7,
    "cross_fwd_kernel": 8,
    "norm_two_kernel": 3,
    "place_ffn_kernel": 5,
    "ffn_fwd_kernel": 6,
    "norm_three_kernel": 3,
    "ffn_bwd_kernel": 6,
    "ffn_grad_kernel": 6,
    "norm_back_kernel": 3,
    "cross_bwd_kernel": 11,
    "memory_grad_kernel": 9,
    "cross_grad_kernel": 4,
    "self_bwd_kernel": 6,
    "self_grad_kernel": 5,
    "memory_back_kernel": 8,
    "pair_sum_kernel": 3,
    "final_sum_kernel": 2,
    "join_kernel": 1,
    "proj_out_kernel": 7,
    "ffn_out_kernel": 6,
    "small_kernel": 1,
}


def run(kernel, args, outs, scratch=(), aliases=None, any_args=(), any_outs=()):
    single = not isinstance(outs, (list, tuple))
    out_list = [outs] if single else list(outs)
    vmem = pl.BlockSpec(memory_space=pltpu.VMEM)
    anywhere = pl.BlockSpec(memory_space=pl.ANY)
    base = getattr(kernel, "func", kernel)
    result = pl.pallas_call(
        kernel,
        name=base.__name__,
        in_specs=[anywhere if i in any_args else vmem for i in range(len(args))],
        out_specs=[anywhere if i in any_outs else vmem for i in range(len(out_list))],
        out_shape=out_list,
        scratch_shapes=list(scratch),
        input_output_aliases=aliases or {},
        cost_estimate=pl.CostEstimate(
            flops=KERNEL_US[base.__name__] * 1_100_000_000, bytes_accessed=0, transcendentals=0
        ),
        compiler_params=pltpu.CompilerParams(vmem_limit_bytes=VMEM_LIMIT),
    )(*args)
    return result[0] if single else result


def shaped(shape, dtype):
    return jax.ShapeDtypeStruct(shape, dtype)


def group_place():
    return lax.axis_index("x") * 2 + lax.axis_index("core")


def lanes(start, size):
    return pl.ds(pl.multiple_of(start, 128), size)


def local_bias(ref, row, j, parts=2):
    n = ref.shape[1]
    size = n // (4 * parts)
    return jnp.concatenate(
        [ref[pl.ds(row, 1), lanes(p * 4 * size + j * size, size)] for p in range(parts)], 1
    )


def whole(refs):
    return jnp.concatenate([r[...] for r in refs], 0)


def halves(product, act, sent_ref, kept_ref):
    half = act.shape[0] // 2
    sent_ref[...] = product(act[half:]).astype(BF16)
    kept_ref[...] = product(act[:half])


def flat_row(ref, r):
    block = ref[:, r]
    return block.reshape(block.shape[0] * block.shape[1], block.shape[2])


def self_fwd_kernel(x0, x1, x2, x3, w, wo, biases, mask, qkv_out, o_out, sent, kept):
    j = group_place()
    tokens = whole([x0, x1, x2, x3])
    width = wo.shape[0]
    bq = local_bias(biases, 0, j)
    bias = jnp.concatenate([bq, jnp.zeros_like(bq), local_bias(biases, 1, j)], 1)
    qkv = (mm(tokens, w[...]) + bias).astype(BF16)
    qkv_out[...] = qkv.reshape(qkv_out.shape)
    for r in range(qkv_out.shape[1]):
        row = flat_row(qkv_out, r)
        out = attend_core(
            row[:, :width], row[:, width : 2 * width], row[:, 2 * width :], mask[r] > 0.5
        )
        o_out[:, r] = out.reshape(o_out.shape[0], o_out.shape[2], width)
    mixed = o_out[...].reshape(tokens.shape[0], width)
    halves(lambda a: mm(a, wo[...]), mixed, sent, kept)


def cross_allowed(qc, kc):
    return (kc >= 0.0) & ((kc == qc) | (qc < -1.5))


def memory_kv_kernel(m0, m1, m2, m3, w, biases, *outs):
    j = group_place()
    width = w.shape[1] // 3
    bv = local_bias(biases, 3, j)
    bias = jnp.concatenate([jnp.zeros_like(bv), bv], 1)
    for r, out in enumerate(outs):
        mem = jnp.concatenate([m[r] for m in (m0, m1, m2, m3)], 0)
        out[...] = (mm(mem, w[:, width:]) + bias).astype(BF16)


def memory_back_kernel(*refs):
    dkvs, (w, sent, kept) = refs[:-3], refs[-3:]
    width = w.shape[1] // 3
    for r, dkv in enumerate(dkvs):
        slots = dkv.shape[0] // 4
        far = mm_t(dkv[2 * slots :], w[:, width:]).astype(BF16)
        near = mm_t(dkv[: 2 * slots], w[:, width:])
        for d in range(2):
            sent[d, r] = far[d * slots : (d + 1) * slots]
            kept[d, r] = near[d * slots : (d + 1) * slots]


def cross_fwd_kernel(rows, *refs):
    h, (w, wo, biases), kvs = refs[:4], refs[4:7], refs[7 : 7 + rows]
    q_code, k_code, q_out, o_out, sent, kept = refs[7 + rows :]
    tokens = whole(h)
    width = wo.shape[0]
    query = (mm(tokens, w[:, :width]) + local_bias(biases, 2, group_place())).astype(BF16)
    q_out[...] = query.reshape(q_out.shape)
    for r, kv in enumerate(kvs):
        allowed = cross_allowed(q_code[r], k_code[r])
        out = attend_core(flat_row(q_out, r), kv[:, :width], kv[:, width:], allowed)
        o_out[:, r] = out.reshape(o_out.shape[0], o_out.shape[2], width)
    mixed = o_out[...].reshape(tokens.shape[0], width)
    halves(lambda a: mm(a, wo[...]), mixed, sent, kept)


def ffn_fwd_kernel(h0, h1, h2, h3, w1, w2, bias, g_out, slope_out, sent, kept):
    j = group_place()
    tokens = whole([h0, h1, h2, h3])
    u = mm(tokens, w1[...]) + local_bias(bias, 0, j, 4)
    normal = 0.5 * (1.0 + lax.erf(u * 0.7071067811865476))
    slope_out[...] = normal + u * (0.3989422804014327 * jnp.exp(-0.5 * u * u))
    g_out[...] = (u * normal).astype(BF16)
    halves(lambda a: mm(a, w2[...]), g_out[...], sent, kept)


def ffn_bwd_kernel(f0, f1, f2, f3, w1, w2, slope, du_out, bias_out, sent, kept):
    grads = whole([f0, f1, f2, f3])
    du = (mm_t(grads, w2[...]) * slope[...]).astype(BF16)
    du_out[...] = du
    bias_out[...] = jnp.sum(du.astype(F32), 0, keepdims=True)
    halves(lambda a: mm_t(a, w1[...]), du, sent, kept)


def cross_bwd_kernel(rows, *refs):
    f, (w, wo, q), kvs = refs[:4], refs[4:7], refs[7 : 7 + rows]
    q_code, k_code, dq_out = refs[7 + rows : 10 + rows]
    dkvs = refs[10 + rows : 10 + 2 * rows]
    sums, sent, kept, do_ref = refs[10 + 2 * rows :]
    grads = whole(f)
    width = wo.shape[0]
    do_ref[...] = mm_t(grads, wo[...]).astype(BF16).reshape(do_ref.shape)
    total_v = jnp.zeros((1, width), F32)
    for r, (kv, dkv) in enumerate(zip(kvs, dkvs)):
        allowed = cross_allowed(q_code[r], k_code[r])
        dq, dk, dv = attend_back_core(
            flat_row(q, r), kv[:, :width], kv[:, width:], allowed, flat_row(do_ref, r)
        )
        dq_out[:, r] = dq.reshape(dq_out.shape[0], dq_out.shape[2], width)
        dkv[:, :width] = dk
        dkv[:, width:] = dv
        total_v = total_v + jnp.sum(dv.astype(F32), 0, keepdims=True)
    dq = dq_out[...].reshape(grads.shape[0], width)
    total_q = jnp.sum(dq.astype(F32), 0, keepdims=True)
    sums[...] = jnp.concatenate([total_q, total_v, jnp.zeros((6, width), F32)], 0)
    halves(lambda a: mm_t(a, w[:, :width]), dq, sent, kept)


def self_bwd_kernel(f0, f1, f2, f3, w, wo, qkv, mask, dqkv_out, sums, sent, kept):
    grads = whole([f0, f1, f2, f3])
    width = wo.shape[0]
    shape = (qkv.shape[0], qkv.shape[1], qkv.shape[2], width)
    do = mm_t(grads, wo[...]).astype(BF16).reshape(shape)
    for r in range(shape[1]):
        row = flat_row(qkv, r)
        grad = do[:, r].reshape(row.shape[0], width)
        parts = attend_back_core(
            row[:, :width], row[:, width : 2 * width], row[:, 2 * width :], mask[r] > 0.5, grad
        )
        dqkv_out[:, r] = jnp.concatenate(parts, 1).reshape(shape[0], shape[2], 3 * width)
    dqkv = dqkv_out[...].reshape(grads.shape[0], 3 * width)
    sums[...] = jnp.sum(dqkv.astype(F32), 0, keepdims=True)
    halves(lambda a: mm_t(a, w[...]), dqkv, sent, kept)


def branch_sum(kept, arrived, crossed):
    n = crossed.shape[0]
    return kept[:n] + arrived[:n].astype(F32) + crossed[...].astype(F32)


def normalise(v):
    centre = v - jnp.mean(v, -1, keepdims=True)
    rstd = lax.rsqrt(jnp.mean(centre * centre, -1, keepdims=True) + EPS)
    return centre * rstd, rstd


def denormalise(e, gain, n, rstd):
    a = e * gain
    return rstd * (a - jnp.mean(a, -1, keepdims=True) - n * jnp.mean(a * n, -1, keepdims=True))


def norm_one_kernel(kept, arrived, crossed, own, bias, gains, shifts, n_out, rstd_out, low_out):
    v = branch_sum(kept, arrived, crossed) + bias[...] + own[...].astype(F32)
    n, rstd = normalise(v)
    n_out[...] = n
    rstd_out[...] = jnp.broadcast_to(rstd, rstd_out.shape)
    low_out[...] = (n * gains[0:1] + shifts[0:1]).astype(BF16)


def norm_two_kernel(kept, arrived, crossed, n_one, biases, gains, shifts, n_out, rstd_out, low_out):
    resid = n_one[...] * gains[0:1] + shifts[0:1]
    n, rstd = normalise(branch_sum(kept, arrived, crossed) + biases[4:5] + resid)
    n_out[...] = n
    rstd_out[...] = jnp.broadcast_to(rstd, rstd_out.shape)
    low_out[...] = (n * gains[1:2] + shifts[1:2]).astype(BF16)


def sums_of(e, n, low):
    return jnp.concatenate(
        [
            jnp.sum(e * n, 0, keepdims=True),
            jnp.sum(e, 0, keepdims=True),
            jnp.sum(low.astype(F32), 0, keepdims=True),
            jnp.zeros((5, e.shape[1]), F32),
        ],
        0,
    )


def norm_three_kernel(
    kept, arrived, crossed, n_two, biases, gains, shifts, cot, live, mixed_out, d_out, low_out, sums
):
    resid = n_two[...] * gains[1:2] + shifts[1:2]
    n, rstd = normalise(branch_sum(kept, arrived, crossed) + biases[5:6] + resid)
    mixed_out[...] = ((n * gains[2:3] + shifts[2:3]) * live[...]).astype(BF16)
    e = cot[...].astype(F32) * live[...]
    d = denormalise(e, gains[2:3], n, rstd)
    low = d.astype(BF16)
    d_out[...] = d
    low_out[...] = low
    sums[...] = sums_of(e, n, low)


def norm_back_kernel(which, kept, arrived, crossed, d_in, n, rstd, gains, d_out, low_out, sums):
    e = branch_sum(kept, arrived, crossed) + d_in[...]
    d = denormalise(e, gains[which : which + 1], n[...], rstd[:, 0:1])
    low = d.astype(BF16)
    d_out[...] = d
    low_out[...] = low
    sums[...] = sums_of(e, n[...], low)


def cut_cols_kernel(proj, first, *outs):
    j = group_place()
    n, _, width = proj.shape
    ff = first.shape[1]
    for d, out in enumerate(outs):
        target = jnp.bitwise_xor(j, d)
        at = 0
        for m in range(n):
            for h in range(2):
                out[:, at : at + width // 8] = proj[
                    m, :, lanes(h * (width // 2) + target * (width // 8), width // 8)
                ]
                at += width // 8
        for q in range(4):
            size = ff // 16
            out[:, at : at + size] = first[:, lanes(q * (ff // 4) + target * size, size)]
            at += size


def pack_kernel(e0, e1, e2, e3, out_w, buf_ab):
    j = group_place()
    quarter = out_w.shape[2] // 4
    six = 6 * quarter
    for d, e in enumerate([e0, e1, e2, e3]):
        buf_ab[jnp.bitwise_xor(j, d), :, :six] = e[:, :six]
    for i in range(4):
        for m in range(2):
            at = six + m * quarter
            buf_ab[i, :, at : at + quarter] = out_w[m, :, i * quarter : (i + 1) * quarter]


def pack_ffn_kernel(e0, e1, e2, e3, second, buf_c):
    j = group_place()
    rows, cols = buf_c.shape[1], buf_c.shape[2]
    for d, e in enumerate([e0, e1, e2, e3]):
        buf_c[jnp.bitwise_xor(j, d)] = e[:, e.shape[1] - cols :]
    for i in range(4):
        buf_c[4 + i] = second[i * rows : (i + 1) * rows]


def place_kernel(blocks, w_qkv, w_two, w_out, w_out2):
    cols = w_qkv.shape[-1]
    quarter = cols // 3
    for h in range(blocks.shape[0]):
        for z in range(blocks.shape[1]):
            for i in range(4):
                w_qkv[h, i, z] = blocks[h, z, i, :, :cols]
                w_two[h, i, z] = blocks[h, z, i, :, cols : 2 * cols]
                for m, out in enumerate([w_out, w_out2]):
                    at = 2 * cols + m * quarter
                    out[h, z, :, i * quarter : (i + 1) * quarter] = blocks[
                        h, z, i, :, at : at + quarter
                    ]


def place_ffn_kernel(blocks, wcol, wrow):
    rows = wcol.shape[-2]
    for h in range(blocks.shape[0]):
        for z in range(blocks.shape[1]):
            for i in range(4):
                wcol[h, i, z] = blocks[h, z, i]
                wrow[h, z, i * rows : (i + 1) * rows] = blocks[h, z, 4 + i]


def select_rows(dst, pieces, n_z, half_index):
    z = lax.axis_index("z")
    at = 0
    for piece in pieces:
        count, width = piece.shape
        for k in range(n_z):
            start = lax.rem(z + k, n_z) * (width // n_z) + half_index * (width // n_z // 2)
            dst[at : at + count, k * 128 : (k + 1) * 128] = piece[:, lanes(start, 128)]
        at += count


def select_cols(dst, pieces, n_z):
    z = lax.axis_index("z")
    at = 0
    for piece in pieces:
        count, width = piece.shape
        size = width // n_z
        for k in range(n_z):
            start = lax.rem(z + k, n_z) * size
            dst[at : at + count, k * size : (k + 1) * size] = piece[:, lanes(start, size)]
        at += count


def put_cols(out, at, block):
    n_z, rows = out.shape[0], out.shape[1]
    cols = block.shape[1]
    out[:, :, at : at + cols] = block.astype(BF16).reshape(n_z, rows, cols)


def put_rows(out, at, block):
    n_z, rows = out.shape[0], out.shape[1]
    size = block.shape[1] // n_z
    for k in range(n_z):
        for i in range(block.shape[0] // rows):
            out[k, :, at + i * size : at + (i + 1) * size] = block[
                i * rows : (i + 1) * rows, k * size : (k + 1) * size
            ].astype(BF16)


def half_of(ref, h):
    size = ref.shape[1] // 2
    return ref[:, lanes(h * size, size)]


def ffn_grad_kernel(a0, a1, a2, a3, du, g, f0, f1, f2, f3, out):
    n_hi, n_z, rows = out.shape[0], out.shape[1], out.shape[2]
    cols = du.shape[1]
    first = t_mm(whole([a0, a1, a2, a3]), du[...]).astype(BF16)
    second = t_mm(g[...], whole([f0, f1, f2, f3])).astype(BF16)
    for z in range(n_z):
        for h in range(n_hi):
            at = (z * n_hi + h) * rows
            out[h, z, :, :cols] = first[at : at + rows]
            out[h, z, :, cols:] = second[at : at + rows]


def memory_grad_kernel(n_z, rows, *refs):
    mems, dkvs, (kept, sent, left) = refs[:4], refs[4 : 4 + rows], refs[4 + rows :]
    hi = lax.axis_index("hi")
    for out, h in ((sent, 1 - hi), (kept, hi)):
        total = 0.0
        for r in range(rows):
            select_rows(left, [m.at[r] for m in mems], n_z, h)
            total = total + t_mm(left[...], dkvs[r][...])
        put_cols(out, 0, total)


def cross_grad_kernel(
    n_z, h0, h1, h2, h3, dq, kv_kept, kv_sent, o2, f0, f1, f2, f3, kept, sent, left, right
):
    hi = lax.axis_index("hi")
    c_q, c_kv = dq.shape[1], kv_kept.shape[2]
    select_cols(right, [f0, f1, f2, f3], n_z)
    for out, h, kv in ((sent, 1 - hi, kv_sent), (kept, hi, kv_kept)):
        select_rows(left, [h0, h1, h2, h3], n_z, h)
        put_cols(out, 0, t_mm(left[...], dq[...]))
        out[:, :, c_q : c_q + c_kv] = kv[...]
        put_rows(out, c_q + c_kv, t_mm(half_of(o2, h), right[...]))


def self_grad_kernel(
    n_z, x0, x1, x2, x3, dqkv, sums, small, o1, f0, f1, f2, f3, kept, sent, left, right
):
    hi = lax.axis_index("hi")
    rows = kept.shape[1] - 16
    cols = dqkv.shape[1]
    last = jnp.concatenate([sums[...], jnp.zeros((1, right.shape[1] - cols), F32)], 1)
    at_last = lax.broadcasted_iota(jnp.int32, small.shape, 0) == small.shape[0] - 1
    lower = jnp.where(at_last, last, small[...]).astype(BF16)
    select_cols(right, [f0, f1, f2, f3], n_z)
    size = right.shape[1] // n_z
    for out, h in ((sent, 1 - hi), (kept, hi)):
        select_rows(left, [x0, x1, x2, x3], n_z, h)
        block = t_mm(left[...], dqkv[...]).astype(BF16)
        other = t_mm(half_of(o1, h), right[...]).astype(BF16)
        for k in range(n_z):
            out[k, :rows, :cols] = block[k * rows : (k + 1) * rows]
            out[k, rows:] = lower
            out[k, :rows, cols:] = other[:, k * size : (k + 1) * size]


def pair_sum_kernel(kept, arrived, own, *sent):
    own[...] = kept[0].astype(F32) + arrived[0].astype(F32)
    for k, out in enumerate(sent):
        out[...] = (kept[k + 1].astype(F32) + arrived[k + 1].astype(F32)).astype(BF16)


def final_sum_kernel(cols, own, *refs):
    total = own[...]
    arrived, outs = refs[: -len(cols)], refs[-len(cols) :]
    for a in arrived:
        total = total + a[...].astype(F32)
    at = 0
    for out, size in zip(outs, cols):
        out[...] = total[:, at : at + size].astype(BF16)
        at += size


def places(index):
    h = jnp.bitwise_xor(lax.axis_index("hi"), (index >> 2) & 1)
    return h, jnp.bitwise_xor(group_place(), index & 3)


def ffn_out_kernel(*refs):
    pieces, first, second = refs[:8], refs[8], refs[9]
    rows = pieces[0].shape[0]
    ff = first.shape[1]
    size = ff // 16
    for index, piece in enumerate(pieces):
        h, j = places(index)
        at_rows = pl.ds(pl.multiple_of(h * rows, 8), rows)
        for q in range(4):
            first[at_rows, lanes(q * 4 * size + j * size, size)] = piece[
                :, q * size : (q + 1) * size
            ].astype(F32)
        second[pl.ds(pl.multiple_of((j * 2 + h) * rows, 8), rows), :] = piece[
            :, 4 * size :
        ].astype(F32)


def place_cols(out, m, rows, piece, at):
    width = out.shape[2]
    for index, p in enumerate(piece):
        h, j = places(index)
        for half in range(2):
            lo = at + half * (width // 8)
            out[
                m,
                pl.ds(pl.multiple_of(h * rows, 8), rows),
                lanes(half * (width // 2) + j * (width // 8), width // 8),
            ] = p[:rows, lo : lo + width // 8].astype(F32)


def place_rows(out, m, rows, pieces, at):
    size = out.shape[2] // 4
    for index, piece in enumerate(pieces):
        h, j = places(index)
        out[m, pl.ds(pl.multiple_of(h * rows, 8), rows), lanes(j * size, size)] = piece[
            :rows, at : at + size
        ].astype(F32)


def join_kernel(cols_b, cols_a, planed, rows_a, out):
    rows = cols_b.shape[0]
    c, r = cols_b.shape[1], rows_a.shape[1]
    out[...] = jnp.zeros_like(out)
    out[:rows, :c] = cols_b[...]
    out[:, c : 2 * c] = cols_a[...]
    out[:rows, 2 * c :] = planed[...]
    out[rows:, 2 * c : 2 * c + r] = rows_a[rows:, :]


def proj_out_kernel(n_z, *refs):
    pieces, (g_proj, g_out, g_biases, g_out_bias, g_ffn_bias, g_norms, sums, small) = (
        refs[:8],
        refs[8:],
    )
    rows = pieces[0].shape[0] - 16
    width = g_proj.shape[2]
    quarter = width // 4
    for m in range(3):
        place_cols(g_proj, m + 3, rows, pieces, m * quarter)
        place_cols(g_proj, m, rows, pieces, (3 + m) * quarter)
    place_rows(g_out, 1, rows, pieces, 6 * quarter)
    place_rows(g_out, 0, rows, pieces, 7 * quarter)
    lowers = [p[rows:, 3 * quarter : 7 * quarter].astype(F32) for p in pieces[:4]]
    small[...] = (lowers[0] + lowers[1]) + (lowers[2] + lowers[3])
    for index, lower in enumerate(lowers):
        _, j = places(index)
        for m in range(3):
            for half in range(2):
                lo = m * quarter + half * (width // 8)
                sums[m : m + 1, lanes(half * (width // 2) + j * (width // 8), width // 8)] = lower[
                    15:16, lo : lo + width // 8
                ]
    z = lax.axis_index("z")
    own = lanes(z * (width // n_z), width // n_z)
    ff_rows = n_z * g_ffn_bias.shape[1] // width
    g_biases[0:1] = sums[0:1, own]
    g_biases[1:2] = sums[2:3, own]
    g_biases[2:6] = small[0:4, own]
    g_out_bias[...] = small[4:5, own]
    g_ffn_bias[...] = small[pl.ds(5 + z * (ff_rows // n_z), 1), :]
    g_norms[...] = small[5 + ff_rows : 11 + ff_rows, own]


def small_kernel(s3, s2, s1, cross_sums, ff_sum, out):
    j = group_place()
    width = out.shape[1]
    ff = ff_sum.shape[1] * 4
    out[...] = jnp.zeros_like(out)
    for half in range(2):
        at = lanes(half * (width // 2) + j * (width // 8), width // 8)
        part = slice(half * (width // 8), (half + 1) * (width // 8))
        out[0:1, at] = cross_sums[0:1, part]
        out[1:2, at] = cross_sums[1:2, part]
    out[2:3] = s2[2:3]
    out[3:4] = s3[2:3]
    out[4:5] = s1[2:3]
    ff_rows = ff // width
    per = ff // 16
    for q in range(4):
        flat_at = q * (ff // 4) + j * per
        row = 5 + flat_at // width
        out[pl.ds(row, 1), lanes(lax.rem(flat_at, width), per)] = ff_sum[
            0:1, q * per : (q + 1) * per
        ]
    at = 5 + ff_rows
    for i, s in enumerate([s1, s2, s3]):
        out[at + i : at + i + 1] = s[0:1]
        out[at + 3 + i : at + 4 + i] = s[1:2]


def per_device(
    dec_in,
    memory,
    proj_w,
    out_w,
    ffn_in,
    ffn_out,
    biases,
    out_bias,
    ffn_bias,
    norm_gain,
    norm_bias,
    mem_len,
    dec_len,
    mem_seg,
    dec_seg,
    cotangent,
):
    n_hi = lax.axis_size("hi")
    n_z = lax.axis_size("z")
    hi = lax.axis_index("hi")
    zi = lax.axis_index("z")
    j = group_place()
    fast = n_hi == 2 and n_z == 4
    row_count, query_count, width = dec_in.shape
    tile_count, tile_part = memory.shape[1], memory.shape[2]
    own_tokens = row_count * query_count
    all_tokens = 4 * own_tokens
    slots = tile_count * tile_part
    ff_width = ffn_in.shape[1]
    local = width // 4
    ff_local = ff_width // 4

    def turned(index):
        return (index & 1) * 2 + (index >> 1)

    to_rows = [
        ((h * 4 + a) * 4 + b, (h * 4 + turned(b)) * 4 + turned(a))
        for h in range(n_hi)
        for a in range(4)
        for b in range(4)
    ]

    def transpose(values):
        return lax.ppermute(values, AXES, to_rows)

    def shift_z(values, k):
        return lax.ppermute(values, "z", [(i, (i + k) % n_z) for i in range(n_z)])

    def gather_j(values):
        across = swap(values, "x")
        return [values, across, swap(values, "core"), swap(across, "core")]

    def cross_links(sent, kept):
        arrived = swap(sent, "core")
        half = kept.shape[0] // 2
        middle = (kept[half:] + arrived[half:].astype(F32)).astype(BF16)
        return kept, arrived, swap(middle, "x")

    def add_crossed(kept, arrived, crossed, other=0.0):
        n = crossed.shape[0]
        total = kept[:n] + arrived[:n].astype(F32) + crossed.astype(F32) + other
        return total.astype(BF16)

    def split_cols(full, parts=2):
        n, total, cols = full.shape
        split = pick(full.reshape(n, total, parts, 4, cols // (4 * parts)), j, 3)
        return split.transpose(1, 0, 2, 3).reshape(total, n * cols // 4)

    def split_rows(full, parts=2):
        total, cols = full.shape
        split = full.reshape(parts, 4, total // (4 * parts), cols)
        return pick(split, j, 1).reshape(total // 4, cols)

    def near_blocks(block):
        return [block] + [shift_z(block, -k) for k in range(1, n_z)]

    def after(values, *others):
        return lax.optimization_barrier((values, *others))[0]

    segs = transpose(jnp.concatenate([mem_seg.reshape(row_count, -1), dec_seg], 1))
    own_in = transpose(dec_in).reshape(own_tokens, width)
    tokens = gather_j(own_in)
    first_rows = transpose(after(memory[:-1], own_in, segs))
    last_row = transpose(after(memory[-1:], own_in, segs))
    own_memory = jnp.concatenate([first_rows, last_row]).reshape(row_count, slots, width)
    mems = gather_j(own_memory)
    if fast:
        rows = proj_w.shape[1]
        cut = shaped((rows, 6 * local + ff_local), BF16)
        e = run(cut_cols_kernel, [proj_w, ffn_in], [cut] * 4)
        diag = [(0, 3), (1, 2), (2, 1), (3, 0)]
        e = [e[0], swap(e[1], "core"), swap(e[2], "x"), lax.ppermute(e[3], ("x", "core"), diag)]
        to_quarter = [
            ((h * 4 + a) * 4 + b, (h * 4 + 2 * (a % 2) + b // 2) * 4 + 2 * (a // 2) + b % 2)
            for h in range(2)
            for a in range(4)
            for b in range(4)
        ]
        buf_ab = run(pack_kernel, e + [out_w], shaped((4, rows, 2 * width), BF16))
        second = lax.ppermute(after(ffn_out, own_memory), AXES, to_quarter)
        buf_c = run(pack_ffn_kernel, e + [second], shaped((8, rows, ff_local), BF16))
        all_ab = lax.all_gather(after(buf_ab, first_rows), ("hi", "z"), axis=0)
        col_shape = shaped((2, 4, n_z, rows, 3 * local), BF16)
        row_shape = shaped((2, n_z, rows, width), BF16)
        placed = run(
            place_kernel,
            [all_ab.reshape((2, n_z) + buf_ab.shape)],
            [col_shape, col_shape, row_shape, row_shape],
        )
        w_qkv, w_two = (w.reshape(-1, 3 * local) for w in placed[:2])
        w_out, w_out2 = (w.reshape(-1, width) for w in placed[2:])
        all_c = lax.all_gather(after(buf_c, all_ab), ("hi", "z"), axis=0)
        w_first, w_second = run(
            place_ffn_kernel,
            [all_c.reshape((2, n_z) + buf_c.shape)],
            [
                shaped((2, 4, n_z, rows, ff_local), BF16),
                shaped((2, n_z, ffn_out.shape[0], width), BF16),
            ],
        )
        w_first = w_first.reshape(-1, ff_local)
        w_second = w_second.reshape(-1, width)
    else:
        proj_full = lax.all_gather(proj_w, AXES, axis=1, tiled=True)
        out_full = lax.all_gather(out_w, AXES, axis=1, tiled=True)
        w_qkv, w_two = split_cols(proj_full[:3]), split_cols(proj_full[3:])
        w_out, w_out2 = split_rows(out_full[0]), split_rows(out_full[1])
        w_first = split_cols(lax.all_gather(ffn_in, AXES, axis=0, tiled=True)[None], 4)
        w_second = split_rows(lax.all_gather(ffn_out, AXES, axis=0, tiled=True), 4)

    own_cot = transpose(after(cotangent, mems[3])).reshape(own_tokens, width)
    mem_full = mem_seg.shape[1] * mem_seg.shape[2]
    group = hi * 4 + turned(zi)
    own_dlen = lax.dynamic_slice_in_dim(dec_len, group * row_count, row_count)
    own_mlen = lax.dynamic_slice_in_dim(mem_len, group * row_count, row_count)
    parts = [turned(j ^ d) for d in ORDER]
    mem_parts = segs[:, :mem_full].reshape(row_count, tile_count, 4, tile_part)
    dec_parts = segs[:, mem_full:].reshape(row_count, 4, query_count)
    dseg = jnp.concatenate([pick(dec_parts, p, 1) for p in parts], 1)
    mseg = jnp.concatenate([pick(mem_parts, p, 2).reshape(row_count, slots) for p in parts], 1)
    dpos = jnp.concatenate([p * query_count + jnp.arange(query_count) for p in parts])
    in_tile = jnp.arange(tile_count)[:, None] * (4 * tile_part) + jnp.arange(tile_part)[None, :]
    mpos = jnp.concatenate([(in_tile + p * tile_part).reshape(-1) for p in parts])
    dlive = dpos[None, :] < own_dlen[:, None]
    mlive = mpos[None, :] < own_mlen[:, None]
    self_mask = (
        (dseg[:, :, None] == dseg[:, None, :])
        & (dpos[None, None, :] <= dpos[None, :, None])
        & dlive[:, None, :]
    ) | (dpos[None, None, :] == dpos[None, :, None])
    self_mask = self_mask.astype(F32)
    q_code = jnp.where(dlive, dseg.astype(F32), -2.0)[:, :, None]
    k_code = jnp.where(mlive, mseg.astype(F32), -1.0)[:, None, :]
    own_pos = parts[0] * query_count + jnp.arange(query_count)
    own_live = (own_pos[None, :] < own_dlen[:, None]).astype(F32).reshape(own_tokens, 1)
    part = width // n_z // 2

    def pair_sums(kept, arrived):
        shape = kept.shape[1:]
        return run(
            pair_sum_kernel,
            [kept, arrived],
            [shaped(shape, F32)] + [shaped(shape, BF16)] * (n_z - 1),
        )

    def sum_z(own, out, cols):
        arrived = [shift_z(block, i + 1) for i, block in enumerate(out)]
        return run(
            functools.partial(final_sum_kernel, cols),
            [own, *arrived],
            [shaped((own.shape[0], c), BF16) for c in cols],
        )

    to_plane = [
        ((h * 4 + 2 * a + b) * 4 + z, (b * 4 + z) * 4 + 2 * h + a)
        for h in range(2)
        for a in range(2)
        for b in range(2)
        for z in range(4)
    ]

    def gather_dp(block):
        pieces = [block, swap(block, "x")]
        pieces = pieces + [swap(p, "hi") for p in pieces]
        return [q for p in pieces for q in (p, swap(p, "core"))]

    def to_planes(rows):
        return lax.ppermute(rows, AXES, to_plane)

    def beside(cols, rows):
        return jnp.concatenate([cols, rows], 1)

    def both(cols, rows=part):
        return [shaped((n_z, rows, cols), BF16)] * 2

    def tokens_scratch(cols):
        return pltpu.VMEM((all_tokens, cols), BF16)


    heads = shaped((4, row_count, query_count, local), BF16)
    sent = shaped((all_tokens // 2, width), BF16)
    kept = shaped((all_tokens // 2, width), F32)
    own_f32 = shaped((own_tokens, width), F32)
    own_low = shaped((own_tokens, width), BF16)
    rstd_shape = shaped((own_tokens, 128), F32)
    sums_shape = shaped((8, width), F32)
    qkv, mixed_self, s, k = run(
        self_fwd_kernel,
        [*[after(t, mems[3]) for t in tokens], w_qkv, w_out, biases, self_mask],
        [shaped((4, row_count, query_count, 3 * local), BF16), heads, sent, kept],
    )
    n_one, rstd_one, one_low = run(
        norm_one_kernel,
        [*cross_links(s, k), own_in, out_bias[None], norm_gain, norm_bias],
        [own_f32, rstd_shape, own_low],
    )
    ones = gather_j(one_low)
    kv_shape = shaped((4 * slots, 2 * local), BF16)
    kv2 = run(memory_kv_kernel, [*mems, w_two, biases], [kv_shape] * row_count)
    query_two, mixed_cross, s, k = run(
        functools.partial(cross_fwd_kernel, row_count),
        [*ones, w_two, w_out2, biases, *kv2, q_code, k_code],
        [heads, heads, sent, kept],
    )
    n_two, rstd_two, two_low = run(
        norm_two_kernel,
        [*cross_links(s, k), n_one, biases, norm_gain, norm_bias],
        [own_f32, rstd_shape, own_low],
    )
    twos = gather_j(two_low)
    active, slope, s, k = run(
        ffn_fwd_kernel,
        [*twos, w_first, w_second, ffn_bias[None]],
        [shaped((all_tokens, ff_local), BF16), shaped((all_tokens, ff_local), F32), sent, kept],
    )
    mixed_out, d_three, own_f3, sums_three = run(
        norm_three_kernel,
        [*cross_links(s, k), n_two, biases, norm_gain, norm_bias, own_cot, own_live],
        [own_low, own_f32, own_low, sums_shape],
    )
    own_out = mixed_out.reshape(dec_in.shape)

    f3 = gather_j(own_f3)
    du, ff_sum, s, k = run(
        ffn_bwd_kernel,
        [*f3, w_first, w_second, slope],
        [shaped((all_tokens, ff_local), BF16), shaped((1, ff_local), F32), sent, kept],
    )
    k, arrived, crossed = cross_links(s, k)
    if fast:
        g_ffn = run(
            ffn_grad_kernel,
            [*twos, du, active, *f3],
            shaped((2, n_z, part, ff_local + width), BF16),
        )
        crossed = after(crossed, g_ffn)
        g_ffn = lax.psum_scatter(
            g_ffn.reshape(2 * n_z * part, -1), ("hi", "z"), scatter_dimension=0, tiled=True
        )
    d_two, own_f2, sums_two = run(
        functools.partial(norm_back_kernel, 1),
        [k, arrived, crossed, d_three, n_two, rstd_two, norm_gain],
        [own_f32, own_low, sums_shape],
    )
    f2 = gather_j(own_f2)
    dq2, *dkv2, cross_sums, s, k = run(
        functools.partial(cross_bwd_kernel, row_count),
        [*f2, w_two, w_out2, query_two, *kv2, q_code, k_code],
        [heads] + [kv_shape] * row_count + [shaped((8, local), F32), sent, kept],
        scratch=[pltpu.VMEM(heads.shape, BF16)],
    )
    d_one, own_f1, sums_one = run(
        functools.partial(norm_back_kernel, 0),
        [*cross_links(s, k), d_two, n_one, rstd_one, norm_gain],
        [own_f32, own_low, sums_shape],
    )
    f1 = gather_j(own_f1)
    dq2 = dq2.reshape(all_tokens, local)
    o2 = mixed_cross.reshape(all_tokens, local)
    if fast:
        kept_m, sent_m = run(
            functools.partial(memory_grad_kernel, n_z, row_count),
            mems + dkv2,
            both(2 * local),
            scratch=[pltpu.VMEM((4 * slots, width // 2), BF16)],
        )
        kept_b, sent_b = run(
            functools.partial(cross_grad_kernel, n_z),
            [*ones, dq2, kept_m, sent_m, o2, *f2],
            both(4 * local),
            scratch=[tokens_scratch(width // 2), tokens_scratch(width)],
        )
        f1 = [after(f, sent_b) for f in f1]
    dqkv, sum_qkv, s, k = run(
        self_bwd_kernel,
        [*f1, w_qkv, w_out, qkv, self_mask],
        [
            shaped((4, row_count, query_count, 3 * local), BF16),
            shaped((1, 3 * local), F32),
            sent,
            kept,
        ],
    )
    own_d = add_crossed(*cross_links(s, k), d_one)

    ff_rows = ff_width // width
    n_small = 16
    small = run(
        small_kernel,
        [sums_three, sums_two, sums_one, cross_sums, ff_sum],
        shaped((n_small, width), F32),
    )
    dqkv = dqkv.reshape(all_tokens, -1)
    o1 = mixed_self.reshape(all_tokens, local)
    half_slots = (2, row_count, slots, width)
    memory_outs = [shaped(half_slots, BF16), shaped(half_slots, F32)]
    if fast:
        arrived_b = swap(sent_b, "hi")
        kept_a, sent_a = run(
            functools.partial(self_grad_kernel, n_z),
            [*tokens, dqkv, sum_qkv, small, o1, *f1],
            both(4 * local, part + 16),
            scratch=[tokens_scratch(width // 2), tokens_scratch(width)],
        )
        sums_c = after(g_ffn, sent_a)
        arrived_a = swap(after(sent_a, arrived_b), "hi")
        own_b, *out_b = pair_sums(kept_b, after(arrived_b, sums_c))
        s_m, k_m = run(
            memory_back_kernel, [after(dkv, out_b[0]) for dkv in dkv2] + [w_two], memory_outs
        )
        links_m = cross_links(s_m, k_m)
        cols_b, rows_b = sum_z(own_b, out_b, (3 * local, local))
        own_a, *out_a = pair_sums(kept_a, after(arrived_a, rows_b, links_m[2]))
        pieces_c = gather_dp(after(sums_c, arrived_a))
        cols_a, rows_a = sum_z(own_a, out_a, (3 * local, local))
        planed = to_planes(beside(rows_b, rows_a[:part]))
        d_memory = add_crossed(*(t.reshape((-1, width)) for t in links_m))
        d_memory = after(d_memory, planed)
        block = run(
            join_kernel,
            [cols_b, cols_a, after(planed, d_memory), rows_a],
            shaped((part + 16, 8 * local), BF16),
        )
        mixed_out = transpose(after(own_out, planed))
        d_dec = transpose(after(own_d, planed).reshape(dec_in.shape))
        d_memory = transpose(after(d_memory, d_dec, mixed_out).reshape(memory.shape))
        g_first, g_second = run(
            ffn_out_kernel,
            pieces_c,
            [shaped((width // n_z, ff_width), F32), shaped((ff_width // n_z, width), F32)],
        )
        n_part = width // n_z
        g_proj, g_out, g_biases, g_out_bias, g_ffn_bias, g_norms = run(
            functools.partial(proj_out_kernel, n_z),
            gather_dp(block),
            [
                shaped((6, n_part, width), F32),
                shaped((2, n_part, width), F32),
                shaped((6, n_part), F32),
                shaped((1, n_part), F32),
                shaped((1, ff_width // n_z), F32),
                shaped((6, n_part), F32),
            ],
            scratch=[pltpu.VMEM((8, width), F32), pltpu.VMEM(small.shape, F32)],
        )
        g_out_bias, g_ffn_bias = g_out_bias[0], g_ffn_bias[0]
        g_gain, g_shift = g_norms[:3], g_norms[3:]
    else:
        mine = (jnp.arange(4) == j).astype(F32)[:, None]

        small = lax.psum(small, AXES)
        d_memory = add_crossed(
            *(
                t.reshape((-1, width))
                for t in cross_links(*run(memory_back_kernel, list(dkv2) + [w_two], memory_outs))
            )
        )

        d_memory = transpose(d_memory.reshape(memory.shape))
        d_dec = transpose(own_d.reshape(dec_in.shape))
        mixed_out = transpose(own_out)

        def col_grads(left, grads, n, parts=2):
            cols = grads.shape[1] // n * 4
            total = t_mm(left, grads).reshape(-1, n, parts, 1, cols // (4 * parts))
            full = (total * mine).reshape(-1, n, cols).transpose(1, 0, 2)
            out = lax.psum_scatter(full.astype(BF16), "z", scatter_dimension=1, tiled=True)
            return lax.psum(out.astype(F32), ("hi", "x", "core"))

        def row_grads(left, grads, parts=2):
            total = t_mm(left, grads).reshape(parts, 1, -1, width)
            full = (total * mine[:, :, None]).reshape(-1, width)
            out = lax.psum_scatter(full.astype(BF16), "z", scatter_dimension=0, tiled=True)
            return lax.psum(out.astype(F32), ("hi", "x", "core"))

        def joined(pieces):
            return jnp.concatenate(pieces, 0)

        g_first = col_grads(joined(twos), du, 1, 4)[0]
        g_second = row_grads(active, joined(f3), 4)
        g_qkv = col_grads(joined(tokens), dqkv, 3)
        g_q2 = col_grads(joined(ones), dq2, 1)
        rows_of = jnp.concatenate(mems, 1).reshape(-1, width)
        g_kv2 = col_grads(rows_of, joined(dkv2), 2)
        g_proj = jnp.concatenate([g_qkv, g_q2, g_kv2], 0)
        g_out = jnp.stack([row_grads(o1, joined(f1)), row_grads(o2, joined(f2))])
        sums_qkv = (sum_qkv.reshape(3, 2, 1, width // 8) * mine).reshape(3, width)
        sums_qkv = lax.psum(sums_qkv, AXES)

        n_part = width // n_z
        cut = lax.dynamic_slice_in_dim(small, zi * n_part, n_part, 1)
        cut_qkv = lax.dynamic_slice_in_dim(sums_qkv, zi * n_part, n_part, 1)
        g_biases = jnp.concatenate([cut_qkv[0:1], cut_qkv[2:3], cut[0:4]], 0)
        g_out_bias = cut[4]
        g_ffn_bias = lax.dynamic_slice_in_dim(
            small[5 : 5 + ff_rows].reshape(-1), zi * (ff_width // n_z), ff_width // n_z
        )
        g_gain = cut[5 + ff_rows : 8 + ff_rows]
        g_shift = cut[8 + ff_rows : 11 + ff_rows]
    d_dec = d_dec.astype(F32)
    return (
        mixed_out,
        d_dec,
        d_memory,
        g_proj,
        g_out,
        g_first,
        g_second,
        g_biases,
        g_out_bias,
        g_ffn_bias,
        g_gain,
        g_shift,
    )


def solution(mesh):
    devices = mesh.devices
    inner = Mesh(devices.reshape(devices.shape[0] // 4, 2, 2, devices.shape[1]), AXES)
    dp = ("hi", "x", "core")
    in_specs = (
        P(dp, "z", None),
        P(dp, None, "z", None),
        P(None, AXES, None),
        P(None, AXES, None),
        P(AXES, None),
        P(AXES, None),
        P(),
        P(),
        P(),
        P(),
        P(),
        P(),
        P(),
        P(dp, None, None),
        P(dp, None),
        P(dp, "z", None),
    )
    out_specs = (
        P(dp, "z", None),
        P(dp, "z", None),
        P(dp, None, "z", None),
        P(None, "z", None),
        P(None, "z", None),
        P("z", None),
        P("z", None),
        P(None, "z"),
        P("z"),
        P("z"),
        P(None, "z"),
        P(None, "z"),
    )
    return jax.shard_map(
        per_device, mesh=inner, in_specs=in_specs, out_specs=out_specs, check_vma=False
    )
```
